512 devices in a mesh: probe: 4 (over x), sky: 128 (over y, z, core).
Axes of the slice: x: 4, y: 8, z: 8, core: 2. Of those that a mesh axis runs over, the one named last changes fastest.
Arguments:
- legendre: float32 [256, 4096, 512], P('sky', 'probe'), may hold values from -2.6958446 to 2.6958446
- signs: int32 [4, 512, 8192], P('probe', 'sky'), may hold values from -1 to 1, as said below
- inv_noise: float32 [512, 8192], P('sky'), may hold values from 0.3 to 3
- inv_signal: float32 [4096], replicated, may hold values from 0.3 to 30
- harmonic_order_values: int32 [256], replicated, may hold values from 0 to 4095, as said below
- cycle_rows: int32 [512], replicated, may hold values from 0 to 511, each once
Outputs:
- residual: float32 [4, 256, 2, 4096], P('probe', 'sky')
- variance: float32 [512, 8192], P('sky')
The draws below stay inside these ranges and needn't reach their ends.
Inputs may be any that keep to these rules, and one draw needn't show every extreme that they name: `harmonic_order_values`: slots 2i and 2i + 1 hold an order m and 4095 - m; no order appears twice; order 0 appears. `signs`: every entry is -1 or 1.
All inputs are finite; a program needn't handle non-finite values.
Results may differ from the reference program's by a relative error of at most 0.0003.
Values sent between devices are 32-bit elements; how exact they have to be, the bound alone decides.
No kernel may reach another device: no remote copies, remote signals or barrier semaphores. Data moves between devices by JAX's collectives and lax.ppermute only.
A program may use at most 64 MiB of HBM per device.

```python
import math
import jax
import jax.numpy as jnp
from jax import lax

L = 4096
NPHI = 8192
PROBES = 4
M_SLOTS = 256
CYCLES = 512


def draw_legendre(key, part):
    key = jax.random.fold_in(key, 11)
    first_key, second_key = jax.random.split(key)
    slot_frac = jnp.arange(M_SLOTS).astype(jnp.float32) / max(M_SLOTS - 1, 1)
    values_drawn = jnp.clip(jax.random.normal(first_key, (M_SLOTS, L, CYCLES), jnp.float32), -6.0, 6.0)
    slot_scale = 10.0 ** (0.5 * slot_frac)
    degree_scale = 10.0 ** (0.5 * jax.random.uniform(second_key, (L,), jnp.float32))
    return values_drawn * slot_scale[:, None, None] * degree_scale[None, :, None] * CYCLES ** (-0.5)


def draw_signs(key, part):
    key = jax.random.fold_in(key, 37)
    return (2 * jax.random.randint(key, (PROBES, CYCLES, NPHI), 0, 2) - 1).astype(jnp.int32)


def draw_harmonic_order_values(key, part):
    key = jax.random.fold_in(key, 23)
    first_key, second_key = jax.random.split(key)
    pair_count = M_SLOTS // 2
    lower_orders = jax.random.permutation(first_key, L // 2 - 1)[:pair_count] + 1
    zero_place = jax.random.randint(second_key, (), 0, pair_count)
    lower_orders = lower_orders.at[zero_place].set(0)
    paired = jnp.stack([lower_orders, L - 1 - lower_orders], axis=1).reshape(M_SLOTS)
    return paired.astype(jnp.int32)


def shard_levels(stream_key, shape, cuts, least, largest):
    factor_of = 1.0
    for dim, shards_of in cuts:
        heights = jax.random.uniform(jax.random.fold_in(jax.random.fold_in(stream_key, 6), dim), (shards_of,), jnp.float32, least / len(cuts), largest / len(cuts))
        factor_of = factor_of * jnp.repeat(jnp.exp(heights), shape[dim] // shards_of).reshape((-1,) + (1,) * (len(shape) - 1 - dim))
    return factor_of


def setup_inputs(seed: int = 0) -> dict:
    keys = jax.random.split(jax.random.key(seed), 7)
    legendre = draw_legendre(jax.random.fold_in(keys[6], 71), 0)
    signs = draw_signs(jax.random.fold_in(keys[6], 71), 0)
    inv_noise = jnp.clip(jnp.exp(math.log(3.0) - 2.3025851 * jax.random.uniform(keys[2], (CYCLES, NPHI), jnp.float32) ** shard_levels(keys[2], (CYCLES, NPHI), ((0, 128),), -0.2, 0.2)), 0.3, 3.0)
    inv_signal = jnp.clip(jnp.exp(jax.random.uniform(keys[3], (L,), jnp.float32, math.log(0.3), math.log(30.0))), 0.3, 30.0)
    harmonic_order_values = draw_harmonic_order_values(jax.random.fold_in(keys[6], 71), 0)
    cycle_rows = jax.random.permutation(keys[5], CYCLES).astype(jnp.int32)
    return dict(legendre=legendre, signs=signs, inv_noise=inv_noise, inv_signal=inv_signal, harmonic_order_values=harmonic_order_values, cycle_rows=cycle_rows)


MULTIPOLE_LIMIT = lax.Precision.HIGHEST

def trig_rows(orders, offset, block_cols, cycle_length):
    columns = (offset + jnp.arange(block_cols)).astype(jnp.int32)
    phases = orders[:, None] * columns[None, :] % cycle_length
    angles = phases.astype(jnp.float32) * (2.0 * math.pi / cycle_length)
    stacked = jnp.stack([jnp.cos(angles), jnp.sin(angles)], axis=1) / math.sqrt(cycle_length)
    return stacked.reshape(2 * orders.shape[0], block_cols)

def reference(legendre, signs, inv_noise, inv_signal, harmonic_order_values, cycle_rows):
    cycle_length = signs.shape[2]
    slot_count = harmonic_order_values.shape[0]
    probe_count = signs.shape[0]
    cycle_count = signs.shape[1]
    trig_table = trig_rows(harmonic_order_values, 0, cycle_length, cycle_length)
    degrees = jnp.arange(legendre.shape[1]).astype(jnp.int32)

    def analysis(pixels):
        harmonic_coefficient_set = jnp.einsum('qj,psj->pqs', trig_table, pixels, precision=MULTIPOLE_LIMIT)
        harmonic_coefficient_set = harmonic_coefficient_set.reshape(probe_count, slot_count, 2, cycle_count)
        latitude = jnp.zeros_like(harmonic_coefficient_set).at[:, :, :, cycle_rows].set(harmonic_coefficient_set)

        def single_slot(inputs):
            rows_table, order_value, probe_fields = inputs
            masked_sky_map = jnp.where((degrees >= order_value)[:, None], rows_table, 0.0)
            return jnp.einsum('im,zvm->zvi', masked_sky_map, probe_fields, precision=MULTIPOLE_LIMIT)
        result = lax.map(single_slot, (legendre, harmonic_order_values, jnp.transpose(latitude, (1, 0, 2, 3))))
        return jnp.transpose(result, (1, 0, 2, 3))

    def harmonic_synthesis(harmonic):

        def single_slot(inputs):
            rows_table, order_value, harmonic_coefficient_set = inputs
            masked_sky_map = jnp.where((degrees >= order_value)[:, None], rows_table, 0.0)
            return jnp.einsum('th,jnt->jnh', masked_sky_map, harmonic_coefficient_set, precision=MULTIPOLE_LIMIT)
        result = lax.map(single_slot, (legendre, harmonic_order_values, jnp.transpose(harmonic, (1, 0, 2, 3))))
        probe_fields = jnp.transpose(result, (1, 0, 2, 3))
        slot_order = jnp.take(probe_fields, cycle_rows, axis=3)
        flattened = slot_order.reshape(probe_count, 2 * slot_count, cycle_count)
        return jnp.einsum('pqs,qj->psj', flattened, trig_table, precision=MULTIPOLE_LIMIT)
    sign_field = signs.astype(jnp.float32)
    first_terms = analysis(sign_field)
    mapped = harmonic_synthesis(first_terms)
    weighted = sign_field * mapped
    image_terms = inv_signal[None, None, None, :] * first_terms + analysis(inv_noise[None] * mapped)
    norm_terms = lax.optimization_barrier(jnp.sum(first_terms * first_terms, axis=(1, 2, 3)))
    curve_terms = lax.optimization_barrier(jnp.sum(first_terms * image_terms, axis=(1, 2, 3)))
    step_ratio = norm_terms / curve_terms
    residual = first_terms - step_ratio[:, None, None, None] * image_terms
    variance = lax.optimization_barrier(jnp.sum(step_ratio[:, None, None] * weighted, axis=0)) / probe_count
    return (residual, variance)
```

```python
import functools
import math

import jax
import jax.numpy as jnp
from jax import lax
from jax.experimental import pallas as pl
from jax.experimental.pallas import tpu as pltpu
from jax.sharding import PartitionSpec as P

F32 = jnp.float32
BF16 = jnp.bfloat16
LANES = 128
SCALARS = 64
VMEM_BYTES = 40 * 1024 * 1024


def iota(shape, dim):
    return lax.broadcasted_iota(jnp.int32, shape, dim)


def dot(a, b):
    return jnp.dot(a, b, preferred_element_type=F32)


def halves(value):
    high = value.astype(BF16)
    return high, (value - high.astype(F32)).astype(BF16)


def turn(value, lanes):
    lanes = lanes % LANES
    return pltpu.roll(value, lanes, 1) if lanes else value


def fold(flat_ref, folded_ref):
    cycles = flat_ref.shape[-2]
    for j in range(folded_ref.shape[0] // cycles):
        folded_ref[j * cycles : (j + 1) * cycles, :] = flat_ref[
            :, j * LANES : (j + 1) * LANES
        ].astype(F32)


def twiddle_sums(parts, inner_cos, inner_sin, acc, lane, base):
    count = inner_cos.shape[0]
    real, imag = parts[:count], parts[count:]
    cos_sum = jnp.sum(inner_cos * real - inner_sin * imag, axis=1, keepdims=True)
    sin_sum = jnp.sum(inner_sin * real + inner_cos * imag, axis=1, keepdims=True)
    acc = jnp.where(lane == base, cos_sum, acc)
    return jnp.where(lane == base + 1, sin_sum, acc)


def join_slots(by_order_ref, slots, width):
    places = by_order_ref.shape[0] // slots
    out = by_order_ref[pl.ds(0, places, stride=slots), :]
    for s in range(1, slots):
        out = out + turn(by_order_ref[pl.ds(s, places, stride=slots), :], s * width)
    return out


def first_kernel(
    slots, orders_ref, signs_ref, send_ref, inner_cos_ref, inner_sin_ref, outer_a_ref, outer_s_ref,
    folded_ref, sums_ref,
):
    count = orders_ref.shape[1]
    probes = send_ref.shape[0]
    cycles = signs_ref.shape[1]
    outer = folded_ref.shape[0] // cycles
    cycle_length = outer * LANES
    own = lax.axis_index("probe")

    order_row = orders_ref[...]
    order_col = jnp.sum(
        jnp.where(iota((count, count), 0) == iota((count, count), 1), order_row.astype(F32), 0.0),
        axis=1,
        keepdims=True,
    ).astype(jnp.int32)
    inner_angles = ((order_col * iota((count, LANES), 1)) & (cycle_length - 1)).astype(F32) * (
        2.0 * math.pi / cycle_length
    )
    scale_factor = 1.0 / math.sqrt(cycle_length)
    inner_cos = jnp.cos(inner_angles) * scale_factor
    inner_sin = jnp.sin(inner_angles) * scale_factor
    inner_cos_ref[...] = inner_cos
    inner_sin_ref[...] = inner_sin
    step = 2.0 * math.pi / outer
    twice = ((order_col * iota((count, LANES), 1)) & (outer - 1)).astype(F32) * step
    cos_hi, cos_lo = halves(jnp.cos(twice))
    sin_hi, sin_lo = halves(jnp.sin(twice))
    outer_a_ref[:count, :LANES] = cos_hi
    outer_a_ref[:count, LANES:] = cos_lo
    outer_a_ref[count:, :LANES] = sin_hi
    outer_a_ref[count:, LANES:] = sin_lo
    across = ((order_row * iota((outer, count), 0)) & (outer - 1)).astype(F32) * step
    cos_hi, cos_lo = halves(jnp.cos(across))
    sin_hi, sin_lo = halves(-jnp.sin(across))
    outer_s_ref[:outer, :count] = cos_hi
    outer_s_ref[:outer, count:] = sin_hi
    outer_s_ref[outer:, :count] = cos_lo
    outer_s_ref[outer:, count:] = sin_lo

    fold(signs_ref.at[0], folded_ref)
    pixels = jnp.concatenate(
        [folded_ref[pl.ds(f, outer, stride=cycles), :] for f in range(cycles)], axis=1
    ).astype(BF16)
    parts = dot(outer_a_ref[:, :outer], pixels) + dot(
        outer_a_ref[:, LANES : LANES + outer], pixels
    )
    lane = iota((count, LANES), 1)
    acc = jnp.zeros((count, LANES), F32)
    width = slots * probes * 2
    for f in range(cycles):
        acc = twiddle_sums(
            parts[:, f * LANES : (f + 1) * LANES], inner_cos, inner_sin, acc, lane,
            f * width + own * 2,
        )
    sums_ref[...] = acc
    out = join_slots(sums_ref, slots, probes * 2)
    for p in range(probes):
        send_ref[p] = out


def latitude_columns(received, rows_ref, slots, probes, stack_ref):
    places = received.shape[0]
    total = rows_ref.shape[1]
    cycles = total // places
    width = slots * probes * 2
    lane = iota((places, LANES), 1)
    for f in range(cycles):
        value = turn(received, -f * width)
        high = value.astype(BF16).astype(F32)
        low = turn(value - high, width)
        stack_ref[pl.ds(f, places, stride=cycles), :] = jnp.where(
            lane < width, high, jnp.where(lane < 2 * width, low, 0.0)
        )
    chosen = jnp.where(iota((total, total), 0) == rows_ref[...], 1.0, 0.0).astype(BF16)
    return dot(chosen, stack_ref[...].astype(BF16)).astype(BF16), chosen


def degree_sums(leg_hi, leg_lo, columns, k, slots, probes, order, first_degree):
    rows = probes * 2
    width = slots * rows
    across = (dot(leg_hi, columns) + dot(leg_lo, columns)).T
    terms = across[k * rows : (k + 1) * rows] + across[
        width + k * rows : width + (k + 1) * rows
    ]
    degrees = first_degree + iota(terms.shape, 1)
    return jnp.where(degrees >= order, terms, 0.0)


def second_kernel(
    slots, orders_ref, received_ref, rows_ref, inv_signal_ref, legendre_ref,
    send_ref, terms_ref, stack_ref, spread_ref,
):
    probes = send_ref.shape[0]
    places = send_ref.shape[1]
    quarter = legendre_ref.shape[1]
    total = rows_ref.shape[1]
    cycles = total // places
    rows = probes * 2
    width = slots * rows
    own = lax.axis_index("probe")
    first_slot = lax.axis_index("sky") * slots

    received = received_ref[:places]
    for p in range(1, probes):
        received = received + received_ref[p * places : (p + 1) * places]
    columns, chosen = latitude_columns(received, rows_ref, slots, probes, stack_ref)
    first_degree = own * quarter
    signal = inv_signal_ref[:, pl.ds(pl.multiple_of(first_degree, LANES), quarter)]
    norm = jnp.zeros((rows, 1), F32)
    prior = jnp.zeros((rows, 1), F32)
    fields = []
    for k in range(slots):
        leg_hi, leg_lo = halves(legendre_ref[k])
        terms = degree_sums(
            leg_hi, leg_lo, columns, k, slots, probes, orders_ref[first_slot + k], first_degree
        )
        terms_ref[k] = terms
        squares = terms * terms
        norm = norm + jnp.sum(squares, axis=1, keepdims=True)
        prior = prior + jnp.sum(squares * signal, axis=1, keepdims=True)
        both = jnp.concatenate(halves(terms), axis=0)
        field = dot(both, leg_hi) + dot(both, leg_lo)
        fields.append(field[:rows] + field[rows:])
    fields = jnp.concatenate(fields, axis=0)
    both = jnp.concatenate(halves(fields), axis=0)
    by_cycle = dot(both, chosen)
    by_cycle = by_cycle[:width] + by_cycle[width:]
    spread_ref[...] = jnp.concatenate(
        [by_cycle, jnp.zeros((LANES - width, total), F32)], axis=0
    ).T
    row, lane = iota((rows, LANES), 0), iota((rows, LANES), 1)
    scalars = jnp.where(lane == SCALARS + row // 2, norm, 0.0)
    scalars = scalars + jnp.where(lane == SCALARS + probes + row // 2, prior, 0.0)
    out = jnp.broadcast_to(jnp.sum(scalars, axis=0, keepdims=True), (places, LANES))
    for f in range(cycles):
        out = out + turn(spread_ref[pl.ds(f, places, stride=cycles), :], f * width)
    for p in range(probes):
        send_ref[p] = out


def third_kernel(
    slots, received_ref, signs_ref, inv_noise_ref, inner_cos_ref, inner_sin_ref, outer_a_ref,
    outer_s_ref, send_ref, weighted_ref, scalars_ref, signs_folded, noise_folded, sums_ref,
    mapped_ref,
):
    places = send_ref.shape[0]
    probes = received_ref.shape[0] // places
    cycles = inv_noise_ref.shape[0]
    outer = signs_folded.shape[0] // cycles
    rows = probes * 2
    width = slots * rows
    own = lax.axis_index("probe")

    received = received_ref[:places]
    for p in range(1, probes):
        received = received + received_ref[p * places : (p + 1) * places]
    scalars_ref[...] = jnp.broadcast_to(
        jnp.sum(received, axis=0, keepdims=True), scalars_ref.shape
    )
    for s in range(slots):
        sums_ref[pl.ds(s, places, stride=slots), :] = turn(received, -s * rows)
    coeffs = sums_ref[...]
    count = coeffs.shape[0]
    fold(signs_ref.at[0], signs_folded)
    fold(inv_noise_ref, noise_folded)
    inner_cos, inner_sin = inner_cos_ref[...], inner_sin_ref[...]
    lane = iota((count, LANES), 1)
    acc = jnp.zeros((count, LANES), F32)
    totals = [jnp.zeros((1, LANES), F32) for _ in range(probes)]
    for f in range(cycles):
        high, low = [], []
        for p in range(probes):
            base = f * width + p * 2
            cos_coeff, sin_coeff = coeffs[:, base : base + 1], coeffs[:, base + 1 : base + 2]
            real = cos_coeff * inner_cos + sin_coeff * inner_sin
            imag = cos_coeff * inner_sin - sin_coeff * inner_cos
            hi, lo = halves(jnp.concatenate([real, imag], axis=0))
            high.append(hi)
            low.append(lo)
        high = jnp.concatenate(high, axis=1)
        low = jnp.concatenate(low, axis=1)
        mapped = dot(outer_s_ref[...], high)
        mapped = mapped[:outer] + mapped[outer:] + dot(outer_s_ref[:outer, :], low)
        mapped_ref[...] = mapped
        picked = mapped_ref[:, pl.ds(pl.multiple_of(own * LANES, LANES), LANES)]
        weighted_ref[pl.ds(f, outer, stride=cycles), :] = (
            picked * signs_folded[pl.ds(f, outer, stride=cycles), :]
        )
        noise = noise_folded[pl.ds(f, outer, stride=cycles), :]
        pixels = jnp.concatenate([noise] * probes, axis=1) * mapped
        power = jnp.sum(pixels * mapped, axis=0, keepdims=True)
        for p in range(probes):
            totals[p] = totals[p] + power[:, p * LANES : (p + 1) * LANES]
        hi, lo = halves(pixels)
        table_hi = outer_a_ref[:, :outer]
        parts = dot(table_hi, hi) + dot(table_hi, lo) + dot(
            outer_a_ref[:, LANES : LANES + outer], hi
        )
        for p in range(probes):
            acc = twiddle_sums(
                parts[:, p * LANES : (p + 1) * LANES], inner_cos, inner_sin, acc, lane,
                f * width + p * 2,
            )
    sums_ref[...] = acc
    out = join_slots(sums_ref, slots, rows)
    lane = iota((1, LANES), 1)
    for p in range(probes):
        value = jnp.sum(totals[p], axis=1, keepdims=True)
        out = out + jnp.where(lane == SCALARS + p, value, 0.0)
    send_ref[...] = out


def fourth_kernel(
    slots, orders_ref, received_ref, rows_ref, inv_signal_ref, legendre_ref, terms_ref,
    weighted_ref, scalars_ref, send_ref, stack_ref,
):
    probes = send_ref.shape[0]
    quarter = legendre_ref.shape[1]
    rows = probes * 2
    blocks = quarter // LANES
    own = lax.axis_index("probe")
    first_slot = lax.axis_index("sky") * slots
    received = received_ref[...]
    columns, _ = latitude_columns(received, rows_ref, slots, probes, stack_ref)
    first_degree = own * quarter
    signal = inv_signal_ref[:, pl.ds(pl.multiple_of(first_degree, LANES), quarter)]
    row, lane = iota((rows, LANES), 0), iota((rows, LANES), 1)

    def column(line, base):
        return jnp.sum(jnp.where(lane == base + row // 2, line, 0.0), axis=1, keepdims=True)

    noise_part = column(jnp.sum(received, axis=0, keepdims=True), SCALARS)
    norm = column(scalars_ref[:1], SCALARS)
    prior = column(scalars_ref[:1], SCALARS + probes)
    ratio = norm / (prior + noise_part)
    own_ratio = jnp.sum(
        jnp.where(iota((rows, 1), 0) == own * 2, ratio, 0.0), axis=0, keepdims=True
    )
    weighted = weighted_ref[...] * own_ratio
    for p in range(probes):
        send_ref[p, blocks * slots * 2 :, :] = weighted
    for k in range(slots):
        leg_hi, leg_lo = halves(legendre_ref[k])
        noise_terms = degree_sums(
            leg_hi, leg_lo, columns, k, slots, probes, orders_ref[first_slot + k], first_degree
        )
        terms = terms_ref[k]
        residual = terms - ratio * (signal * terms + noise_terms)
        for p in range(probes):
            for b in range(blocks):
                send_ref[p, pl.ds((b * slots + k) * 2, 2), :] = residual[
                    p * 2 : p * 2 + 2, b * LANES : (b + 1) * LANES
                ]


def last_kernel(received_ref, residual_ref, variance_ref):
    probes = received_ref.shape[0]
    slots = residual_ref.shape[1]
    quarter = residual_ref.shape[3] // probes
    blocks = quarter // LANES
    cycles, length = variance_ref.shape
    start = blocks * slots * 2
    total = received_ref[0, start:, :]
    for p in range(1, probes):
        total = total + received_ref[p, start:, :]
    total = total * (1.0 / probes)
    for j in range(length // LANES):
        variance_ref[:, j * LANES : (j + 1) * LANES] = total[j * cycles : (j + 1) * cycles]
    for x in range(probes):
        for b in range(blocks):
            for k in range(slots):
                place = x * quarter + b * LANES
                residual_ref[0, k, :, place : place + LANES] = received_ref[
                    x, pl.ds((b * slots + k) * 2, 2), :
                ]


def call(kernel, outs, scratch, in_smem, args, name):
    vmem = pl.BlockSpec(memory_space=pltpu.VMEM)
    smem = pl.BlockSpec(memory_space=pltpu.SMEM)
    return pl.pallas_call(
        kernel,
        out_shape=[jax.ShapeDtypeStruct(shape, dtype) for shape, dtype in outs],
        in_specs=[smem if i in in_smem else vmem for i in range(len(args))],
        out_specs=[vmem] * len(outs),
        scratch_shapes=[pltpu.VMEM(shape, dtype) for shape, dtype in scratch],
        compiler_params=pltpu.CompilerParams(vmem_limit_bytes=VMEM_BYTES),
        name=name,
    )(*args)


def per_device(legendre, signs, inv_noise, inv_signal, harmonic_order_values, cycle_rows):
    slots, quarter, total = legendre.shape
    _, cycles, length = signs.shape
    probes = lax.axis_size("probe")
    places = lax.axis_size("sky")
    count = harmonic_order_values.shape[0]
    outer = length // LANES
    rows = probes * 2
    orders = harmonic_order_values
    order_row = orders.reshape(1, count)
    row_line = cycle_rows.reshape(1, total)
    signal_line = inv_signal.reshape(1, probes * quarter)

    def everywhere(send):
        return lax.all_to_all(
            send.reshape(probes * places, LANES), ("probe", "sky"), 0, 0, tiled=True
        )

    send, inner_cos, inner_sin, outer_a, outer_s = call(
        functools.partial(first_kernel, slots),
        [
            ((probes, places, LANES), F32),
            ((count, LANES), F32),
            ((count, LANES), F32),
            ((2 * count, 2 * LANES), BF16),
            ((2 * outer, 2 * count), BF16),
        ],
        [((outer * cycles, LANES), F32), ((count, LANES), F32)],
        (),
        (order_row, signs),
        "cycle_sums",
    )
    received = everywhere(send)
    send, terms = call(
        functools.partial(second_kernel, slots),
        [((probes, places, LANES), F32), ((slots, rows, quarter), F32)],
        [((total, LANES), F32), ((total, LANES), F32)],
        (0,),
        (orders, received, row_line, signal_line, legendre),
        "degrees_there_and_back",
    )
    received = everywhere(send)
    send, weighted, scalars = call(
        functools.partial(third_kernel, slots),
        [((places, LANES), F32), ((outer * cycles, LANES), F32), ((8, LANES), F32)],
        [
            ((outer * cycles, LANES), F32),
            ((outer * cycles, LANES), F32),
            ((count, LANES), F32),
            ((outer, probes * LANES), F32),
        ],
        (),
        (received, signs, inv_noise, inner_cos, inner_sin, outer_a, outer_s),
        "cycles_there_and_back",
    )
    received = lax.all_to_all(send, "sky", 0, 0, tiled=True)
    height = quarter // LANES * slots * 2 + outer * cycles
    (send,) = call(
        functools.partial(fourth_kernel, slots),
        [((probes, height, LANES), F32)],
        [((total, LANES), F32)],
        (0,),
        (orders, received, row_line, signal_line, legendre, terms, weighted, scalars),
        "residual_terms",
    )
    received = lax.all_to_all(send, "probe", 0, 0, tiled=True)
    residual, variance = call(
        last_kernel,
        [((1, slots, 2, probes * quarter), F32), ((cycles, length), F32)],
        [],
        (),
        (received,),
        "outputs",
    )
    return residual, variance


def solution(mesh):
    in_specs = (P("sky", "probe", None), P("probe", "sky", None), P("sky", None), P(), P(), P())
    out_specs = (P("probe", "sky", None, None), P("sky", None))
    return jax.shard_map(
        per_device, mesh=mesh, in_specs=in_specs, out_specs=out_specs, check_vma=False
    )
```

```python
import functools
import math

import jax
import jax.numpy as jnp
from jax import lax
from jax.experimental import pallas as pl
from jax.experimental.pallas import tpu as pltpu
from jax.sharding import PartitionSpec as P

F32 = jnp.float32
BF16 = jnp.bfloat16
LANES = 128
SCALARS = 64
VMEM_BYTES = 24 * 1024 * 1024


def iota(shape, dim):
    return lax.broadcasted_iota(jnp.int32, shape, dim)


def dot(a, b):
    return jnp.dot(a, b, preferred_element_type=F32)


def halves(value):
    high = value.astype(BF16)
    return high, (value - high.astype(F32)).astype(BF16)


def turn(value, lanes):
    lanes = lanes % LANES
    return pltpu.roll(value, lanes, 1) if lanes else value


def fold(flat_ref, folded_ref):
    cycles = flat_ref.shape[-2]
    for j in range(folded_ref.shape[0] // cycles):
        folded_ref[j * cycles : (j + 1) * cycles, :] = flat_ref[
            :, j * LANES : (j + 1) * LANES
        ].astype(F32)


def twiddle_sums(parts, inner_cos, inner_sin, acc, lane, base):
    count = inner_cos.shape[0]
    real, imag = parts[:count], parts[count:]
    cos_sum = jnp.sum(inner_cos * real - inner_sin * imag, axis=1, keepdims=True)
    sin_sum = jnp.sum(inner_sin * real + inner_cos * imag, axis=1, keepdims=True)
    acc = jnp.where(lane == base, cos_sum, acc)
    return jnp.where(lane == base + 1, sin_sum, acc)


def gather_rows(by_row_ref, places, shifts):
    out = by_row_ref[pl.ds(0, places, stride=len(shifts)), :]
    for s in range(1, len(shifts)):
        out = out + turn(by_row_ref[pl.ds(s, places, stride=len(shifts)), :], shifts[s])
    return out


def own_half(received_ref, source, groups):
    places = received_ref.shape[1] // groups
    total = received_ref[source, :places]
    for g in range(1, groups):
        total = total + received_ref[source, g * places : (g + 1) * places]
    return jnp.where(lax.axis_index("core") == 0, total, turn(total, LANES // 2))


def first_kernel(
    slots, orders_hbm, signs_hbm, rows_hbm, signal_hbm, noise_hbm, legendre_hbm,
    send_ref, inner_cos_ref, inner_sin_ref, outer_a_ref, outer_s_ref, limits_ref, signs_ref,
    rows_ref, signal_ref, noise_ref, legendre_ref,
    orders_ref, folded_ref, sums_ref, sems,
):
    count = orders_ref.shape[1]
    probes, places = send_ref.shape[:2]
    cycles = signs_ref.shape[1]
    outer = folded_ref.shape[0] // cycles
    cycle_length = outer * LANES
    cores = count // slots // places
    own = lax.axis_index("probe")
    quarter = signal_ref.shape[1]
    own_signal = signal_hbm.at[:, pl.ds(pl.multiple_of(own * quarter, LANES), quarter)]

    copies = [
        pltpu.make_async_copy(source, target, sems.at[n])
        for n, (source, target) in enumerate(
            [
                (orders_hbm, orders_ref),
                (signs_hbm, signs_ref),
                (rows_hbm, rows_ref),
                (own_signal, signal_ref),
                (noise_hbm, noise_ref),
                (legendre_hbm, legendre_ref),
            ]
        )
    ]
    for copy in copies:
        copy.start()
    copies[0].wait()

    order_row = orders_ref[...]
    first_slot = (lax.axis_index("place") * cores + lax.axis_index("core")) * slots
    for k in range(slots):
        picked = jnp.where(iota((1, count), 1) == first_slot + k, order_row, 0).astype(F32)
        picked = jnp.sum(picked, axis=1, keepdims=True).astype(jnp.int32)
        limits_ref[k : k + 1, :] = jnp.broadcast_to(picked, (1, LANES))
    order_col = jnp.sum(
        jnp.where(iota((count, count), 0) == iota((count, count), 1), order_row.astype(F32), 0.0),
        axis=1,
        keepdims=True,
    ).astype(jnp.int32)
    inner_angles = ((order_col * iota((count, LANES), 1)) & (cycle_length - 1)).astype(F32) * (
        2.0 * math.pi / cycle_length
    )
    scale_factor = 1.0 / math.sqrt(cycle_length)
    inner_cos = jnp.cos(inner_angles) * scale_factor
    inner_sin = jnp.sin(inner_angles) * scale_factor
    inner_cos_ref[...] = inner_cos
    inner_sin_ref[...] = inner_sin
    step = 2.0 * math.pi / outer
    twice = ((order_col * iota((count, LANES), 1)) & (outer - 1)).astype(F32) * step
    cos_hi, cos_lo = halves(jnp.cos(twice))
    sin_hi, sin_lo = halves(jnp.sin(twice))
    outer_a_ref[:count, :LANES] = cos_hi
    outer_a_ref[:count, LANES:] = cos_lo
    outer_a_ref[count:, :LANES] = sin_hi
    outer_a_ref[count:, LANES:] = sin_lo
    across = ((order_row * iota((outer, count), 0)) & (outer - 1)).astype(F32) * step
    cos_hi, cos_lo = halves(jnp.cos(across))
    sin_hi, sin_lo = halves(-jnp.sin(across))
    outer_s_ref[:outer, :count] = cos_hi
    outer_s_ref[:outer, count:] = sin_hi
    outer_s_ref[outer:, :count] = cos_lo
    outer_s_ref[outer:, count:] = sin_lo

    copies[1].wait()
    fold(signs_ref.at[0], folded_ref)
    pixels = jnp.concatenate(
        [folded_ref[pl.ds(f, outer, stride=cycles), :] for f in range(cycles)], axis=1
    ).astype(BF16)
    parts = dot(outer_a_ref[:, :outer], pixels) + dot(
        outer_a_ref[:, LANES : LANES + outer], pixels
    )
    lane = iota((count, LANES), 1)
    acc = jnp.zeros((count, LANES), F32)
    rows = probes * 2
    for f in range(cycles):
        acc = twiddle_sums(
            parts[:, f * LANES : (f + 1) * LANES], inner_cos, inner_sin, acc, lane,
            f * slots * rows + own * 2,
        )
    sums_ref[...] = acc
    shifts = [c * (LANES // 2) + k * rows for c in range(cores) for k in range(slots)]
    out = gather_rows(sums_ref, places, shifts)
    for p in range(probes):
        send_ref[p] = out
    for copy in copies[2:]:
        copy.wait()


def latitude_columns(received, cores, rows_ref, width, stack_ref):
    total = rows_ref.shape[1]
    for c in range(cores):
        values = received(c)
        places = values.shape[0]
        cycles = total // (places * cores)
        lane = iota((places, LANES), 1)
        for f in range(cycles):
            value = turn(values, -f * width)
            high = value.astype(BF16).astype(F32)
            low = turn(value - high, width)
            stack_ref[pl.ds(c * cycles + f, places, stride=cores * cycles), :] = jnp.where(
                lane < width, high, jnp.where(lane < 2 * width, low, 0.0)
            )
    chosen = jnp.where(iota((total, total), 0) == rows_ref[...], 1.0, 0.0).astype(BF16)
    return dot(chosen, stack_ref[...].astype(BF16)).astype(BF16), chosen


def degree_sums(leg_hi, leg_lo, columns, k, rows, width, order, first_degree):
    across = (dot(leg_hi, columns) + dot(leg_lo, columns)).T
    terms = across[k * rows : (k + 1) * rows] + across[
        width + k * rows : width + (k + 1) * rows
    ]
    degrees = first_degree + iota(terms.shape, 1)
    return jnp.where(degrees >= order, terms, 0.0)


def second_kernel(
    received_ref, rows_ref, signal_ref, limits_ref, legendre_ref,
    send_ref, terms_ref, scalars_ref, hi_ref, lo_ref, stack_ref, spread_ref,
):
    cores = received_ref.shape[0]
    probes, places = send_ref.shape[:2]
    slots, quarter, total = legendre_ref.shape
    cycles = total // (places * cores)
    rows = probes * 2
    width = slots * rows
    columns, chosen = latitude_columns(
        lambda c: own_half(received_ref, c, probes), cores, rows_ref, width, stack_ref
    )
    first_degree = lax.axis_index("probe") * quarter
    signal = signal_ref[...]
    norm = jnp.zeros((rows, 1), F32)
    prior = jnp.zeros((rows, 1), F32)
    fields = []
    for k in range(slots):
        leg_hi, leg_lo = halves(legendre_ref[k])
        hi_ref[k] = leg_hi
        lo_ref[k] = leg_lo
        terms = degree_sums(
            leg_hi, leg_lo, columns, k, rows, width, limits_ref[k : k + 1, :1], first_degree
        )
        terms_ref[k] = terms
        squares = terms * terms
        norm = norm + jnp.sum(squares, axis=1, keepdims=True)
        prior = prior + jnp.sum(squares * signal, axis=1, keepdims=True)
        both = jnp.concatenate(halves(terms), axis=0)
        field = dot(both, leg_hi) + dot(both, leg_lo)
        fields.append(field[:rows] + field[rows:])
    fields = jnp.concatenate(fields, axis=0)
    both = jnp.concatenate(halves(fields), axis=0)
    by_cycle = dot(both, chosen)
    by_cycle = by_cycle[:width] + by_cycle[width:]
    spread_ref[...] = jnp.concatenate(
        [by_cycle, jnp.zeros((LANES - width, total), F32)], axis=0
    ).T
    out = gather_rows(spread_ref, places, [s * width for s in range(cores * cycles)])
    for p in range(probes):
        send_ref[p] = out
    row, lane = iota((rows, LANES), 0), iota((rows, LANES), 1)
    scalars = jnp.where(lane == SCALARS + row // 2, norm, 0.0)
    scalars = scalars + jnp.where(lane == SCALARS + probes + row // 2, prior, 0.0)
    scalars_ref[...] = jnp.broadcast_to(
        jnp.sum(scalars, axis=0, keepdims=True), scalars_ref.shape
    )


def third_kernel(
    slots, received_ref, signs_ref, inv_noise_ref, inner_cos_ref, inner_sin_ref, outer_a_ref,
    outer_s_ref, scalars_ref, send_ref, weighted_ref, signs_folded, noise_folded, sums_ref,
    mapped_ref,
):
    cores = received_ref.shape[0]
    all_places = send_ref.shape[0]
    places = all_places // cores
    probes = received_ref.shape[1] // places
    cycles = inv_noise_ref.shape[0]
    outer = signs_folded.shape[0] // cycles
    rows = probes * 2
    width = slots * rows
    own = lax.axis_index("probe")

    for c in range(cores):
        received = own_half(received_ref, c, probes)
        for k in range(slots):
            sums_ref[pl.ds(c * slots + k, places, stride=cores * slots), :] = turn(
                received, -k * rows
            )
    coeffs = sums_ref[...]
    count = coeffs.shape[0]
    fold(signs_ref.at[0], signs_folded)
    fold(inv_noise_ref, noise_folded)
    inner_cos, inner_sin = inner_cos_ref[...], inner_sin_ref[...]
    lane = iota((count, LANES), 1)
    acc = jnp.zeros((count, LANES), F32)
    totals = [jnp.zeros((1, LANES), F32) for _ in range(probes)]
    for f in range(cycles):
        high, low = [], []
        for p in range(probes):
            base = f * width + p * 2
            cos_coeff, sin_coeff = coeffs[:, base : base + 1], coeffs[:, base + 1 : base + 2]
            real = cos_coeff * inner_cos + sin_coeff * inner_sin
            imag = cos_coeff * inner_sin - sin_coeff * inner_cos
            hi, lo = halves(jnp.concatenate([real, imag], axis=0))
            high.append(hi)
            low.append(lo)
        high = jnp.concatenate(high, axis=1)
        low = jnp.concatenate(low, axis=1)
        mapped = dot(outer_s_ref[...], high)
        mapped = mapped[:outer] + mapped[outer:] + dot(outer_s_ref[:outer, :], low)
        mapped_ref[...] = mapped
        picked = mapped_ref[:, pl.ds(pl.multiple_of(own * LANES, LANES), LANES)]
        weighted_ref[pl.ds(f, outer, stride=cycles), :] = (
            picked * signs_folded[pl.ds(f, outer, stride=cycles), :]
        )
        noise = noise_folded[pl.ds(f, outer, stride=cycles), :]
        pixels = jnp.concatenate([noise] * probes, axis=1) * mapped
        power = jnp.sum(pixels * mapped, axis=0, keepdims=True)
        for p in range(probes):
            totals[p] = totals[p] + power[:, p * LANES : (p + 1) * LANES]
        hi, lo = halves(pixels)
        table_hi = outer_a_ref[:, :outer]
        parts = dot(table_hi, hi) + dot(table_hi, lo) + dot(
            outer_a_ref[:, LANES : LANES + outer], hi
        )
        for p in range(probes):
            acc = twiddle_sums(
                parts[:, p * LANES : (p + 1) * LANES], inner_cos, inner_sin, acc, lane,
                f * width + p * 2,
            )
    sums_ref[...] = acc
    out = gather_rows(sums_ref, all_places, [k * rows for k in range(slots)])
    line = scalars_ref[:1]
    lane = iota((1, LANES), 1)
    for p in range(probes):
        value = jnp.sum(totals[p], axis=1, keepdims=True)
        line = line + jnp.where(lane == SCALARS + 2 * probes + p, value, 0.0)
    send_ref[...] = out + line


def fourth_kernel(
    received_ref, rows_ref, signal_ref, limits_ref, hi_ref, lo_ref, terms_ref, weighted_ref,
    send_ref, stack_ref,
):
    probes = send_ref.shape[0]
    slots, quarter, _ = hi_ref.shape
    rows = probes * 2
    blocks = quarter // LANES
    block_rows = blocks * slots * 2
    received = received_ref[...]
    columns, _ = latitude_columns(lambda c: received, 1, rows_ref, slots * rows, stack_ref)
    first_degree = lax.axis_index("probe") * quarter
    signal = signal_ref[...]
    line = jnp.broadcast_to(jnp.sum(received, axis=0, keepdims=True), (8, LANES))
    for p in range(probes):
        send_ref[p, 2 * block_rows : 2 * block_rows + 8, :] = line
        send_ref[p, 2 * block_rows + 8 :, :] = weighted_ref[...]
    for k in range(slots):
        noise_terms = degree_sums(
            hi_ref[k], lo_ref[k], columns, k, rows, slots * rows, limits_ref[k : k + 1, :1],
            first_degree,
        )
        terms = terms_ref[k]
        image = signal * terms + noise_terms
        for p in range(probes):
            for b in range(blocks):
                place = (b * slots + k) * 2
                own = (slice(p * 2, p * 2 + 2), slice(b * LANES, (b + 1) * LANES))
                send_ref[p, place : place + 2, :] = terms[own]
                send_ref[p, block_rows + place : block_rows + place + 2, :] = image[own]


def last_kernel(received_ref, residual_ref, variance_ref):
    probes = received_ref.shape[0]
    slots = residual_ref.shape[1]
    quarter = residual_ref.shape[3] // probes
    blocks = quarter // LANES
    block_rows = blocks * slots * 2
    cycles, length = variance_ref.shape
    own = lax.axis_index("probe")
    lane = iota((8, LANES), 1)
    lines = [received_ref[p, 2 * block_rows : 2 * block_rows + 8, :] for p in range(probes)]
    degree_line = lines[0]
    for p in range(1, probes):
        degree_line = degree_line + lines[p]

    def ratio(p):
        def value(line, base):
            return jnp.sum(jnp.where(lane == base + p, line, 0.0), axis=1, keepdims=True)

        norm = value(degree_line, SCALARS)
        prior = value(degree_line, SCALARS + probes)
        return norm / (prior + value(lines[0], SCALARS + 2 * probes))

    start = 2 * block_rows + 8
    total = received_ref[0, start:, :] * ratio(0)[:1]
    for p in range(1, probes):
        total = total + received_ref[p, start:, :] * ratio(p)[:1]
    total = total * (1.0 / probes)
    for j in range(length // LANES):
        variance_ref[:, j * LANES : (j + 1) * LANES] = total[j * cycles : (j + 1) * cycles]
    own_ratio = ratio(own)[:1]
    for x in range(probes):
        residual = (
            received_ref[x, :block_rows, :]
            - own_ratio * received_ref[x, block_rows : 2 * block_rows, :]
        )
        for b in range(blocks):
            for k in range(slots):
                place = x * quarter + b * LANES
                row = (b * slots + k) * 2
                residual_ref[0, k, :, place : place + LANES] = residual[row : row + 2]


def call(kernel, outs, scratch, args, name, space=pltpu.VMEM):
    return pl.pallas_call(
        kernel,
        out_shape=[jax.ShapeDtypeStruct(shape, dtype) for shape, dtype in outs],
        in_specs=[pl.BlockSpec(memory_space=space)] * len(args),
        out_specs=[pl.BlockSpec(memory_space=pltpu.VMEM)] * len(outs),
        scratch_shapes=scratch,
        compiler_params=pltpu.CompilerParams(vmem_limit_bytes=VMEM_BYTES),
        name=name,
    )(*args)


def per_device(legendre, signs, inv_noise, inv_signal, harmonic_order_values, cycle_rows):
    slots, quarter, total = legendre.shape
    _, cycles, length = signs.shape
    probes = lax.axis_size("probe")
    places = lax.axis_size("place")
    cores = lax.axis_size("core")
    count = harmonic_order_values.shape[0]
    outer = length // LANES
    rows = probes * 2
    wide = ((total, LANES), F32)
    by_order = ((count, LANES), F32)
    folded = ((outer * cycles, LANES), F32)

    def everywhere(send):
        received = lax.all_to_all(
            send.reshape(probes * places, LANES), ("probe", "place"), 0, 0, tiled=True
        )
        return lax.all_gather(received, "core", axis=0)

    (
        send, inner_cos, inner_sin, outer_a, outer_s, limits, signs_near, row_line, signal,
        noise_near, legendre_near,
    ) = call(
        functools.partial(first_kernel, slots),
        [
            ((probes, places, LANES), F32),
            by_order,
            by_order,
            ((2 * count, 2 * LANES), BF16),
            ((2 * outer, 2 * count), BF16),
            ((8, LANES), jnp.int32),
            (signs.shape, jnp.int32),
            ((1, total), jnp.int32),
            ((1, quarter), F32),
            (inv_noise.shape, F32),
            (legendre.shape, F32),
        ],
        [
            pltpu.VMEM((1, count), jnp.int32),
            pltpu.VMEM(*folded),
            pltpu.VMEM(*by_order),
            pltpu.SemaphoreType.DMA((6,)),
        ],
        (
            harmonic_order_values.reshape(1, count), signs, cycle_rows.reshape(1, total),
            inv_signal.reshape(1, probes * quarter), inv_noise, legendre,
        ),
        "cycle_sums",
        pltpu.HBM,
    )
    received = everywhere(send)
    send, terms, scalars, leg_hi, leg_lo = call(
        second_kernel,
        [
            ((probes, places, LANES), F32),
            ((slots, rows, quarter), F32),
            ((8, LANES), F32),
            (legendre.shape, BF16),
            (legendre.shape, BF16),
        ],
        [pltpu.VMEM(*wide), pltpu.VMEM(*wide)],
        (received, row_line, signal, limits, legendre_near),
        "degrees_there_and_back",
    )
    received = everywhere(send)
    send, weighted = call(
        functools.partial(third_kernel, slots),
        [((places * cores, LANES), F32), folded],
        [
            pltpu.VMEM(*folded),
            pltpu.VMEM(*folded),
            pltpu.VMEM(*by_order),
            pltpu.VMEM((outer, probes * LANES), F32),
        ],
        (
            received, signs_near, noise_near, inner_cos, inner_sin, outer_a, outer_s, scalars,
        ),
        "cycles_there_and_back",
    )
    received = lax.all_to_all(send, ("place", "core"), 0, 0, tiled=True)
    height = quarter // LANES * slots * 4 + 8 + outer * cycles
    (send,) = call(
        fourth_kernel,
        [((probes, height, LANES), F32)],
        [pltpu.VMEM(*wide)],
        (received, row_line, signal, limits, leg_hi, leg_lo, terms, weighted),
        "image_terms",
    )
    received = lax.all_to_all(send, "probe", 0, 0, tiled=True)
    return call(
        last_kernel,
        [((1, slots, 2, probes * quarter), F32), ((cycles, length), F32)],
        [],
        (received,),
        "outputs",
    )


def solution(mesh):
    cores = 2
    split = jax.sharding.Mesh(
        mesh.devices.reshape(mesh.shape["probe"], -1, cores), ("probe", "place", "core")
    )
    sky = ("place", "core")
    in_specs = (P(sky, "probe", None), P("probe", sky, None), P(sky, None), P(), P(), P())
    out_specs = (P("probe", sky, None, None), P(sky, None))

    def run(*args):
        return tuple(
            jax.shard_map(
                per_device, mesh=split, in_specs=in_specs, out_specs=out_specs, check_vma=False
            )(*args)
        )

    return run
```

```python
import functools
import math

import jax
import jax.numpy as jnp
from jax import lax
from jax.experimental import pallas as pl
from jax.experimental.pallas import tpu as pltpu
from jax.sharding import PartitionSpec as P

F32 = jnp.float32
BF16 = jnp.bfloat16
LANES = 128
SCALARS = 64
VMEM_BYTES = 24 * 1024 * 1024


def iota(shape, dim):
    return lax.broadcasted_iota(jnp.int32, shape, dim)


def dot(a, b):
    return jnp.dot(a, b, preferred_element_type=F32)


def dot_rows(a, b):
    return lax.dot_general(a, b, (((1,), (1,)), ((), ())), preferred_element_type=F32)


def halves(value):
    high = value.astype(BF16)
    return high, (value - high.astype(F32)).astype(BF16)


def turn(value, lanes):
    lanes = lanes % LANES
    return pltpu.roll(value, lanes, 1) if lanes else value


def fold(flat_ref, folded_ref):
    cycles = flat_ref.shape[-2]
    for j in range(folded_ref.shape[0] // cycles):
        folded_ref[j * cycles : (j + 1) * cycles, :] = flat_ref[
            :, j * LANES : (j + 1) * LANES
        ].astype(F32)


def outer_sums(table_ref, hi, lo):
    repeat = LANES // hi.shape[0]
    return dot(table_ref[...], jnp.concatenate([hi, lo] * repeat, axis=0))


def twiddle_sums(parts, inner_cos, inner_sin, acc, lane, base):
    count = inner_cos.shape[0]
    real, imag = parts[:count], parts[count:]
    cos_sum = jnp.sum(inner_cos * real - inner_sin * imag, axis=1, keepdims=True)
    sin_sum = jnp.sum(inner_sin * real + inner_cos * imag, axis=1, keepdims=True)
    acc = jnp.where(lane == base, cos_sum, acc)
    return jnp.where(lane == base + 1, sin_sum, acc)


def gather_rows(by_row_ref, places, shifts):
    out = by_row_ref[pl.ds(0, places, stride=len(shifts)), :]
    for s in range(1, len(shifts)):
        out = out + turn(by_row_ref[pl.ds(s, places, stride=len(shifts)), :], shifts[s])
    return out


def own_half(received_ref, source, groups):
    places = received_ref.shape[1] // groups
    total = received_ref[source, :places]
    for g in range(1, groups):
        total = total + received_ref[source, g * places : (g + 1) * places]
    return jnp.where(lax.axis_index("core") == 0, total, turn(total, LANES // 2))


def first_kernel(
    slots, orders_hbm, signs_hbm, rows_hbm, signal_hbm, noise_hbm, legendre_hbm,
    send_ref, inner_cos_ref, inner_sin_ref, outer_a_ref, outer_s_ref, limits_ref, signs_ref,
    rows_ref, signal_ref, noise_ref, legendre_ref,
    orders_ref, folded_ref, sums_ref, sems,
):
    count = orders_ref.shape[1]
    probes, places = send_ref.shape[:2]
    cycles = signs_ref.shape[1]
    outer = folded_ref.shape[0] // cycles
    cycle_length = outer * LANES
    cores = count // slots // places
    own = lax.axis_index("probe")
    quarter = signal_ref.shape[1]
    own_signal = signal_hbm.at[:, pl.ds(pl.multiple_of(own * quarter, LANES), quarter)]

    copies = [
        pltpu.make_async_copy(source, target, sems.at[n])
        for n, (source, target) in enumerate(
            [
                (orders_hbm, orders_ref),
                (signs_hbm, signs_ref),
                (rows_hbm, rows_ref),
                (own_signal, signal_ref),
                (noise_hbm, noise_ref),
                (legendre_hbm, legendre_ref),
            ]
        )
    ]
    for copy in copies:
        copy.start()
    copies[0].wait()

    order_row = orders_ref[...]
    first_slot = (lax.axis_index("place") * cores + lax.axis_index("core")) * slots
    for k in range(slots):
        picked = jnp.where(iota((1, count), 1) == first_slot + k, order_row, 0).astype(F32)
        picked = jnp.sum(picked, axis=1, keepdims=True).astype(jnp.int32)
        limits_ref[k : k + 1, :] = jnp.broadcast_to(picked, (1, LANES))
    order_col = jnp.sum(
        jnp.where(iota((count, count), 0) == iota((count, count), 1), order_row.astype(F32), 0.0),
        axis=1,
        keepdims=True,
    ).astype(jnp.int32)
    inner_angles = ((order_col * iota((count, LANES), 1)) & (cycle_length - 1)).astype(F32) * (
        2.0 * math.pi / cycle_length
    )
    scale_factor = 1.0 / math.sqrt(cycle_length)
    inner_cos = jnp.cos(inner_angles) * scale_factor
    inner_sin = jnp.sin(inner_angles) * scale_factor
    inner_cos_ref[...] = inner_cos
    inner_sin_ref[...] = inner_sin
    step = 2.0 * math.pi / outer
    twice = ((order_col * iota((count, LANES), 1)) & (outer - 1)).astype(F32) * step
    cos_hi, cos_lo = halves(jnp.cos(twice))
    sin_hi, sin_lo = halves(jnp.sin(twice))
    outer_a_ref[:count, :LANES] = cos_hi
    outer_a_ref[:count, LANES:] = cos_lo
    outer_a_ref[count:, :LANES] = sin_hi
    outer_a_ref[count:, LANES:] = sin_lo
    across = ((order_row * iota((outer, count), 0)) & (outer - 1)).astype(F32) * step
    cos_hi, cos_lo = halves(jnp.cos(across))
    sin_hi, sin_lo = halves(-jnp.sin(across))
    outer_s_ref[:outer, :count] = cos_hi
    outer_s_ref[:outer, count:] = sin_hi
    outer_s_ref[outer:, :count] = cos_lo
    outer_s_ref[outer:, count:] = sin_lo

    copies[1].wait()
    fold(signs_ref.at[0], folded_ref)
    pixels = jnp.concatenate(
        [folded_ref[pl.ds(f, outer, stride=cycles), :] for f in range(cycles)], axis=1
    ).astype(BF16)
    parts = outer_sums(outer_a_ref, pixels, jnp.zeros_like(pixels))
    lane = iota((count, LANES), 1)
    acc = jnp.zeros((count, LANES), F32)
    rows = probes * 2
    for f in range(cycles):
        acc = twiddle_sums(
            parts[:, f * LANES : (f + 1) * LANES], inner_cos, inner_sin, acc, lane,
            f * slots * rows + own * 2,
        )
    sums_ref[...] = acc
    shifts = [c * (LANES // 2) + k * rows for c in range(cores) for k in range(slots)]
    out = gather_rows(sums_ref, places, shifts)
    for p in range(probes):
        send_ref[p] = out
    for copy in copies[2:]:
        copy.wait()


def latitude_columns(received, cores, rows_ref, width, stack_ref):
    total = rows_ref.shape[1]
    for c in range(cores):
        values = received(c)
        places = values.shape[0]
        cycles = total // (places * cores)
        lane = iota((places, LANES), 1)
        for f in range(cycles):
            value = turn(values, -f * width)
            high = value.astype(BF16).astype(F32)
            low = turn(value - high, width)
            stack_ref[pl.ds(c * cycles + f, places, stride=cores * cycles), :] = jnp.where(
                lane < width, high, jnp.where(lane < 2 * width, low, 0.0)
            )
    chosen = jnp.where(iota((total, total), 0) == rows_ref[...], 1.0, 0.0).astype(BF16)
    turned = stack_ref[...].T[: 2 * width].astype(BF16)
    return dot_rows(turned, chosen).astype(BF16), chosen


def degree_sums(leg_hi, leg_lo, columns, k, rows, width, order, first_degree):
    across = dot_rows(columns, leg_hi) + dot_rows(columns, leg_lo)
    terms = across[k * rows : (k + 1) * rows] + across[
        width + k * rows : width + (k + 1) * rows
    ]
    degrees = first_degree + iota(terms.shape, 1)
    return jnp.where(degrees >= order, terms, 0.0)


def second_kernel(
    received_ref, rows_ref, signal_ref, limits_ref, legendre_ref,
    send_ref, terms_ref, scalars_ref, hi_ref, lo_ref, stack_ref, spread_ref,
):
    cores = received_ref.shape[0]
    probes, places = send_ref.shape[:2]
    slots, quarter, total = hi_ref.shape
    cycles = total // (places * cores)
    rows = probes * 2
    width = slots * rows
    columns, chosen = latitude_columns(
        lambda c: own_half(received_ref, c, probes), cores, rows_ref, width, stack_ref
    )
    first_degree = lax.axis_index("probe") * quarter
    signal = signal_ref[...]
    norm = jnp.zeros((rows, 1), F32)
    prior = jnp.zeros((rows, 1), F32)
    fields = []
    for k in range(slots):
        leg_hi, leg_lo = halves(legendre_ref[k])
        hi_ref[k] = leg_hi
        lo_ref[k] = leg_lo
        terms = degree_sums(
            leg_hi, leg_lo, columns, k, rows, width, limits_ref[k : k + 1, :1], first_degree
        )
        terms_ref[k] = terms
        squares = terms * terms
        norm = norm + jnp.sum(squares, axis=1, keepdims=True)
        prior = prior + jnp.sum(squares * signal, axis=1, keepdims=True)
        both = jnp.concatenate(halves(terms), axis=0)
        field = dot(both, leg_hi) + dot(both, leg_lo)
        fields.append(field[:rows] + field[rows:])
    fields = jnp.concatenate(fields, axis=0)
    both = jnp.concatenate(halves(fields), axis=0)
    by_cycle = dot(both, chosen)
    by_cycle = by_cycle[:width] + by_cycle[width:]
    spread_ref[...] = jnp.concatenate(
        [by_cycle, jnp.zeros((LANES - width, total), F32)], axis=0
    ).T
    out = gather_rows(spread_ref, places, [s * width for s in range(cores * cycles)])
    for p in range(probes):
        send_ref[p] = out
    row, lane = iota((rows, LANES), 0), iota((rows, LANES), 1)
    scalars = jnp.where(lane == SCALARS + row // 2, norm, 0.0)
    scalars = scalars + jnp.where(lane == SCALARS + probes + row // 2, prior, 0.0)
    scalars_ref[...] = jnp.broadcast_to(
        jnp.sum(scalars, axis=0, keepdims=True), scalars_ref.shape
    )


def third_kernel(
    slots, received_ref, signs_ref, inv_noise_ref, inner_cos_ref, inner_sin_ref, outer_a_ref,
    outer_s_ref, scalars_ref, send_ref, weighted_ref, signs_folded, noise_folded, sums_ref,
    mapped_ref,
):
    cores = received_ref.shape[0]
    all_places = send_ref.shape[0]
    places = all_places // cores
    probes = received_ref.shape[1] // places
    cycles = inv_noise_ref.shape[0]
    outer = signs_folded.shape[0] // cycles
    rows = probes * 2
    width = slots * rows
    own = lax.axis_index("probe")

    for c in range(cores):
        received = own_half(received_ref, c, probes)
        for k in range(slots):
            sums_ref[pl.ds(c * slots + k, places, stride=cores * slots), :] = turn(
                received, -k * rows
            )
    coeffs = sums_ref[...]
    count = coeffs.shape[0]
    fold(signs_ref.at[0], signs_folded)
    fold(inv_noise_ref, noise_folded)
    inner_cos, inner_sin = inner_cos_ref[...], inner_sin_ref[...]
    lane = iota((count, LANES), 1)
    acc = jnp.zeros((count, LANES), F32)
    totals = [jnp.zeros((1, LANES), F32) for _ in range(probes)]
    for f in range(cycles):
        high, low = [], []
        for p in range(probes):
            base = f * width + p * 2
            cos_coeff, sin_coeff = coeffs[:, base : base + 1], coeffs[:, base + 1 : base + 2]
            real = cos_coeff * inner_cos + sin_coeff * inner_sin
            imag = cos_coeff * inner_sin - sin_coeff * inner_cos
            hi, lo = halves(jnp.concatenate([real, imag], axis=0))
            high.append(hi)
            low.append(lo)
        high = jnp.concatenate(high, axis=1)
        low = jnp.concatenate(low, axis=1)
        mapped = dot(outer_s_ref[...], high)
        mapped = mapped[:outer] + mapped[outer:] + dot(outer_s_ref[:outer, :], low)
        mapped_ref[...] = mapped
        picked = mapped_ref[:, pl.ds(pl.multiple_of(own * LANES, LANES), LANES)]
        weighted_ref[pl.ds(f, outer, stride=cycles), :] = (
            picked * signs_folded[pl.ds(f, outer, stride=cycles), :]
        )
        noise = noise_folded[pl.ds(f, outer, stride=cycles), :]
        pixels = jnp.concatenate([noise] * probes, axis=1) * mapped
        power = jnp.sum(pixels * mapped, axis=0, keepdims=True)
        for p in range(probes):
            totals[p] = totals[p] + power[:, p * LANES : (p + 1) * LANES]
        hi, lo = halves(pixels)
        table_hi = outer_a_ref[:, :outer]
        parts = dot(table_hi, hi) + dot(table_hi, lo) + dot(
            outer_a_ref[:, LANES : LANES + outer], hi
        )
        for p in range(probes):
            acc = twiddle_sums(
                parts[:, p * LANES : (p + 1) * LANES], inner_cos, inner_sin, acc, lane,
                f * width + p * 2,
            )
    sums_ref[...] = acc
    out = gather_rows(sums_ref, all_places, [k * rows for k in range(slots)])
    line = scalars_ref[:1]
    lane = iota((1, LANES), 1)
    for p in range(probes):
        value = jnp.sum(totals[p], axis=1, keepdims=True)
        line = line + jnp.where(lane == SCALARS + 2 * probes + p, value, 0.0)
    send_ref[...] = out + line


def fourth_kernel(
    received_ref, rows_ref, signal_ref, limits_ref, hi_ref, lo_ref, terms_ref, weighted_ref,
    send_ref, stack_ref,
):
    probes = send_ref.shape[0]
    slots, quarter, _ = hi_ref.shape
    rows = probes * 2
    blocks = quarter // LANES
    block_rows = blocks * slots * 2
    received = received_ref[...]
    columns, _ = latitude_columns(lambda c: received, 1, rows_ref, slots * rows, stack_ref)
    first_degree = lax.axis_index("probe") * quarter
    signal = signal_ref[...]
    line = jnp.broadcast_to(jnp.sum(received, axis=0, keepdims=True), (8, LANES))
    for p in range(probes):
        send_ref[p, 2 * block_rows : 2 * block_rows + 8, :] = line
        send_ref[p, 2 * block_rows + 8 :, :] = weighted_ref[...]
    for k in range(slots):
        noise_terms = degree_sums(
            hi_ref[k], lo_ref[k], columns, k, rows, slots * rows, limits_ref[k : k + 1, :1],
            first_degree,
        )
        terms = terms_ref[k]
        image = signal * terms + noise_terms
        for p in range(probes):
            for b in range(blocks):
                place = (b * slots + k) * 2
                own = (slice(p * 2, p * 2 + 2), slice(b * LANES, (b + 1) * LANES))
                send_ref[p, place : place + 2, :] = terms[own]
                send_ref[p, block_rows + place : block_rows + place + 2, :] = image[own]


def last_kernel(received_ref, residual_ref, variance_ref):
    probes = received_ref.shape[0]
    slots = residual_ref.shape[1]
    quarter = residual_ref.shape[3] // probes
    blocks = quarter // LANES
    block_rows = blocks * slots * 2
    cycles, length = variance_ref.shape
    own = lax.axis_index("probe")
    lane = iota((8, LANES), 1)
    lines = [received_ref[p, 2 * block_rows : 2 * block_rows + 8, :] for p in range(probes)]
    degree_line = lines[0]
    for p in range(1, probes):
        degree_line = degree_line + lines[p]

    def ratio(p):
        def value(line, base):
            return jnp.sum(jnp.where(lane == base + p, line, 0.0), axis=1, keepdims=True)

        norm = value(degree_line, SCALARS)
        prior = value(degree_line, SCALARS + probes)
        return norm / (prior + value(lines[0], SCALARS + 2 * probes))

    start = 2 * block_rows + 8
    total = received_ref[0, start:, :] * ratio(0)[:1]
    for p in range(1, probes):
        total = total + received_ref[p, start:, :] * ratio(p)[:1]
    total = total * (1.0 / probes)
    for j in range(length // LANES):
        variance_ref[:, j * LANES : (j + 1) * LANES] = total[j * cycles : (j + 1) * cycles]
    own_ratio = ratio(own)[:1]
    for x in range(probes):
        residual = (
            received_ref[x, :block_rows, :]
            - own_ratio * received_ref[x, block_rows : 2 * block_rows, :]
        )
        for b in range(blocks):
            for k in range(slots):
                place = x * quarter + b * LANES
                row = (b * slots + k) * 2
                residual_ref[0, k, :, place : place + LANES] = residual[row : row + 2]


def call(kernel, outs, scratch, args, name, far=()):
    spaces = [pltpu.HBM if i in far else pltpu.VMEM for i in range(len(args))]
    args = [
        pltpu.with_memory_space_constraint(arg, space) if space == pltpu.HBM else arg
        for arg, space in zip(args, spaces)
    ]
    return pl.pallas_call(
        kernel,
        out_shape=[jax.ShapeDtypeStruct(shape, dtype) for shape, dtype in outs],
        in_specs=[pl.BlockSpec(memory_space=space) for space in spaces],
        out_specs=[pl.BlockSpec(memory_space=pltpu.VMEM)] * len(outs),
        scratch_shapes=scratch,
        compiler_params=pltpu.CompilerParams(vmem_limit_bytes=VMEM_BYTES),
        name=name,
    )(*args)


def per_device(legendre, signs, inv_noise, inv_signal, harmonic_order_values, cycle_rows):
    slots, quarter, total = legendre.shape
    _, cycles, length = signs.shape
    probes = lax.axis_size("probe")
    places = lax.axis_size("place")
    cores = lax.axis_size("core")
    count = harmonic_order_values.shape[0]
    outer = length // LANES
    rows = probes * 2
    wide = ((total, LANES), F32)
    by_order = ((count, LANES), F32)
    folded = ((outer * cycles, LANES), F32)

    def everywhere(send):
        received = lax.all_to_all(
            send.reshape(probes * places, LANES), ("probe", "place"), 0, 0, tiled=True
        )
        return lax.all_gather(received, "core", axis=0)

    (
        send, inner_cos, inner_sin, outer_a, outer_s, limits, signs_near, row_line, signal,
        noise_near, legendre_near,
    ) = call(
        functools.partial(first_kernel, slots),
        [
            ((probes, places, LANES), F32),
            by_order,
            by_order,
            ((2 * count, 2 * LANES), BF16),
            ((2 * outer, 2 * count), BF16),
            ((8, LANES), jnp.int32),
            (signs.shape, jnp.int32),
            ((1, total), jnp.int32),
            ((1, quarter), F32),
            (inv_noise.shape, F32),
            (legendre.shape, F32),
        ],
        [
            pltpu.VMEM((1, count), jnp.int32),
            pltpu.VMEM(*folded),
            pltpu.VMEM(*by_order),
            pltpu.SemaphoreType.DMA((6,)),
        ],
        (
            harmonic_order_values.reshape(1, count), signs, cycle_rows.reshape(1, total),
            inv_signal.reshape(1, probes * quarter), inv_noise, legendre,
        ),
        "cycle_sums",
        range(6),
    )
    received = everywhere(send)
    send, terms, scalars, leg_hi, leg_lo = call(
        second_kernel,
        [
            ((probes, places, LANES), F32),
            ((slots, rows, quarter), F32),
            ((8, LANES), F32),
            (legendre.shape, BF16),
            (legendre.shape, BF16),
        ],
        [
            pltpu.VMEM(*wide),
            pltpu.VMEM(*wide),
        ],
        (received, row_line, signal, limits, legendre_near),
        "degrees_there_and_back",
    )
    received = everywhere(send)
    send, weighted = call(
        functools.partial(third_kernel, slots),
        [((places * cores, LANES), F32), folded],
        [
            pltpu.VMEM(*folded),
            pltpu.VMEM(*folded),
            pltpu.VMEM(*by_order),
            pltpu.VMEM((outer, probes * LANES), F32),
        ],
        (
            received, signs_near, noise_near, inner_cos, inner_sin, outer_a, outer_s, scalars,
        ),
        "cycles_there_and_back",
    )
    received = lax.all_to_all(send, ("place", "core"), 0, 0, tiled=True)
    height = quarter // LANES * slots * 4 + 8 + outer * cycles
    (send,) = call(
        fourth_kernel,
        [((probes, height, LANES), F32)],
        [pltpu.VMEM(*wide)],
        (received, row_line, signal, limits, leg_hi, leg_lo, terms, weighted),
        "image_terms",
    )
    received = lax.all_to_all(send, "probe", 0, 0, tiled=True)
    return call(
        last_kernel,
        [((1, slots, 2, probes * quarter), F32), ((cycles, length), F32)],
        [],
        (received,),
        "outputs",
    )


def solution(mesh):
    cores = 2
    split = jax.sharding.Mesh(
        mesh.devices.reshape(mesh.shape["probe"], -1, cores), ("probe", "place", "core")
    )
    sky = ("place", "core")
    in_specs = (P(sky, "probe", None), P("probe", sky, None), P(sky, None), P(), P(), P())
    out_specs = (P("probe", sky, None, None), P(sky, None))

    def run(*args):
        return tuple(
            jax.shard_map(
                per_device, mesh=split, in_specs=in_specs, out_specs=out_specs, check_vma=False
            )(*args)
        )

    return run
```

```python
import functools
import math

import jax
import jax.numpy as jnp
from jax import lax
from jax.experimental import pallas as pl
from jax.experimental.pallas import tpu as pltpu
from jax.sharding import PartitionSpec as P

F32 = jnp.float32
BF16 = jnp.bfloat16
LANES = 128
VMEM_BYTES = 24 * 1024 * 1024


def iota(shape, dim):
    return lax.broadcasted_iota(jnp.int32, shape, dim)


def dot(a, b):
    return jnp.dot(a, b, preferred_element_type=F32)


def dot_rows(a, b):
    return lax.dot_general(a, b, (((1,), (1,)), ((), ())), preferred_element_type=F32)


def halves(value):
    high = value.astype(BF16)
    return high, (value - high.astype(F32)).astype(BF16)


def fold(flat_ref, f, copies):
    rows = [
        flat_ref[f : f + 1, j * LANES : (j + 1) * LANES] for j in range(flat_ref.shape[1] // LANES)
    ]
    return jnp.concatenate(rows * copies, axis=0)


def cosine(phase, turn):
    shift = turn.bit_length() - 3
    quadrant = (phase + turn // 8) >> shift
    angle = (phase - (quadrant << shift)).astype(F32) * (2.0 * math.pi / turn)
    square = angle * angle
    cos = 1.0 + square * (
        -1.0 / 2 + square * (1.0 / 24 + square * (-1.0 / 720 + square * (1.0 / 40320)))
    )
    sin = angle * (
        1.0 + square * (-1.0 / 6 + square * (1.0 / 120 + square * (-1.0 / 5040 + square / 362880)))
    )
    value = jnp.where((quadrant & 1) == 1, sin, cos)
    return jnp.where(((quadrant + 1) & 2) == 2, -value, value)


def cosine_and_sine(rows, step, turn):
    half = LANES // 2
    lane = iota((rows, LANES), 1)
    phase = iota((rows, LANES), 0) * (lane & (half - 1)) * step
    return cosine(phase - jnp.where(lane >= half, turn // 4, 0), turn)


def ones_where(condition):
    return jnp.where(condition, 1.0, 0.0).astype(BF16)


def both_picks(line):
    half = LANES // 2
    count = line.shape[1]
    shape = (LANES, 2 * count)
    row, col = iota(shape, 0), iota(shape, 1)
    wide = jnp.concatenate([line, line], axis=1)
    return ones_where(row == wide + jnp.where(col >= count, half, 0))


def turned_rows(pieces):
    rows = jnp.concatenate(pieces, axis=0)
    if rows.shape[0] < LANES:
        rows = jnp.concatenate(
            [rows, jnp.zeros((LANES - rows.shape[0], rows.shape[1]), F32)], axis=0
        )
    return rows.T


def own_rows(received_ref, source, groups):
    places = received_ref.shape[1] // groups
    total = received_ref[source, :places]
    for g in range(1, groups):
        total = total + received_ref[source, g * places : (g + 1) * places]
    total = total.T
    half = LANES // 2
    return jnp.where(lax.axis_index("core") == 0, total[:half], total[half:])


def first_kernel(
    slots, orders_hbm, signs_hbm, rows_hbm, signal_hbm, noise_hbm,
    send_ref, inner_cos_ref, inner_sin_ref, outer_ref, limits_ref, signs_ref,
    rows_ref, signal_ref, noise_ref,
    orders_ref, near_rows_ref, sems,
):
    count = orders_ref.shape[1]
    probes, places = send_ref.shape[:2]
    _, cycles, cycle_length = signs_ref.shape
    outer = cycle_length // LANES
    cores = count // slots // places
    total = rows_ref.shape[1]
    own = lax.axis_index("probe")
    quarter = signal_ref.shape[1]
    own_signal = signal_hbm.at[:, pl.ds(pl.multiple_of(own * quarter, LANES), quarter)]

    copies = [
        pltpu.make_async_copy(source, target, sems.at[n])
        for n, (source, target) in enumerate(
            [
                (orders_hbm, orders_ref),
                (signs_hbm, signs_ref),
                (rows_hbm, near_rows_ref),
                (own_signal, signal_ref),
                (noise_hbm, noise_ref),
            ]
        )
    ]
    for copy in copies:
        copy.start()

    high_table = halves(cosine_and_sine(LANES, 64, cycle_length))
    low_table = halves(cosine_and_sine(LANES, 1, cycle_length))
    outer_table = halves(cosine_and_sine(outer, cycle_length // outer, cycle_length))
    slot, place = iota((count, count), 0), iota((count, count), 1)
    slot_picks = ones_where(
        slot == (place % places * cores + place // places % cores) * slots
        + place // (places * cores)
    )

    copies[0].wait()
    orders = orders_ref[...]
    row = iota((8, count), 0)
    parts = jnp.where(row == 0, orders >> 6, jnp.where(row == 1, orders & 63, 0))
    parts = dot(parts.astype(F32).astype(BF16), slot_picks).astype(jnp.int32)
    high, low = parts[:1], parts[1:2]
    for k in range(slots):
        own_place = (k * cores + lax.axis_index("core")) * places + lax.axis_index("place")
        picked = jnp.where(iota((1, count), 1) == own_place, high * 64 + low, 0).astype(F32)
        picked = jnp.sum(picked, axis=1, keepdims=True).astype(jnp.int32)
        limits_ref[k : k + 1, :] = jnp.broadcast_to(picked, (1, LANES))
    high_picks, low_picks = both_picks(high), both_picks(low)
    high_part = dot(high_table[0], high_picks) + dot(high_table[1], high_picks)
    low_part = dot(low_table[0], low_picks) + dot(low_table[1], low_picks)
    scale_factor = 1.0 / math.sqrt(cycle_length)
    high_cos, high_sin = high_part[:, :count] * scale_factor, high_part[:, count:] * scale_factor
    low_cos, low_sin = low_part[:, :count], low_part[:, count:]
    inner_cos = high_cos * low_cos - high_sin * low_sin
    inner_sin = high_sin * low_cos + high_cos * low_sin
    inner_cos_ref[...] = inner_cos
    inner_sin_ref[...] = inner_sin
    for h in range(2):
        table = dot(outer_table[h], low_picks).astype(BF16)
        outer_ref[2 * h * outer : (2 * h + 1) * outer, :] = table
        outer_ref[(2 * h + 1) * outer : (2 * h + 2) * outer, :] = table

    copies[1].wait()
    rows = probes * 2
    row = iota((rows, count), 0)
    pixels = jnp.concatenate(
        [fold(signs_ref.at[0], f, 2).astype(F32).T for f in range(cycles)], axis=0
    ).astype(BF16)
    sums = dot(pixels, outer_ref[outer : 3 * outer, :])
    pieces = [[None] * cycles for _ in range(slots)]
    per_slot = count // slots
    for f in range(cycles):
        cos_sum, sin_sum = twiddle_sums(sums[f * LANES : (f + 1) * LANES], inner_cos, inner_sin)
        field = jnp.where(
            row == own * 2, cos_sum, jnp.where(row == own * 2 + 1, sin_sum, 0.0)
        )
        for k in range(slots):
            pieces[k][f] = field[:, k * per_slot : (k + 1) * per_slot]
    out = turned_rows(
        [
            pieces[k][f][:, c * places : (c + 1) * places]
            for c in range(cores)
            for k in range(slots)
            for f in range(cycles)
        ]
    )
    for p in range(probes):
        send_ref[p] = out

    for copy in copies[2:]:
        copy.wait()
    cycle_rows = near_rows_ref[...]
    row = iota((8, total), 0)
    parts = jnp.where(row == 0, cycle_rows >> 6, jnp.where(row == 1, cycle_rows & 63, 0))
    cycle, place = iota((total, total), 0), iota((total, total), 1)
    picks = ones_where(
        cycle == (place % places * cores + place // (places * cycles)) * cycles
        + place // places % cycles
    )
    parts = dot(parts.astype(F32).astype(BF16), picks).astype(jnp.int32)
    rows_ref[...] = parts[:1] * 64 + parts[1:2]


def twiddle_sums(sums, inner_cos, inner_sin):
    count = inner_cos.shape[1]
    real, imag = sums[:, :count], sums[:, count:]
    return (
        jnp.sum(inner_cos * real - inner_sin * imag, axis=0, keepdims=True),
        jnp.sum(inner_sin * real + inner_cos * imag, axis=0, keepdims=True),
    )


def latitude_values(by_core, chosen, slots, cycles, rows):
    values = [
        jnp.concatenate(
            [
                values[(k * cycles + f) * rows : (k * cycles + f + 1) * rows]
                for values in by_core
                for f in range(cycles)
            ],
            axis=1,
        )
        for k in range(slots)
    ]
    both = jnp.concatenate(halves(jnp.concatenate(values, axis=0)), axis=0)
    return dot_rows(both, chosen).astype(BF16)


def degree_sums(leg_hi, leg_lo, values, k, rows, order, first_degree):
    width = values.shape[0] // 2
    across = dot_rows(values, leg_hi) + dot_rows(values, leg_lo)
    terms = across[k * rows : (k + 1) * rows] + across[
        width + k * rows : width + (k + 1) * rows
    ]
    degrees = first_degree + iota(terms.shape, 1)
    return jnp.where(degrees >= order, terms, 0.0)


def second_kernel(
    received_ref, rows_ref, signal_ref, limits_ref, legendre_ref,
    send_ref, terms_ref, scalars_ref, hi_ref, lo_ref, chosen_ref,
):
    cores = received_ref.shape[0]
    probes, places = send_ref.shape[:2]
    slots, quarter, total = legendre_ref.shape
    cycles = total // (places * cores)
    rows = probes * 2
    width = slots * rows
    chosen = ones_where(iota((total, total), 0) == rows_ref[...])
    chosen_ref[...] = chosen
    values = latitude_values(
        [own_rows(received_ref, c, probes) for c in range(cores)], chosen, slots, cycles, rows
    )
    first_degree = lax.axis_index("probe") * quarter
    signal = signal_ref[...]
    norm = jnp.zeros((rows, 1), F32)
    prior = jnp.zeros((rows, 1), F32)
    halved = []
    for k in range(slots):
        leg_hi, leg_lo = halves(legendre_ref[k])
        hi_ref[k] = leg_hi
        lo_ref[k] = leg_lo
        halved.append((leg_hi, leg_lo))
    both = []
    for k in range(slots):
        terms = degree_sums(
            *halved[k], values, k, rows, limits_ref[k : k + 1, :1], first_degree
        )
        terms_ref[k] = terms
        squares = terms * terms
        norm = norm + jnp.sum(squares, axis=1, keepdims=True)
        prior = prior + jnp.sum(squares * signal, axis=1, keepdims=True)
        both.append(jnp.concatenate(halves(terms), axis=0))
    fields = []
    for k in range(slots):
        field = dot(both[k], halved[k][0]) + dot(both[k], halved[k][1])
        fields.append(field[:rows] + field[rows:])
    both = jnp.concatenate(halves(jnp.concatenate(fields, axis=0)), axis=0)
    by_cycle = dot(both, chosen)
    by_cycle = by_cycle[:width] + by_cycle[width:]
    out = turned_rows(
        [
            by_cycle[k * rows : (k + 1) * rows, place * places : (place + 1) * places]
            for c in range(cores)
            for k in range(slots)
            for place in range(c * cycles, (c + 1) * cycles)
        ]
    )
    for p in range(probes):
        send_ref[p] = out
    scalars_ref[:rows, :] = jnp.broadcast_to(norm, (rows, LANES))
    scalars_ref[rows:, :] = jnp.broadcast_to(prior, (rows, LANES))


def third_kernel(
    slots, received_ref, signs_ref, inv_noise_ref, inner_cos_ref, inner_sin_ref, outer_ref,
    scalars_ref, send_ref, weighted_ref, mapped_ref,
):
    cores = received_ref.shape[0]
    places = send_ref.shape[0] // cores
    probes = received_ref.shape[1] // places
    cycles = inv_noise_ref.shape[0]
    outer = outer_ref.shape[0] // 4
    rows = probes * 2
    own = lax.axis_index("probe")

    by_core = [own_rows(received_ref, c, probes) for c in range(cores)]
    inner_cos, inner_sin = inner_cos_ref[...], inner_sin_ref[...]
    count = inner_cos.shape[1]
    per_slot = count // slots
    row = iota((rows, count), 0)
    power = jnp.zeros((rows, LANES), F32)
    power_row = iota((rows, LANES), 0)
    pieces = [[None] * cycles for _ in range(slots)]
    table = outer_ref[outer : 3 * outer, :]

    def map_cycle(f):
        coeffs = jnp.concatenate(
            [
                by_core[c][(k * cycles + f) * rows : (k * cycles + f + 1) * rows]
                for k in range(slots)
                for c in range(cores)
            ],
            axis=1,
        )
        fields = []
        for p in range(probes):
            cos_coeff, sin_coeff = coeffs[2 * p : 2 * p + 1], coeffs[2 * p + 1 : 2 * p + 2]
            real = cos_coeff * inner_cos + sin_coeff * inner_sin
            imag = sin_coeff * inner_cos - cos_coeff * inner_sin
            hi, lo = halves(jnp.concatenate([real, imag], axis=1))
            fields.append(dot_rows(hi, table) + dot_rows(lo, table))
        mapped = jnp.concatenate(fields, axis=0)
        return mapped + pltpu.roll(mapped, outer, 1)

    def weigh_cycle(f, mapped):
        mapped_ref[f] = mapped
        noise = fold(inv_noise_ref, f, 2).T
        pixels = jnp.concatenate([noise] * probes, axis=0) * mapped
        squares = pixels * mapped
        lines = [
            jnp.sum(squares[p * LANES : (p + 1) * LANES], axis=0, keepdims=True)
            for p in range(probes)
        ]
        hi = pixels.astype(BF16).astype(F32)
        hi_lo = jnp.where(iota(pixels.shape, 1) < outer, hi, pixels - hi).astype(BF16)
        return lines, outer_sums(hi_lo)

    def outer_sums(hi_lo):
        sums = dot(jnp.concatenate([hi_lo, hi_lo], axis=1), outer_ref[...])
        return [sums[p * LANES : (p + 1) * LANES] for p in range(probes)]

    def finish_cycle(f, lines, sums):
        nonlocal power
        field = jnp.zeros((rows, count), F32)
        for p in range(probes):
            power = power + jnp.where(power_row == 2 * p, lines[p], 0.0)
            cos_sum, sin_sum = twiddle_sums(sums[p], inner_cos, inner_sin)
            field = jnp.where(row == 2 * p, cos_sum, field)
            field = jnp.where(row == 2 * p + 1, sin_sum, field)
        for k in range(slots):
            pieces[k][f] = field[:, k * per_slot : (k + 1) * per_slot]

    mapped, done = map_cycle(0), None
    for f in range(cycles):
        later = map_cycle(f + 1) if f + 1 < cycles else None
        lines, sums = weigh_cycle(f, mapped)
        if done:
            finish_cycle(*done)
        mapped, done = later, (f, lines, sums)
    finish_cycle(*done)
    for f in range(cycles):
        picked = mapped_ref[f, pl.ds(pl.multiple_of(own * LANES, LANES), LANES), :].T
        weighted_ref[pl.ds(f, outer, stride=cycles), :] = picked[:outer] * fold(
            signs_ref.at[0], f, 1
        ).astype(F32)
    power = jnp.broadcast_to(0.5 * jnp.sum(power, axis=1, keepdims=True), (rows, per_slot))
    out = turned_rows(
        [pieces[k][f] for k in range(slots) for f in range(cycles)]
        + [scalars_ref[:, :per_slot], power]
    )
    for c in range(cores):
        send_ref[pl.ds(c, places, stride=cores), :] = out[c * places : (c + 1) * places]


def fourth_kernel(
    cores, received_ref, signal_ref, limits_ref, hi_ref, lo_ref, chosen_ref, terms_ref,
    weighted_ref, send_ref,
):
    probes = send_ref.shape[0]
    slots, quarter, total = hi_ref.shape
    cycles = total // received_ref.shape[0]
    places = received_ref.shape[0] // cores
    rows = probes * 2
    blocks = quarter // LANES
    block_rows = blocks * slots * 2
    by_core = [received_ref[pl.ds(c, places, stride=cores), :].T for c in range(cores)]
    start = slots * cycles * rows
    scalars = jnp.sum(by_core[0][start : start + 3 * rows], axis=1, keepdims=True)
    for values in by_core[1:]:
        scalars = scalars + jnp.sum(values[start : start + 3 * rows], axis=1, keepdims=True)
    scalars = jnp.broadcast_to(scalars, (3 * rows, LANES))
    for p in range(probes):
        send_ref[p, 2 * block_rows : 2 * block_rows + 3 * rows, :] = scalars
        send_ref[p, 2 * block_rows + 3 * rows :, :] = weighted_ref[...]
    values = latitude_values(by_core, chosen_ref[...], slots, cycles, rows)
    first_degree = lax.axis_index("probe") * quarter
    signal = signal_ref[...]
    for k in range(slots):
        noise_terms = degree_sums(
            hi_ref[k], lo_ref[k], values, k, rows, limits_ref[k : k + 1, :1], first_degree
        )
        terms = terms_ref[k]
        image = signal * terms + noise_terms
        for p in range(probes):
            for b in range(blocks):
                place = (b * slots + k) * 2
                own = (slice(p * 2, p * 2 + 2), slice(b * LANES, (b + 1) * LANES))
                send_ref[p, place : place + 2, :] = terms[own]
                send_ref[p, block_rows + place : block_rows + place + 2, :] = image[own]


def last_kernel(received_ref, residual_ref, variance_ref):
    probes = received_ref.shape[0]
    slots = residual_ref.shape[1]
    quarter = residual_ref.shape[3] // probes
    blocks = quarter // LANES
    block_rows = blocks * slots * 2
    rows = probes * 2
    cycles, length = variance_ref.shape
    own = lax.axis_index("probe")
    start = 2 * block_rows
    degree_sums = received_ref[0, start : start + 2 * rows, :]
    for p in range(1, probes):
        degree_sums = degree_sums + received_ref[p, start : start + 2 * rows, :]
    norm, prior = degree_sums[:rows], degree_sums[rows:]
    curve = prior + received_ref[0, start + 2 * rows : start + 3 * rows, :]
    ratios = [
        (norm[2 * p : 2 * p + 1] + norm[2 * p + 1 : 2 * p + 2])
        / (curve[2 * p : 2 * p + 1] + curve[2 * p + 1 : 2 * p + 2])
        for p in range(probes)
    ]
    start = start + 3 * rows
    total = received_ref[0, start:, :] * ratios[0]
    for p in range(1, probes):
        total = total + received_ref[p, start:, :] * ratios[p]
    total = total * (1.0 / probes)
    for j in range(length // LANES):
        variance_ref[:, j * LANES : (j + 1) * LANES] = total[j * cycles : (j + 1) * cycles]
    own_ratio = ratios[0]
    for p in range(1, probes):
        own_ratio = jnp.where(own == p, ratios[p], own_ratio)
    for x in range(probes):
        residual = (
            received_ref[x, :block_rows, :]
            - own_ratio * received_ref[x, block_rows : 2 * block_rows, :]
        )
        for b in range(blocks):
            for k in range(slots):
                place = x * quarter + b * LANES
                row = (b * slots + k) * 2
                residual_ref[0, k, :, place : place + LANES] = residual[row : row + 2]


def call(kernel, outs, scratch, args, name, far=()):
    spaces = [pltpu.HBM if i in far else pltpu.VMEM for i in range(len(args))]
    args = [
        pltpu.with_memory_space_constraint(arg, space) if space == pltpu.HBM else arg
        for arg, space in zip(args, spaces)
    ]
    return pl.pallas_call(
        kernel,
        out_shape=[jax.ShapeDtypeStruct(shape, dtype) for shape, dtype in outs],
        in_specs=[pl.BlockSpec(memory_space=space) for space in spaces],
        out_specs=[pl.BlockSpec(memory_space=pltpu.VMEM)] * len(outs),
        scratch_shapes=scratch,
        compiler_params=pltpu.CompilerParams(vmem_limit_bytes=VMEM_BYTES),
        name=name,
        cost_estimate=pl.CostEstimate(flops=2000000000, bytes_accessed=20000000, transcendentals=0),
    )(*args)


def per_device(legendre, signs, inv_noise, inv_signal, harmonic_order_values, cycle_rows):
    slots, quarter, total = legendre.shape
    _, cycles, length = signs.shape
    probes = lax.axis_size("probe")
    places = lax.axis_size("place")
    cores = lax.axis_size("core")
    count = harmonic_order_values.shape[0]
    outer = length // LANES
    rows = probes * 2
    by_order = ((LANES, count), F32)
    folded = ((outer * cycles, LANES), F32)

    def everywhere(send):
        received = lax.all_to_all(
            send.reshape(probes * places, LANES), ("probe", "place"), 0, 0, tiled=True
        )
        return lax.all_gather(received, "core", axis=0)

    (
        send, inner_cos, inner_sin, outer_table, limits, signs_near, row_line, signal,
        noise_near,
    ) = call(
        functools.partial(first_kernel, slots),
        [
            ((probes, places, LANES), F32),
            by_order,
            by_order,
            ((4 * outer, 2 * count), BF16),
            ((8, LANES), jnp.int32),
            (signs.shape, jnp.int32),
            ((1, total), jnp.int32),
            ((1, quarter), F32),
            (inv_noise.shape, F32),
        ],
        [
            pltpu.VMEM((1, count), jnp.int32),
            pltpu.VMEM((1, total), jnp.int32),
            pltpu.SemaphoreType.DMA((5,)),
        ],
        (
            harmonic_order_values.reshape(1, count), signs, cycle_rows.reshape(1, total),
            inv_signal.reshape(1, probes * quarter), inv_noise,
        ),
        "cycle_sums",
        range(5),
    )
    received = everywhere(send)
    send, terms, scalars, leg_hi, leg_lo, chosen = call(
        second_kernel,
        [
            ((probes, places, LANES), F32),
            ((slots, rows, quarter), F32),
            ((2 * rows, LANES), F32),
            (legendre.shape, BF16),
            (legendre.shape, BF16),
            ((total, total), BF16),
        ],
        [],
        (received, row_line, signal, limits, legendre),
        "degrees_there_and_back",
    )
    received = everywhere(send)
    send, weighted = call(
        functools.partial(third_kernel, slots),
        [((places * cores, LANES), F32), folded],
        [pltpu.VMEM((cycles, probes * LANES, LANES), F32)],
        (received, signs_near, noise_near, inner_cos, inner_sin, outer_table, scalars),
        "cycles_there_and_back",
    )
    received = lax.all_to_all(send, ("place", "core"), 0, 0, tiled=True)
    height = quarter // LANES * slots * 4 + 3 * rows + outer * cycles
    (send,) = call(
        functools.partial(fourth_kernel, cores),
        [((probes, height, LANES), F32)],
        [],
        (received, signal, limits, leg_hi, leg_lo, chosen, terms, weighted),
        "image_terms",
    )
    received = lax.all_to_all(send, "probe", 0, 0, tiled=True)
    return call(
        last_kernel,
        [((1, slots, 2, probes * quarter), F32), ((cycles, length), F32)],
        [],
        (received,),
        "outputs",
    )


def solution(mesh):
    cores = 2
    split = jax.sharding.Mesh(
        mesh.devices.reshape(mesh.shape["probe"], -1, cores), ("probe", "place", "core")
    )
    sky = ("place", "core")
    in_specs = (P(sky, "probe", None), P("probe", sky, None), P(sky, None), P(), P(), P())
    out_specs = (P("probe", sky, None, None), P(sky, None))

    def run(*args):
        return tuple(
            jax.shard_map(
                per_device, mesh=split, in_specs=in_specs, out_specs=out_specs, check_vma=False
            )(*args)
        )

    return run
```

```python
import functools
import math

import jax
import jax.numpy as jnp
from jax import lax
from jax.experimental import pallas as pl
from jax.experimental.pallas import tpu as pltpu
from jax.sharding import PartitionSpec as P

F32 = jnp.float32
BF16 = jnp.bfloat16
LANES = 128
VMEM_BYTES = 24 * 1024 * 1024


def iota(shape, dim):
    return lax.broadcasted_iota(jnp.int32, shape, dim)


def dot(a, b):
    return jnp.dot(a, b, preferred_element_type=F32)


def dot_rows(a, b):
    return lax.dot_general(a, b, (((1,), (1,)), ((), ())), preferred_element_type=F32)


def halves(value):
    high = value.astype(BF16)
    return high, (value - high.astype(F32)).astype(BF16)


def fold(flat_ref, f):
    return jnp.concatenate(
        [
            flat_ref[f : f + 1, j * LANES : (j + 1) * LANES]
            for j in range(flat_ref.shape[1] // LANES)
        ],
        axis=0,
    )


def cosine(phase, turn):
    shift = turn.bit_length() - 3
    quadrant = (phase + turn // 8) >> shift
    angle = (phase - (quadrant << shift)).astype(F32) * (2.0 * math.pi / turn)
    square = angle * angle
    cos = 1.0 + square * (
        -1.0 / 2 + square * (1.0 / 24 + square * (-1.0 / 720 + square * (1.0 / 40320)))
    )
    sin = angle * (
        1.0 + square * (-1.0 / 6 + square * (1.0 / 120 + square * (-1.0 / 5040 + square / 362880)))
    )
    value = jnp.where((quadrant & 1) == 1, sin, cos)
    return jnp.where(((quadrant + 1) & 2) == 2, -value, value)


def cosine_and_sine(rows, step, turn):
    half = LANES // 2
    lane = iota((rows, LANES), 1)
    phase = iota((rows, LANES), 0) * (lane & (half - 1)) * step
    return cosine(phase - jnp.where(lane >= half, turn // 4, 0), turn)


def ones_where(condition):
    return jnp.where(condition, 1.0, 0.0).astype(BF16)


def both_picks(line):
    half = LANES // 2
    count = line.shape[1]
    shape = (LANES, 2 * count)
    row, col = iota(shape, 0), iota(shape, 1)
    wide = jnp.concatenate([line, line], axis=1)
    return ones_where(row == wide + jnp.where(col >= count, half, 0))


def turned_rows(pieces):
    rows = jnp.concatenate(pieces, axis=0)
    if rows.shape[0] < LANES:
        rows = jnp.concatenate(
            [rows, jnp.zeros((LANES - rows.shape[0], rows.shape[1]), F32)], axis=0
        )
    return rows.T


def own_rows(received_ref, source, groups):
    places = received_ref.shape[1] // groups
    total = received_ref[source, :places]
    for g in range(1, groups):
        total = total + received_ref[source, g * places : (g + 1) * places]
    total = total.T
    half = LANES // 2
    return jnp.where(lax.axis_index("core") == 0, total[:half], total[half:])


def first_kernel(
    slots, orders_hbm, signs_hbm, rows_hbm, signal_hbm, noise_hbm,
    send_ref, inner_ref, outer_ref, limits_ref, signs_ref,
    rows_ref, signal_ref, noise_ref,
    orders_ref, near_rows_ref, sems,
):
    count = orders_ref.shape[1]
    probes, places = send_ref.shape[:2]
    _, cycles, cycle_length = signs_ref.shape
    outer = cycle_length // LANES
    cores = count // slots // places
    total = rows_ref.shape[1]
    own = lax.axis_index("probe")
    quarter = signal_ref.shape[1]
    own_signal = signal_hbm.at[:, pl.ds(pl.multiple_of(own * quarter, LANES), quarter)]

    copies = [
        pltpu.make_async_copy(source, target, sems.at[n])
        for n, (source, target) in enumerate(
            [
                (orders_hbm, orders_ref),
                (signs_hbm, signs_ref),
                (rows_hbm, near_rows_ref),
                (own_signal, signal_ref),
                (noise_hbm, noise_ref),
            ]
        )
    ]
    for copy in copies:
        copy.start()

    high_table = halves(cosine_and_sine(LANES, 64, cycle_length))
    low_table = halves(cosine_and_sine(LANES, 1, cycle_length))
    outer_table = halves(cosine_and_sine(outer, cycle_length // outer, cycle_length))
    slot, place = iota((count, count), 0), iota((count, count), 1)
    slot_picks = ones_where(
        slot == (place % places * cores + place // places % cores) * slots
        + place // (places * cores)
    )

    copies[0].wait()
    orders = orders_ref[...]
    row = iota((8, count), 0)
    parts = jnp.where(row == 0, orders >> 6, jnp.where(row == 1, orders & 63, 0))
    parts = dot(parts.astype(F32).astype(BF16), slot_picks).astype(jnp.int32)
    high, low = parts[:1], parts[1:2]
    for k in range(slots):
        own_place = (k * cores + lax.axis_index("core")) * places + lax.axis_index("place")
        picked = jnp.where(iota((1, count), 1) == own_place, high * 64 + low, 0).astype(F32)
        picked = jnp.sum(picked, axis=1, keepdims=True).astype(jnp.int32)
        limits_ref[k : k + 1, :] = jnp.broadcast_to(picked, (1, LANES))
    high_picks, low_picks = both_picks(high), both_picks(low)
    high_part = dot(high_table[0], high_picks) + dot(high_table[1], high_picks)
    low_part = dot(low_table[0], low_picks) + dot(low_table[1], low_picks)
    scale_factor = 1.0 / math.sqrt(cycle_length)
    high_cos, high_sin = high_part[:, :count] * scale_factor, high_part[:, count:] * scale_factor
    low_cos, low_sin = low_part[:, :count], low_part[:, count:]
    inner_cos = high_cos * low_cos - high_sin * low_sin
    inner_sin = high_sin * low_cos + high_cos * low_sin
    inner = halves(jnp.concatenate([inner_cos, inner_sin], axis=1))
    for n in range(4):
        inner_ref[n * LANES : (n + 1) * LANES, :] = inner[n // 2]
    outer_part = dot(outer_table[0], low_picks) + dot(outer_table[1], low_picks)
    outer_ref[...] = outer_part

    copies[1].wait()
    rows = probes * 2
    row = iota((rows, count), 0)
    pixels = jnp.concatenate(
        [fold(signs_ref.at[0], f).astype(F32) for f in range(cycles)], axis=0
    ).astype(BF16)
    sums = dot(jnp.concatenate([pixels, pixels], axis=1), inner_ref[LANES : 3 * LANES, :])
    pieces = [[None] * cycles for _ in range(slots)]
    per_slot = count // slots
    for f in range(cycles):
        cos_sum, sin_sum = twiddle_sums(sums[f * outer : (f + 1) * outer], outer_part)
        field = jnp.where(
            row == own * 2, cos_sum, jnp.where(row == own * 2 + 1, sin_sum, 0.0)
        )
        for k in range(slots):
            pieces[k][f] = field[:, k * per_slot : (k + 1) * per_slot]
    out = turned_rows(
        [
            pieces[k][f][:, c * places : (c + 1) * places]
            for c in range(cores)
            for k in range(slots)
            for f in range(cycles)
        ]
    )
    for p in range(probes):
        send_ref[p] = out

    for copy in copies[2:]:
        copy.wait()
    cycle_rows = near_rows_ref[...]
    row = iota((8, total), 0)
    parts = jnp.where(row == 0, cycle_rows >> 6, jnp.where(row == 1, cycle_rows & 63, 0))
    cycle, place = iota((total, total), 0), iota((total, total), 1)
    picks = ones_where(
        cycle == (place % places * cores + place // (places * cycles)) * cycles
        + place // places % cycles
    )
    parts = dot(parts.astype(F32).astype(BF16), picks).astype(jnp.int32)
    rows_ref[...] = parts[:1] * 64 + parts[1:2]


def twiddle_sums(sums, table):
    count = table.shape[1] // 2
    cos, sin = table[:, :count], table[:, count:]
    by_cos, by_sin = sums[:, :count], sums[:, count:]
    return (
        jnp.sum(cos * by_cos - sin * by_sin, axis=0, keepdims=True),
        jnp.sum(sin * by_cos + cos * by_sin, axis=0, keepdims=True),
    )


def latitude_values(by_core, chosen, slots, cycles, rows):
    values = [
        jnp.concatenate(
            [
                values[(k * cycles + f) * rows : (k * cycles + f + 1) * rows]
                for values in by_core
                for f in range(cycles)
            ],
            axis=1,
        )
        for k in range(slots)
    ]
    both = jnp.concatenate(halves(jnp.concatenate(values, axis=0)), axis=0)
    return dot_rows(both, chosen).astype(BF16)


def degree_sums(leg_hi, leg_lo, values, k, rows, order, first_degree):
    width = values.shape[0] // 2
    across = dot_rows(values, leg_hi) + dot_rows(values, leg_lo)
    terms = across[k * rows : (k + 1) * rows] + across[
        width + k * rows : width + (k + 1) * rows
    ]
    degrees = first_degree + iota(terms.shape, 1)
    return jnp.where(degrees >= order, terms, 0.0)


def second_kernel(
    received_ref, rows_ref, signal_ref, limits_ref, legendre_ref,
    send_ref, terms_ref, scalars_ref, hi_ref, lo_ref, chosen_ref,
):
    cores = received_ref.shape[0]
    probes, places = send_ref.shape[:2]
    slots, quarter, total = legendre_ref.shape
    cycles = total // (places * cores)
    rows = probes * 2
    width = slots * rows
    chosen = ones_where(iota((total, total), 0) == rows_ref[...])
    chosen_ref[...] = chosen
    values = latitude_values(
        [own_rows(received_ref, c, probes) for c in range(cores)], chosen, slots, cycles, rows
    )
    first_degree = lax.axis_index("probe") * quarter
    signal = signal_ref[...]
    norm = jnp.zeros((rows, 1), F32)
    prior = jnp.zeros((rows, 1), F32)
    halved = []
    for k in range(slots):
        leg_hi, leg_lo = halves(legendre_ref[k])
        hi_ref[k] = leg_hi
        lo_ref[k] = leg_lo
        halved.append((leg_hi, leg_lo))
    both = []
    for k in range(slots):
        terms = degree_sums(
            *halved[k], values, k, rows, limits_ref[k : k + 1, :1], first_degree
        )
        terms_ref[k] = terms
        squares = terms * terms
        norm = norm + jnp.sum(squares, axis=1, keepdims=True)
        prior = prior + jnp.sum(squares * signal, axis=1, keepdims=True)
        both.append(jnp.concatenate(halves(terms), axis=0))
    fields = []
    for k in range(slots):
        field = dot(both[k], halved[k][0]) + dot(both[k], halved[k][1])
        fields.append(field[:rows] + field[rows:])
    both = jnp.concatenate(halves(jnp.concatenate(fields, axis=0)), axis=0)
    by_cycle = dot(both, chosen)
    by_cycle = by_cycle[:width] + by_cycle[width:]
    out = turned_rows(
        [
            by_cycle[k * rows : (k + 1) * rows, place * places : (place + 1) * places]
            for c in range(cores)
            for k in range(slots)
            for place in range(c * cycles, (c + 1) * cycles)
        ]
    )
    for p in range(probes):
        send_ref[p] = out
    scalars_ref[:rows, :] = jnp.broadcast_to(norm, (rows, LANES))
    scalars_ref[rows:, :] = jnp.broadcast_to(prior, (rows, LANES))


def third_kernel(
    slots, received_ref, signs_ref, inv_noise_ref, inner_ref, outer_ref, scalars_ref,
    send_ref, weighted_ref, mapped_ref,
):
    cores = received_ref.shape[0]
    places = send_ref.shape[0] // cores
    probes = received_ref.shape[1] // places
    cycles = inv_noise_ref.shape[0]
    outer, count = outer_ref.shape[0], outer_ref.shape[1] // 2
    rows = probes * 2
    own = lax.axis_index("probe")

    by_core = [own_rows(received_ref, c, probes) for c in range(cores)]
    outer_cos, outer_sin = outer_ref[:, :count], outer_ref[:, count:]
    per_slot = count // slots
    row = iota((rows, count), 0)
    power = jnp.zeros((rows, LANES), F32)
    power_row = iota((rows, LANES), 0)
    pieces = [[None] * cycles for _ in range(slots)]
    table = inner_ref[LANES : 3 * LANES, :]

    def map_cycle(f):
        coeffs = jnp.concatenate(
            [
                by_core[c][(k * cycles + f) * rows : (k * cycles + f + 1) * rows]
                for k in range(slots)
                for c in range(cores)
            ],
            axis=1,
        )
        high, low = [], []
        for p in range(probes):
            cos_coeff, sin_coeff = coeffs[2 * p : 2 * p + 1], coeffs[2 * p + 1 : 2 * p + 2]
            by_cos = cos_coeff * outer_cos + sin_coeff * outer_sin
            by_sin = sin_coeff * outer_cos - cos_coeff * outer_sin
            hi, lo = halves(jnp.concatenate([by_cos, by_sin], axis=1))
            high.append(hi)
            low.append(lo)
        mapped = dot_rows(jnp.concatenate(high, axis=0), table) + dot_rows(
            jnp.concatenate(low, axis=0), table
        )
        return mapped[:, :LANES] + mapped[:, LANES:]

    def weigh_cycle(f, mapped):
        mapped_ref[f] = mapped
        pixels = jnp.concatenate([fold(inv_noise_ref, f)] * probes, axis=0) * mapped
        squares = pixels * mapped
        lines = [
            jnp.sum(squares[p * outer : (p + 1) * outer], axis=0, keepdims=True)
            for p in range(probes)
        ]
        hi, lo = halves(pixels)
        sums = dot(jnp.concatenate([hi, lo, hi, lo], axis=1), inner_ref[...])
        return lines, [sums[p * outer : (p + 1) * outer] for p in range(probes)]

    def finish_cycle(f, lines, sums):
        nonlocal power
        field = jnp.zeros((rows, count), F32)
        for p in range(probes):
            power = power + jnp.where(power_row == 2 * p, lines[p], 0.0)
            cos_sum, sin_sum = twiddle_sums(sums[p], outer_ref[...])
            field = jnp.where(row == 2 * p, cos_sum, field)
            field = jnp.where(row == 2 * p + 1, sin_sum, field)
        for k in range(slots):
            pieces[k][f] = field[:, k * per_slot : (k + 1) * per_slot]

    mapped, done = map_cycle(0), None
    for f in range(cycles):
        later = map_cycle(f + 1) if f + 1 < cycles else None
        lines, sums = weigh_cycle(f, mapped)
        if done:
            finish_cycle(*done)
        mapped, done = later, (f, lines, sums)
    finish_cycle(*done)
    for f in range(cycles):
        picked = mapped_ref[f, pl.ds(pl.multiple_of(own * outer, outer), outer), :]
        weighted_ref[pl.ds(f, outer, stride=cycles), :] = picked * fold(
            signs_ref.at[0], f
        ).astype(F32)
    power = jnp.broadcast_to(jnp.sum(power, axis=1, keepdims=True), (rows, per_slot))
    out = turned_rows(
        [pieces[k][f] for k in range(slots) for f in range(cycles)]
        + [scalars_ref[:, :per_slot], power]
    )
    for c in range(cores):
        send_ref[pl.ds(c, places, stride=cores), :] = out[c * places : (c + 1) * places]


def fourth_kernel(
    cores, received_ref, signal_ref, limits_ref, hi_ref, lo_ref, chosen_ref, terms_ref,
    weighted_ref, send_ref,
):
    probes = send_ref.shape[0]
    slots, quarter, total = hi_ref.shape
    cycles = total // received_ref.shape[0]
    places = received_ref.shape[0] // cores
    rows = probes * 2
    blocks = quarter // LANES
    block_rows = blocks * slots * 2
    by_core = [received_ref[pl.ds(c, places, stride=cores), :].T for c in range(cores)]
    start = slots * cycles * rows
    scalars = jnp.sum(by_core[0][start : start + 3 * rows], axis=1, keepdims=True)
    for values in by_core[1:]:
        scalars = scalars + jnp.sum(values[start : start + 3 * rows], axis=1, keepdims=True)
    lane = iota((rows, LANES), 1)
    tile = jnp.where(
        lane == 0, scalars[:rows], jnp.where(lane == 1, scalars[rows : 2 * rows], scalars[2 * rows :])
    )
    for p in range(probes):
        send_ref[p, 2 * block_rows : 2 * block_rows + rows, :] = tile
        send_ref[p, 2 * block_rows + rows :, :] = weighted_ref[...]
    values = latitude_values(by_core, chosen_ref[...], slots, cycles, rows)
    first_degree = lax.axis_index("probe") * quarter
    signal = signal_ref[...]
    for k in range(slots):
        noise_terms = degree_sums(
            hi_ref[k], lo_ref[k], values, k, rows, limits_ref[k : k + 1, :1], first_degree
        )
        terms = terms_ref[k]
        image = signal * terms + noise_terms
        for p in range(probes):
            for b in range(blocks):
                place = (b * slots + k) * 2
                own = (slice(p * 2, p * 2 + 2), slice(b * LANES, (b + 1) * LANES))
                send_ref[p, place : place + 2, :] = terms[own]
                send_ref[p, block_rows + place : block_rows + place + 2, :] = image[own]


def last_kernel(received_ref, residual_ref, variance_ref):
    probes = received_ref.shape[0]
    slots = residual_ref.shape[1]
    quarter = residual_ref.shape[3] // probes
    blocks = quarter // LANES
    block_rows = blocks * slots * 2
    rows = probes * 2
    cycles, length = variance_ref.shape
    own = lax.axis_index("probe")
    start = 2 * block_rows
    tiles = [received_ref[p, start : start + rows, :] for p in range(probes)]
    degree_part = tiles[0]
    for tile in tiles[1:]:
        degree_part = degree_part + tile
    shape = (rows, LANES)
    norm = jnp.broadcast_to(degree_part[:, :1], shape)
    curve = jnp.broadcast_to(degree_part[:, 1:2] + tiles[0][:, 2:3], shape)
    ratios = [
        (norm[2 * p : 2 * p + 1] + norm[2 * p + 1 : 2 * p + 2])
        / (curve[2 * p : 2 * p + 1] + curve[2 * p + 1 : 2 * p + 2])
        for p in range(probes)
    ]
    start = start + rows
    total = received_ref[0, start:, :] * ratios[0]
    for p in range(1, probes):
        total = total + received_ref[p, start:, :] * ratios[p]
    total = total * (1.0 / probes)
    for j in range(length // LANES):
        variance_ref[:, j * LANES : (j + 1) * LANES] = total[j * cycles : (j + 1) * cycles]
    own_ratio = ratios[0]
    for p in range(1, probes):
        own_ratio = jnp.where(own == p, ratios[p], own_ratio)
    for x in range(probes):
        residual = (
            received_ref[x, :block_rows, :]
            - own_ratio * received_ref[x, block_rows : 2 * block_rows, :]
        )
        for b in range(blocks):
            for k in range(slots):
                place = x * quarter + b * LANES
                row = (b * slots + k) * 2
                residual_ref[0, k, :, place : place + LANES] = residual[row : row + 2]


def call(kernel, outs, scratch, args, name, far=()):
    spaces = [pltpu.HBM if i in far else pltpu.VMEM for i in range(len(args))]
    args = [
        pltpu.with_memory_space_constraint(arg, space) if space == pltpu.HBM else arg
        for arg, space in zip(args, spaces)
    ]
    return pl.pallas_call(
        kernel,
        out_shape=[jax.ShapeDtypeStruct(shape, dtype) for shape, dtype in outs],
        in_specs=[pl.BlockSpec(memory_space=space) for space in spaces],
        out_specs=[pl.BlockSpec(memory_space=pltpu.VMEM)] * len(outs),
        scratch_shapes=scratch,
        compiler_params=pltpu.CompilerParams(vmem_limit_bytes=VMEM_BYTES),
        name=name,
        cost_estimate=pl.CostEstimate(flops=2000000000, bytes_accessed=20000000, transcendentals=0),
    )(*args)


def per_device(legendre, signs, inv_noise, inv_signal, harmonic_order_values, cycle_rows):
    slots, quarter, total = legendre.shape
    _, cycles, length = signs.shape
    probes = lax.axis_size("probe")
    places = lax.axis_size("place")
    cores = lax.axis_size("core")
    count = harmonic_order_values.shape[0]
    outer = length // LANES
    rows = probes * 2
    folded = ((outer * cycles, LANES), F32)

    def everywhere(send):
        received = lax.all_to_all(
            send.reshape(probes * places, LANES), ("probe", "place"), 0, 0, tiled=True
        )
        return lax.all_gather(received, "core", axis=0)

    (
        send, inner_table, outer_table, limits, signs_near, row_line, signal,
        noise_near,
    ) = call(
        functools.partial(first_kernel, slots),
        [
            ((probes, places, LANES), F32),
            ((4 * LANES, 2 * count), BF16),
            ((outer, 2 * count), F32),
            ((8, LANES), jnp.int32),
            (signs.shape, jnp.int32),
            ((1, total), jnp.int32),
            ((1, quarter), F32),
            (inv_noise.shape, F32),
        ],
        [
            pltpu.VMEM((1, count), jnp.int32),
            pltpu.VMEM((1, total), jnp.int32),
            pltpu.SemaphoreType.DMA((5,)),
        ],
        (
            harmonic_order_values.reshape(1, count), signs, cycle_rows.reshape(1, total),
            inv_signal.reshape(1, probes * quarter), inv_noise,
        ),
        "cycle_sums",
        range(5),
    )
    received = everywhere(send)
    send, terms, scalars, leg_hi, leg_lo, chosen = call(
        second_kernel,
        [
            ((probes, places, LANES), F32),
            ((slots, rows, quarter), F32),
            ((2 * rows, LANES), F32),
            (legendre.shape, BF16),
            (legendre.shape, BF16),
            ((total, total), BF16),
        ],
        [],
        (received, row_line, signal, limits, legendre),
        "degrees_there_and_back",
    )
    received = everywhere(send)
    send, weighted = call(
        functools.partial(third_kernel, slots),
        [((places * cores, LANES), F32), folded],
        [pltpu.VMEM((cycles, probes * outer, LANES), F32)],
        (received, signs_near, noise_near, inner_table, outer_table, scalars),
        "cycles_there_and_back",
    )
    received = lax.all_to_all(send, ("place", "core"), 0, 0, tiled=True)
    height = quarter // LANES * slots * 4 + rows + outer * cycles
    (send,) = call(
        functools.partial(fourth_kernel, cores),
        [((probes, height, LANES), F32)],
        [],
        (received, signal, limits, leg_hi, leg_lo, chosen, terms, weighted),
        "image_terms",
    )
    received = lax.all_to_all(send, "probe", 0, 0, tiled=True)
    return call(
        last_kernel,
        [((1, slots, 2, probes * quarter), F32), ((cycles, length), F32)],
        [],
        (received,),
        "outputs",
    )


def solution(mesh):
    cores = 2
    split = jax.sharding.Mesh(
        mesh.devices.reshape(mesh.shape["probe"], -1, cores), ("probe", "place", "core")
    )
    sky = ("place", "core")
    in_specs = (P(sky, "probe", None), P("probe", sky, None), P(sky, None), P(), P(), P())
    out_specs = (P("probe", sky, None, None), P(sky, None))

    def run(*args):
        return tuple(
            jax.shard_map(
                per_device, mesh=split, in_specs=in_specs, out_specs=out_specs, check_vma=False
            )(*args)
        )

    return run
```

```python
import functools
import math

import jax
import jax.numpy as jnp
from jax import lax
from jax.experimental import pallas as pl
from jax.experimental.pallas import tpu as pltpu
from jax.sharding import PartitionSpec as P

F32 = jnp.float32
BF16 = jnp.bfloat16
LANES = 128
VMEM_BYTES = 24 * 1024 * 1024


def iota(shape, dim):
    return lax.broadcasted_iota(jnp.int32, shape, dim)


def dot(a, b):
    return jnp.dot(a, b, preferred_element_type=F32)


def dot_rows(a, b):
    return lax.dot_general(a, b, (((1,), (1,)), ((), ())), preferred_element_type=F32)


def halves(value):
    high = value.astype(BF16)
    return high, (value - high.astype(F32)).astype(BF16)


def fold(flat_ref, f):
    return jnp.concatenate(
        [
            flat_ref[f : f + 1, j * LANES : (j + 1) * LANES]
            for j in range(flat_ref.shape[1] // LANES)
        ],
        axis=0,
    )


def cosine(phase, turn):
    shift = turn.bit_length() - 3
    quadrant = (phase + turn // 8) >> shift
    angle = (phase - (quadrant << shift)).astype(F32) * (2.0 * math.pi / turn)
    square = angle * angle
    cos = 1.0 + square * (
        -1.0 / 2 + square * (1.0 / 24 + square * (-1.0 / 720 + square * (1.0 / 40320)))
    )
    sin = angle * (
        1.0 + square * (-1.0 / 6 + square * (1.0 / 120 + square * (-1.0 / 5040 + square / 362880)))
    )
    value = jnp.where((quadrant & 1) == 1, sin, cos)
    return jnp.where(((quadrant + 1) & 2) == 2, -value, value)


def cosine_and_sine(rows, step, turn):
    half = LANES // 2
    lane = iota((rows, LANES), 1)
    phase = iota((rows, LANES), 0) * (lane & (half - 1)) * step
    return cosine(phase - jnp.where(lane >= half, turn // 4, 0), turn)


def ones_where(condition):
    return jnp.where(condition, 1.0, 0.0).astype(BF16)


def both_picks(line):
    half = LANES // 2
    count = line.shape[1]
    shape = (LANES, 2 * count)
    row, col = iota(shape, 0), iota(shape, 1)
    wide = jnp.concatenate([line, line], axis=1)
    return ones_where(row == wide + jnp.where(col >= count, half, 0))


def turned_rows(pieces):
    rows = jnp.concatenate(pieces, axis=0)
    if rows.shape[0] < LANES:
        rows = jnp.concatenate(
            [rows, jnp.zeros((LANES - rows.shape[0], rows.shape[1]), F32)], axis=0
        )
    return rows.T


def own_rows(received_ref, source, groups):
    places = received_ref.shape[1] // groups
    total = received_ref[source, :places]
    for g in range(1, groups):
        total = total + received_ref[source, g * places : (g + 1) * places]
    total = total.T
    half = LANES // 2
    return jnp.where(lax.axis_index("core") == 0, total[:half], total[half:])


def first_kernel(
    slots, orders_hbm, signs_hbm, rows_hbm, signal_hbm, noise_hbm,
    send_ref, inner_ref, outer_ref, limits_ref, signs_ref,
    rows_ref, signal_ref, noise_ref,
    orders_ref, near_rows_ref, sems,
):
    count = orders_ref.shape[1]
    probes, places = send_ref.shape[:2]
    _, cycles, cycle_length = signs_ref.shape
    outer = cycle_length // LANES
    cores = count // slots // places
    total = rows_ref.shape[1]
    own = lax.axis_index("probe")
    quarter = signal_ref.shape[1]
    own_signal = signal_hbm.at[:, pl.ds(pl.multiple_of(own * quarter, LANES), quarter)]

    copies = [
        pltpu.make_async_copy(source, target, sems.at[n])
        for n, (source, target) in enumerate(
            [
                (orders_hbm, orders_ref),
                (signs_hbm, signs_ref),
                (rows_hbm, near_rows_ref),
                (own_signal, signal_ref),
                (noise_hbm, noise_ref),
            ]
        )
    ]
    for copy in copies:
        copy.start()

    high_table = halves(cosine_and_sine(LANES, 64, cycle_length))
    low_table = halves(cosine_and_sine(LANES, 1, cycle_length))
    outer_table = halves(cosine_and_sine(outer, cycle_length // outer, cycle_length))
    slot, place = iota((count, count), 0), iota((count, count), 1)
    slot_picks = ones_where(
        slot == (place % places * cores + place // places % cores) * slots
        + place // (places * cores)
    )

    copies[0].wait()
    orders = orders_ref[...]
    row = iota((8, count), 0)
    parts = jnp.where(row == 0, orders >> 6, jnp.where(row == 1, orders & 63, 0))
    parts = dot(parts.astype(F32).astype(BF16), slot_picks).astype(jnp.int32)
    high, low = parts[:1], parts[1:2]
    for k in range(slots):
        own_place = (k * cores + lax.axis_index("core")) * places + lax.axis_index("place")
        picked = jnp.where(iota((1, count), 1) == own_place, high * 64 + low, 0).astype(F32)
        picked = jnp.sum(picked, axis=1, keepdims=True).astype(jnp.int32)
        limits_ref[k : k + 1, :] = jnp.broadcast_to(picked, (1, LANES))
    high_picks, low_picks = both_picks(high), both_picks(low)
    high_part = dot(high_table[0], high_picks) + dot(high_table[1], high_picks)
    low_part = dot(low_table[0], low_picks) + dot(low_table[1], low_picks)
    scale_factor = 1.0 / math.sqrt(cycle_length)
    high_cos, high_sin = high_part[:, :count] * scale_factor, high_part[:, count:] * scale_factor
    low_cos, low_sin = low_part[:, :count], low_part[:, count:]
    inner_cos = high_cos * low_cos - high_sin * low_sin
    inner_sin = high_sin * low_cos + high_cos * low_sin
    inner = halves(jnp.concatenate([inner_cos, inner_sin], axis=1))
    for n in range(4):
        inner_ref[n * LANES : (n + 1) * LANES, :] = inner[n // 2]
    outer_part = dot(outer_table[0], low_picks) + dot(outer_table[1], low_picks)
    outer_ref[...] = outer_part

    copies[1].wait()
    rows = probes * 2
    row = iota((rows, count), 0)
    pixels = jnp.concatenate(
        [fold(signs_ref.at[0], f).astype(F32) for f in range(cycles)], axis=0
    ).astype(BF16)
    sums = dot(jnp.concatenate([pixels, pixels], axis=1), inner_ref[LANES : 3 * LANES, :])
    pieces = [[None] * cycles for _ in range(slots)]
    per_slot = count // slots
    for f in range(cycles):
        cos_sum, sin_sum = twiddle_sums(sums[f * outer : (f + 1) * outer], outer_part)
        field = jnp.where(
            row == own * 2, cos_sum, jnp.where(row == own * 2 + 1, sin_sum, 0.0)
        )
        for k in range(slots):
            pieces[k][f] = field[:, k * per_slot : (k + 1) * per_slot]
    out = turned_rows(
        [
            pieces[k][f][:, c * places : (c + 1) * places]
            for c in range(cores)
            for k in range(slots)
            for f in range(cycles)
        ]
    )
    for p in range(probes):
        send_ref[p] = out

    for copy in copies[2:]:
        copy.wait()
    cycle_rows = near_rows_ref[...]
    row = iota((8, total), 0)
    parts = jnp.where(row == 0, cycle_rows >> 6, jnp.where(row == 1, cycle_rows & 63, 0))
    cycle, place = iota((total, total), 0), iota((total, total), 1)
    picks = ones_where(
        cycle == (place % places * cores + place // (places * cycles)) * cycles
        + place // places % cycles
    )
    parts = dot(parts.astype(F32).astype(BF16), picks).astype(jnp.int32)
    rows_ref[...] = parts[:1] * 64 + parts[1:2]


def twiddle_sums(sums, table):
    count = table.shape[1] // 2
    cos, sin = table[:, :count], table[:, count:]
    by_cos, by_sin = sums[:, :count], sums[:, count:]
    return (
        jnp.sum(cos * by_cos - sin * by_sin, axis=0, keepdims=True),
        jnp.sum(sin * by_cos + cos * by_sin, axis=0, keepdims=True),
    )


def latitude_values(by_core, chosen, slots, cycles, rows):
    values = [
        jnp.concatenate(
            [
                values[(k * cycles + f) * rows : (k * cycles + f + 1) * rows]
                for values in by_core
                for f in range(cycles)
            ],
            axis=1,
        )
        for k in range(slots)
    ]
    both = jnp.concatenate(halves(jnp.concatenate(values, axis=0)), axis=0)
    return dot_rows(both, chosen).astype(BF16)


def degree_sums(leg_hi, leg_lo, values, k, rows, order, first_degree):
    width = values.shape[0] // 2
    across = dot(values, leg_hi) + dot(values, leg_lo)
    terms = across[k * rows : (k + 1) * rows] + across[
        width + k * rows : width + (k + 1) * rows
    ]
    degrees = first_degree + iota(terms.shape, 1)
    return jnp.where(degrees >= order, terms, 0.0)


def second_kernel(
    received_ref, rows_ref, signal_ref, limits_ref, legendre_ref,
    send_ref, terms_ref, scalars_ref, hi_ref, lo_ref, chosen_ref,
):
    cores = received_ref.shape[0]
    probes, places = send_ref.shape[:2]
    slots, quarter, total = legendre_ref.shape
    cycles = total // (places * cores)
    rows = probes * 2
    width = slots * rows
    chosen = ones_where(iota((total, total), 0) == rows_ref[...])
    chosen_ref[...] = chosen
    values = latitude_values(
        [own_rows(received_ref, c, probes) for c in range(cores)], chosen, slots, cycles, rows
    )
    first_degree = lax.axis_index("probe") * quarter
    signal = signal_ref[...]
    norm = jnp.zeros((rows, 1), F32)
    prior = jnp.zeros((rows, 1), F32)
    for k in range(slots):
        hi_ref[k], lo_ref[k] = halves(legendre_ref[k].T)
    both = []
    for k in range(slots):
        terms = degree_sums(
            hi_ref[k], lo_ref[k], values, k, rows, limits_ref[k : k + 1, :1], first_degree
        )
        terms_ref[k] = terms
        squares = terms * terms
        norm = norm + jnp.sum(squares, axis=1, keepdims=True)
        prior = prior + jnp.sum(squares * signal, axis=1, keepdims=True)
        both.append(jnp.concatenate(halves(terms), axis=0))
    fields = []
    for k in range(slots):
        leg_hi, leg_lo = halves(legendre_ref[k])
        field = dot(both[k], leg_hi) + dot(both[k], leg_lo)
        fields.append(field[:rows] + field[rows:])
    both = jnp.concatenate(halves(jnp.concatenate(fields, axis=0)), axis=0)
    by_cycle = dot(both, chosen)
    by_cycle = by_cycle[:width] + by_cycle[width:]
    out = turned_rows(
        [
            by_cycle[k * rows : (k + 1) * rows, place * places : (place + 1) * places]
            for c in range(cores)
            for k in range(slots)
            for place in range(c * cycles, (c + 1) * cycles)
        ]
    )
    for p in range(probes):
        send_ref[p] = out
    scalars_ref[:rows, :] = jnp.broadcast_to(norm, (rows, LANES))
    scalars_ref[rows:, :] = jnp.broadcast_to(prior, (rows, LANES))


def third_kernel(
    slots, received_ref, signs_ref, inv_noise_ref, inner_ref, outer_ref, scalars_ref,
    send_ref, weighted_ref, mapped_ref,
):
    cores = received_ref.shape[0]
    places = send_ref.shape[0] // cores
    probes = received_ref.shape[1] // places
    cycles = inv_noise_ref.shape[0]
    outer, count = outer_ref.shape[0], outer_ref.shape[1] // 2
    rows = probes * 2
    own = lax.axis_index("probe")

    by_core = [own_rows(received_ref, c, probes) for c in range(cores)]
    outer_cos, outer_sin = outer_ref[:, :count], outer_ref[:, count:]
    per_slot = count // slots
    row = iota((rows, count), 0)
    power = jnp.zeros((rows, LANES), F32)
    power_row = iota((rows, LANES), 0)
    pieces = [[None] * cycles for _ in range(slots)]
    table = inner_ref[LANES : 3 * LANES, :]

    def map_cycle(f):
        coeffs = jnp.concatenate(
            [
                by_core[c][(k * cycles + f) * rows : (k * cycles + f + 1) * rows]
                for k in range(slots)
                for c in range(cores)
            ],
            axis=1,
        )
        high, low = [], []
        for p in range(probes):
            cos_coeff, sin_coeff = coeffs[2 * p : 2 * p + 1], coeffs[2 * p + 1 : 2 * p + 2]
            by_cos = cos_coeff * outer_cos + sin_coeff * outer_sin
            by_sin = sin_coeff * outer_cos - cos_coeff * outer_sin
            hi, lo = halves(jnp.concatenate([by_cos, by_sin], axis=1))
            high.append(hi)
            low.append(lo)
        mapped = dot_rows(jnp.concatenate(high, axis=0), table) + dot_rows(
            jnp.concatenate(low, axis=0), table
        )
        return mapped[:, :LANES] + mapped[:, LANES:]

    def weigh_cycle(f, mapped):
        mapped_ref[f] = mapped
        pixels = jnp.concatenate([fold(inv_noise_ref, f)] * probes, axis=0) * mapped
        squares = pixels * mapped
        lines = [
            jnp.sum(squares[p * outer : (p + 1) * outer], axis=0, keepdims=True)
            for p in range(probes)
        ]
        hi, lo = halves(pixels)
        sums = dot(jnp.concatenate([hi, lo, hi, lo], axis=1), inner_ref[...])
        return lines, [sums[p * outer : (p + 1) * outer] for p in range(probes)]

    def finish_cycle(f, lines, sums):
        nonlocal power
        field = jnp.zeros((rows, count), F32)
        for p in range(probes):
            power = power + jnp.where(power_row == 2 * p, lines[p], 0.0)
            cos_sum, sin_sum = twiddle_sums(sums[p], outer_ref[...])
            field = jnp.where(row == 2 * p, cos_sum, field)
            field = jnp.where(row == 2 * p + 1, sin_sum, field)
        for k in range(slots):
            pieces[k][f] = field[:, k * per_slot : (k + 1) * per_slot]

    mapped, done = map_cycle(0), None
    for f in range(cycles):
        later = map_cycle(f + 1) if f + 1 < cycles else None
        lines, sums = weigh_cycle(f, mapped)
        if done:
            finish_cycle(*done)
        mapped, done = later, (f, lines, sums)
    finish_cycle(*done)
    for f in range(cycles):
        picked = mapped_ref[f, pl.ds(pl.multiple_of(own * outer, outer), outer), :]
        weighted_ref[pl.ds(f, outer, stride=cycles), :] = picked * fold(
            signs_ref.at[0], f
        ).astype(F32)
    power = jnp.broadcast_to(jnp.sum(power, axis=1, keepdims=True), (rows, per_slot))
    out = turned_rows(
        [pieces[k][f] for k in range(slots) for f in range(cycles)]
        + [scalars_ref[:, :per_slot], power]
    )
    for c in range(cores):
        send_ref[pl.ds(c, places, stride=cores), :] = out[c * places : (c + 1) * places]


def fourth_kernel(
    cores, received_ref, signal_ref, limits_ref, hi_ref, lo_ref, chosen_ref, terms_ref,
    weighted_ref, send_ref,
):
    probes = send_ref.shape[0]
    slots, total, quarter = hi_ref.shape
    cycles = total // received_ref.shape[0]
    places = received_ref.shape[0] // cores
    rows = probes * 2
    blocks = quarter // LANES
    block_rows = blocks * slots * 2
    by_core = [received_ref[pl.ds(c, places, stride=cores), :].T for c in range(cores)]
    start = slots * cycles * rows
    scalars = jnp.sum(by_core[0][start : start + 3 * rows], axis=1, keepdims=True)
    for values in by_core[1:]:
        scalars = scalars + jnp.sum(values[start : start + 3 * rows], axis=1, keepdims=True)
    lane = iota((rows, LANES), 1)
    tile = jnp.where(
        lane == 0, scalars[:rows], jnp.where(lane == 1, scalars[rows : 2 * rows], scalars[2 * rows :])
    )
    for p in range(probes):
        send_ref[p, 2 * block_rows : 2 * block_rows + rows, :] = tile
        send_ref[p, 2 * block_rows + rows :, :] = weighted_ref[...]
    values = latitude_values(by_core, chosen_ref[...], slots, cycles, rows)
    first_degree = lax.axis_index("probe") * quarter
    signal = signal_ref[...]
    for k in range(slots):
        noise_terms = degree_sums(
            hi_ref[k], lo_ref[k], values, k, rows, limits_ref[k : k + 1, :1], first_degree
        )
        terms = terms_ref[k]
        image = signal * terms + noise_terms
        for p in range(probes):
            for b in range(blocks):
                place = (b * slots + k) * 2
                own = (slice(p * 2, p * 2 + 2), slice(b * LANES, (b + 1) * LANES))
                send_ref[p, place : place + 2, :] = terms[own]
                send_ref[p, block_rows + place : block_rows + place + 2, :] = image[own]


def last_kernel(received_ref, residual_ref, variance_ref):
    probes = received_ref.shape[0]
    slots = residual_ref.shape[1]
    quarter = residual_ref.shape[3] // probes
    blocks = quarter // LANES
    block_rows = blocks * slots * 2
    rows = probes * 2
    cycles, length = variance_ref.shape
    own = lax.axis_index("probe")
    start = 2 * block_rows
    tiles = [received_ref[p, start : start + rows, :] for p in range(probes)]
    degree_part = tiles[0]
    for tile in tiles[1:]:
        degree_part = degree_part + tile
    shape = (rows, LANES)
    norm = jnp.broadcast_to(degree_part[:, :1], shape)
    curve = jnp.broadcast_to(degree_part[:, 1:2] + tiles[0][:, 2:3], shape)
    ratios = [
        (norm[2 * p : 2 * p + 1] + norm[2 * p + 1 : 2 * p + 2])
        / (curve[2 * p : 2 * p + 1] + curve[2 * p + 1 : 2 * p + 2])
        for p in range(probes)
    ]
    start = start + rows
    total = received_ref[0, start:, :] * ratios[0]
    for p in range(1, probes):
        total = total + received_ref[p, start:, :] * ratios[p]
    total = total * (1.0 / probes)
    for j in range(length // LANES):
        variance_ref[:, j * LANES : (j + 1) * LANES] = total[j * cycles : (j + 1) * cycles]
    own_ratio = ratios[0]
    for p in range(1, probes):
        own_ratio = jnp.where(own == p, ratios[p], own_ratio)
    for x in range(probes):
        residual = (
            received_ref[x, :block_rows, :]
            - own_ratio * received_ref[x, block_rows : 2 * block_rows, :]
        )
        for b in range(blocks):
            for k in range(slots):
                place = x * quarter + b * LANES
                row = (b * slots + k) * 2
                residual_ref[0, k, :, place : place + LANES] = residual[row : row + 2]


def call(kernel, outs, scratch, args, name, far=()):
    spaces = [pltpu.HBM if i in far else pltpu.VMEM for i in range(len(args))]
    args = [
        pltpu.with_memory_space_constraint(arg, space) if space == pltpu.HBM else arg
        for arg, space in zip(args, spaces)
    ]
    return pl.pallas_call(
        kernel,
        out_shape=[jax.ShapeDtypeStruct(shape, dtype) for shape, dtype in outs],
        in_specs=[pl.BlockSpec(memory_space=space) for space in spaces],
        out_specs=[pl.BlockSpec(memory_space=pltpu.VMEM)] * len(outs),
        scratch_shapes=scratch,
        compiler_params=pltpu.CompilerParams(vmem_limit_bytes=VMEM_BYTES),
        name=name,
        cost_estimate=pl.CostEstimate(flops=2000000000, bytes_accessed=20000000, transcendentals=0),
    )(*args)


def per_device(legendre, signs, inv_noise, inv_signal, harmonic_order_values, cycle_rows):
    slots, quarter, total = legendre.shape
    _, cycles, length = signs.shape
    probes = lax.axis_size("probe")
    places = lax.axis_size("place")
    cores = lax.axis_size("core")
    count = harmonic_order_values.shape[0]
    outer = length // LANES
    rows = probes * 2
    folded = ((outer * cycles, LANES), F32)

    def everywhere(send):
        received = lax.all_to_all(
            send.reshape(probes * places, LANES), ("probe", "place"), 0, 0, tiled=True
        )
        return lax.all_gather(received, "core", axis=0)

    (
        send, inner_table, outer_table, limits, signs_near, row_line, signal,
        noise_near,
    ) = call(
        functools.partial(first_kernel, slots),
        [
            ((probes, places, LANES), F32),
            ((4 * LANES, 2 * count), BF16),
            ((outer, 2 * count), F32),
            ((8, LANES), jnp.int32),
            (signs.shape, jnp.int32),
            ((1, total), jnp.int32),
            ((1, quarter), F32),
            (inv_noise.shape, F32),
        ],
        [
            pltpu.VMEM((1, count), jnp.int32),
            pltpu.VMEM((1, total), jnp.int32),
            pltpu.SemaphoreType.DMA((5,)),
        ],
        (
            harmonic_order_values.reshape(1, count), signs, cycle_rows.reshape(1, total),
            inv_signal.reshape(1, probes * quarter), inv_noise,
        ),
        "cycle_sums",
        range(5),
    )
    received = everywhere(send)
    send, terms, scalars, leg_hi, leg_lo, chosen = call(
        second_kernel,
        [
            ((probes, places, LANES), F32),
            ((slots, rows, quarter), F32),
            ((2 * rows, LANES), F32),
            ((slots, total, quarter), BF16),
            ((slots, total, quarter), BF16),
            ((total, total), BF16),
        ],
        [],
        (received, row_line, signal, limits, legendre),
        "degrees_there_and_back",
    )
    received = everywhere(send)
    send, weighted = call(
        functools.partial(third_kernel, slots),
        [((places * cores, LANES), F32), folded],
        [pltpu.VMEM((cycles, probes * outer, LANES), F32)],
        (received, signs_near, noise_near, inner_table, outer_table, scalars),
        "cycles_there_and_back",
    )
    received = lax.all_to_all(send, ("place", "core"), 0, 0, tiled=True)
    height = quarter // LANES * slots * 4 + rows + outer * cycles
    (send,) = call(
        functools.partial(fourth_kernel, cores),
        [((probes, height, LANES), F32)],
        [],
        (received, signal, limits, leg_hi, leg_lo, chosen, terms, weighted),
        "image_terms",
    )
    received = lax.all_to_all(send, "probe", 0, 0, tiled=True)
    return call(
        last_kernel,
        [((1, slots, 2, probes * quarter), F32), ((cycles, length), F32)],
        [],
        (received,),
        "outputs",
    )


def solution(mesh):
    cores = 2
    split = jax.sharding.Mesh(
        mesh.devices.reshape(mesh.shape["probe"], -1, cores), ("probe", "place", "core")
    )
    sky = ("place", "core")
    in_specs = (P(sky, "probe", None), P("probe", sky, None), P(sky, None), P(), P(), P())
    out_specs = (P("probe", sky, None, None), P(sky, None))

    def run(*args):
        return tuple(
            jax.shard_map(
                per_device, mesh=split, in_specs=in_specs, out_specs=out_specs, check_vma=False
            )(*args)
        )

    return run
```

```python
import functools
import math

import jax
import jax.numpy as jnp
from jax import lax
from jax.experimental import pallas as pl
from jax.experimental.pallas import tpu as pltpu
from jax.sharding import PartitionSpec as P

F32 = jnp.float32
BF16 = jnp.bfloat16
LANES = 128
VMEM_BYTES = 24 * 1024 * 1024


def iota(shape, dim):
    return lax.broadcasted_iota(jnp.int32, shape, dim)


def dot(a, b):
    return jnp.dot(a, b, preferred_element_type=F32)


def dot_rows(a, b):
    return lax.dot_general(a, b, (((1,), (1,)), ((), ())), preferred_element_type=F32)


def halves(value):
    high = value.astype(BF16)
    return high, (value - high.astype(F32)).astype(BF16)


def fold(flat_ref, f):
    return jnp.concatenate(
        [
            flat_ref[f : f + 1, j * LANES : (j + 1) * LANES]
            for j in range(flat_ref.shape[1] // LANES)
        ],
        axis=0,
    )


def cosine(phase, turn):
    shift = turn.bit_length() - 3
    quadrant = (phase + turn // 8) >> shift
    angle = (phase - (quadrant << shift)).astype(F32) * (2.0 * math.pi / turn)
    square = angle * angle
    cos = 1.0 + square * (
        -1.0 / 2 + square * (1.0 / 24 + square * (-1.0 / 720 + square * (1.0 / 40320)))
    )
    sin = angle * (
        1.0 + square * (-1.0 / 6 + square * (1.0 / 120 + square * (-1.0 / 5040 + square / 362880)))
    )
    value = jnp.where((quadrant & 1) == 1, sin, cos)
    return jnp.where(((quadrant + 1) & 2) == 2, -value, value)


def cosine_and_sine(rows, step, turn):
    half = LANES // 2
    lane = iota((rows, LANES), 1)
    phase = iota((rows, LANES), 0) * (lane & (half - 1)) * step
    return cosine(phase - jnp.where(lane >= half, turn // 4, 0), turn)


def ones_where(condition):
    return jnp.where(condition, 1.0, 0.0).astype(BF16)


def both_picks(line):
    half = LANES // 2
    count = line.shape[1]
    shape = (LANES, 2 * count)
    row, col = iota(shape, 0), iota(shape, 1)
    wide = jnp.concatenate([line, line], axis=1)
    return ones_where(row == wide + jnp.where(col >= count, half, 0))


def turned_rows(pieces):
    rows = jnp.concatenate(pieces, axis=0)
    if rows.shape[0] < LANES:
        rows = jnp.concatenate(
            [rows, jnp.zeros((LANES - rows.shape[0], rows.shape[1]), F32)], axis=0
        )
    return rows.T


def device_of(place, tall, count):
    return place % tall * (count // tall) + place // tall


def store_by_device(rows, target_ref, tall):
    lines = rows.shape[0] // tall
    for n in range(lines):
        target_ref[pl.ds(n, tall, stride=lines), :] = rows[n * tall : (n + 1) * tall]


def first_kernel(
    slots, tall, orders_hbm, signs_hbm, rows_hbm, signal_hbm, noise_hbm,
    send_ref, inner_ref, outer_ref, limits_ref, signs_ref,
    rows_ref, signal_ref, noise_ref,
    orders_ref, near_rows_ref, sems,
):
    count = orders_ref.shape[1]
    probes, places = send_ref.shape[:2]
    _, cycles, cycle_length = signs_ref.shape
    outer = cycle_length // LANES
    total = rows_ref.shape[1]
    own = lax.axis_index("probe")
    quarter = signal_ref.shape[1]
    own_signal = signal_hbm.at[:, pl.ds(pl.multiple_of(own * quarter, LANES), quarter)]

    copies = [
        pltpu.make_async_copy(source, target, sems.at[n])
        for n, (source, target) in enumerate(
            [
                (orders_hbm, orders_ref),
                (signs_hbm, signs_ref),
                (rows_hbm, near_rows_ref),
                (own_signal, signal_ref),
                (noise_hbm, noise_ref),
            ]
        )
    ]
    for copy in copies:
        copy.start()

    high_table = halves(cosine_and_sine(LANES, 64, cycle_length))
    low_table = halves(cosine_and_sine(LANES, 1, cycle_length))
    outer_table = halves(cosine_and_sine(outer, cycle_length // outer, cycle_length))
    slot, place = iota((count, count), 0), iota((count, count), 1)
    slot_picks = ones_where(
        slot == device_of(place % places, tall, places) * slots + place // places
    )

    copies[0].wait()
    orders = orders_ref[...]
    row = iota((8, count), 0)
    parts = jnp.where(row == 0, orders >> 6, jnp.where(row == 1, orders & 63, 0))
    parts = dot(parts.astype(F32).astype(BF16), slot_picks).astype(jnp.int32)
    high, low = parts[:1], parts[1:2]
    own_line = lax.axis_index("z") * lax.axis_size("core") + lax.axis_index("core")
    for k in range(slots):
        own_place = k * places + own_line * tall + lax.axis_index("y")
        picked = jnp.where(iota((1, count), 1) == own_place, high * 64 + low, 0).astype(F32)
        picked = jnp.sum(picked, axis=1, keepdims=True).astype(jnp.int32)
        limits_ref[k : k + 1, :] = jnp.broadcast_to(picked, (1, LANES))
    high_picks, low_picks = both_picks(high), both_picks(low)
    high_part = dot(high_table[0], high_picks) + dot(high_table[1], high_picks)
    low_part = dot(low_table[0], low_picks) + dot(low_table[1], low_picks)
    scale_factor = 1.0 / math.sqrt(cycle_length)
    high_cos, high_sin = high_part[:, :count] * scale_factor, high_part[:, count:] * scale_factor
    low_cos, low_sin = low_part[:, :count], low_part[:, count:]
    inner_cos = high_cos * low_cos - high_sin * low_sin
    inner_sin = high_sin * low_cos + high_cos * low_sin
    inner = halves(jnp.concatenate([inner_cos, inner_sin], axis=1))
    for n in range(4):
        inner_ref[n * LANES : (n + 1) * LANES, :] = inner[n // 2]
    outer_part = dot(outer_table[0], low_picks) + dot(outer_table[1], low_picks)
    outer_ref[...] = outer_part

    copies[1].wait()
    rows = probes * 2
    row = iota((rows, count), 0)
    pixels = jnp.concatenate(
        [fold(signs_ref.at[0], f).astype(F32) for f in range(cycles)], axis=0
    ).astype(BF16)
    sums = dot(jnp.concatenate([pixels, pixels], axis=1), inner_ref[LANES : 3 * LANES, :])
    pieces = [[None] * cycles for _ in range(slots)]
    per_slot = count // slots
    for f in range(cycles):
        cos_sum, sin_sum = twiddle_sums(sums[f * outer : (f + 1) * outer], outer_part)
        field = jnp.where(
            row == own * 2, cos_sum, jnp.where(row == own * 2 + 1, sin_sum, 0.0)
        )
        for k in range(slots):
            pieces[k][f] = field[:, k * per_slot : (k + 1) * per_slot]
    out = turned_rows([pieces[k][f] for k in range(slots) for f in range(cycles)])
    for p in range(probes):
        store_by_device(out, send_ref.at[p], tall)

    for copy in copies[2:]:
        copy.wait()
    cycle_rows = near_rows_ref[...]
    row = iota((8, total), 0)
    parts = jnp.where(row == 0, cycle_rows >> 6, jnp.where(row == 1, cycle_rows & 63, 0))
    cycle, place = iota((total, total), 0), iota((total, total), 1)
    picks = ones_where(
        cycle == device_of(place % places, tall, places) * cycles + place // places
    )
    parts = dot(parts.astype(F32).astype(BF16), picks).astype(jnp.int32)
    rows_ref[...] = parts[:1] * 64 + parts[1:2]


def twiddle_sums(sums, table):
    count = table.shape[1] // 2
    cos, sin = table[:, :count], table[:, count:]
    by_cos, by_sin = sums[:, :count], sums[:, count:]
    return (
        jnp.sum(cos * by_cos - sin * by_sin, axis=0, keepdims=True),
        jnp.sum(sin * by_cos + cos * by_sin, axis=0, keepdims=True),
    )


def join_kernel(tall, received_ref, out_ref):
    places = out_ref.shape[0]
    lines = places // tall
    for n in range(lines):
        total = received_ref[pl.ds(n, tall, stride=lines), :]
        for start in range(places, received_ref.shape[0], places):
            total = total + received_ref[pl.ds(start + n, tall, stride=lines), :]
        out_ref[n * tall : (n + 1) * tall, :] = total


def latitude_values(values, chosen, slots, cycles, rows):
    values = [
        jnp.concatenate(
            [
                values[(k * cycles + f) * rows : (k * cycles + f + 1) * rows]
                for f in range(cycles)
            ],
            axis=1,
        )
        for k in range(slots)
    ]
    both = jnp.concatenate(halves(jnp.concatenate(values, axis=0)), axis=0)
    return dot_rows(both, chosen).astype(BF16)


def degree_sums(leg_hi, leg_lo, values, k, rows, order, first_degree):
    width = values.shape[0] // 2
    across = dot(values, leg_hi) + dot(values, leg_lo)
    terms = across[k * rows : (k + 1) * rows] + across[
        width + k * rows : width + (k + 1) * rows
    ]
    degrees = first_degree + iota(terms.shape, 1)
    return jnp.where(degrees >= order, terms, 0.0)


def second_kernel(
    tall, received_ref, rows_ref, signal_ref, limits_ref, legendre_ref,
    send_ref, terms_ref, hi_ref, lo_ref, chosen_ref,
):
    probes, places = send_ref.shape[:2]
    slots, quarter, total = legendre_ref.shape
    cycles = total // places
    rows = probes * 2
    width = slots * rows
    chosen = ones_where(iota((total, total), 0) == rows_ref[...])
    chosen_ref[...] = chosen
    values = latitude_values(received_ref[...].T, chosen, slots, cycles, rows)
    first_degree = lax.axis_index("probe") * quarter
    signal = signal_ref[...]
    norm = jnp.zeros((rows, 1), F32)
    prior = jnp.zeros((rows, 1), F32)
    for k in range(slots):
        hi_ref[k], lo_ref[k] = halves(legendre_ref[k].T)
    both = []
    for k in range(slots):
        terms = degree_sums(
            hi_ref[k], lo_ref[k], values, k, rows, limits_ref[k : k + 1, :1], first_degree
        )
        terms_ref[k] = terms
        squares = terms * terms
        norm = norm + jnp.sum(squares, axis=1, keepdims=True)
        prior = prior + jnp.sum(squares * signal, axis=1, keepdims=True)
        both.append(jnp.concatenate(halves(terms), axis=0))
    fields = []
    for k in range(slots):
        leg_hi, leg_lo = halves(legendre_ref[k])
        field = dot(both[k], leg_hi) + dot(both[k], leg_lo)
        fields.append(field[:rows] + field[rows:])
    both = jnp.concatenate(halves(jnp.concatenate(fields, axis=0)), axis=0)
    by_cycle = dot(both, chosen)
    by_cycle = by_cycle[:width] + by_cycle[width:]
    out = turned_rows(
        [
            by_cycle[k * rows : (k + 1) * rows, f * places : (f + 1) * places]
            for k in range(slots)
            for f in range(cycles)
        ]
        + [jnp.broadcast_to(column, (rows, places)) for column in (norm, prior)]
    )
    for p in range(probes):
        store_by_device(out, send_ref.at[p], tall)


def third_kernel(
    slots, probes, tall, received_ref, signs_ref, inv_noise_ref, inner_ref, outer_ref,
    send_ref, weighted_ref, scalars_ref, mapped_ref,
):
    cycles = inv_noise_ref.shape[0]
    outer, count = outer_ref.shape[0], outer_ref.shape[1] // 2
    rows = probes * 2
    own = lax.axis_index("probe")

    received = received_ref[...].T
    start = slots * cycles * rows
    scalars_ref[...] = jnp.broadcast_to(
        jnp.sum(received[start : start + 2 * rows], axis=1, keepdims=True), scalars_ref.shape
    )
    outer_cos, outer_sin = outer_ref[:, :count], outer_ref[:, count:]
    per_slot = count // slots
    row = iota((rows, count), 0)
    power = jnp.zeros((rows, LANES), F32)
    power_row = iota((rows, LANES), 0)
    pieces = [[None] * cycles for _ in range(slots)]
    table = inner_ref[LANES : 3 * LANES, :]

    def map_cycle(f):
        coeffs = jnp.concatenate(
            [
                received[(k * cycles + f) * rows : (k * cycles + f + 1) * rows]
                for k in range(slots)
            ],
            axis=1,
        )
        high, low = [], []
        for p in range(probes):
            cos_coeff, sin_coeff = coeffs[2 * p : 2 * p + 1], coeffs[2 * p + 1 : 2 * p + 2]
            by_cos = cos_coeff * outer_cos + sin_coeff * outer_sin
            by_sin = sin_coeff * outer_cos - cos_coeff * outer_sin
            hi, lo = halves(jnp.concatenate([by_cos, by_sin], axis=1))
            high.append(hi)
            low.append(lo)
        mapped = dot_rows(jnp.concatenate(high, axis=0), table) + dot_rows(
            jnp.concatenate(low, axis=0), table
        )
        return mapped[:, :LANES] + mapped[:, LANES:]

    def weigh_cycle(f, mapped):
        mapped_ref[f] = mapped
        pixels = jnp.concatenate([fold(inv_noise_ref, f)] * probes, axis=0) * mapped
        squares = pixels * mapped
        lines = [
            jnp.sum(squares[p * outer : (p + 1) * outer], axis=0, keepdims=True)
            for p in range(probes)
        ]
        hi, lo = halves(pixels)
        sums = dot(jnp.concatenate([hi, lo, hi, lo], axis=1), inner_ref[...])
        return lines, [sums[p * outer : (p + 1) * outer] for p in range(probes)]

    def finish_cycle(f, lines, sums):
        nonlocal power
        field = jnp.zeros((rows, count), F32)
        for p in range(probes):
            power = power + jnp.where(power_row == 2 * p, lines[p], 0.0)
            cos_sum, sin_sum = twiddle_sums(sums[p], outer_ref[...])
            field = jnp.where(row == 2 * p, cos_sum, field)
            field = jnp.where(row == 2 * p + 1, sin_sum, field)
        for k in range(slots):
            pieces[k][f] = field[:, k * per_slot : (k + 1) * per_slot]

    mapped, done = map_cycle(0), None
    for f in range(cycles):
        later = map_cycle(f + 1) if f + 1 < cycles else None
        lines, sums = weigh_cycle(f, mapped)
        if done:
            finish_cycle(*done)
        mapped, done = later, (f, lines, sums)
    finish_cycle(*done)
    for f in range(cycles):
        picked = mapped_ref[f, pl.ds(pl.multiple_of(own * outer, outer), outer), :]
        weighted_ref[pl.ds(f, outer, stride=cycles), :] = picked * fold(
            signs_ref.at[0], f
        ).astype(F32)
    power = jnp.broadcast_to(jnp.sum(power, axis=1, keepdims=True), (rows, per_slot))
    out = turned_rows([pieces[k][f] for k in range(slots) for f in range(cycles)] + [power])
    store_by_device(out, send_ref, tall)


def fourth_kernel(
    tall, received_ref, signal_ref, limits_ref, hi_ref, lo_ref, chosen_ref, terms_ref,
    weighted_ref, scalars_ref, send_ref,
):
    probes = send_ref.shape[0]
    slots, total, quarter = hi_ref.shape
    places = received_ref.shape[0]
    cycles = total // places
    lines = places // tall
    rows = probes * 2
    blocks = quarter // LANES
    block_rows = blocks * slots * 2
    own = lax.axis_index("probe")
    received = jnp.concatenate(
        [received_ref[pl.ds(n, tall, stride=lines), :] for n in range(lines)], axis=0
    ).T
    values = latitude_values(received, chosen_ref[...], slots, cycles, rows)
    start = slots * cycles * rows
    norm = scalars_ref[:rows, :]
    curve = scalars_ref[rows:, :] + jnp.sum(
        received[start : start + rows], axis=1, keepdims=True
    )
    ratios = [
        (norm[2 * p : 2 * p + 1] + norm[2 * p + 1 : 2 * p + 2])
        / (curve[2 * p : 2 * p + 1] + curve[2 * p + 1 : 2 * p + 2])
        for p in range(probes)
    ]
    own_ratio = ratios[0]
    for p in range(1, probes):
        own_ratio = jnp.where(own == p, ratios[p], own_ratio)
    weighted = weighted_ref[...] * own_ratio
    for p in range(probes):
        send_ref[p, block_rows:, :] = weighted
    ratio = jnp.concatenate([ratios[p] for p in range(probes) for _ in range(2)], axis=0)
    ratio = jnp.concatenate([ratio] * blocks, axis=1)
    first_degree = own * quarter
    signal = signal_ref[...]
    for k in range(slots):
        noise_terms = degree_sums(
            hi_ref[k], lo_ref[k], values, k, rows, limits_ref[k : k + 1, :1], first_degree
        )
        terms = terms_ref[k]
        residual = terms - ratio * (signal * terms + noise_terms)
        for p in range(probes):
            for b in range(blocks):
                place = (b * slots + k) * 2
                send_ref[p, place : place + 2, :] = residual[
                    p * 2 : p * 2 + 2, b * LANES : (b + 1) * LANES
                ]


def last_kernel(received_ref, residual_ref, variance_ref):
    probes = received_ref.shape[0]
    slots = residual_ref.shape[1]
    quarter = residual_ref.shape[3] // probes
    blocks = quarter // LANES
    start = blocks * slots * 2
    cycles, length = variance_ref.shape
    total = received_ref[0, start:, :]
    for p in range(1, probes):
        total = total + received_ref[p, start:, :]
    total = total * (1.0 / probes)
    for j in range(length // LANES):
        variance_ref[:, j * LANES : (j + 1) * LANES] = total[j * cycles : (j + 1) * cycles]
    for x in range(probes):
        for b in range(blocks):
            for k in range(slots):
                place = x * quarter + b * LANES
                row = (b * slots + k) * 2
                residual_ref[0, k, :, place : place + LANES] = received_ref[x, row : row + 2, :]


def call(kernel, outs, scratch, args, name, far=()):
    spaces = [pltpu.HBM if i in far else pltpu.VMEM for i in range(len(args))]
    args = [
        pltpu.with_memory_space_constraint(arg, space) if space == pltpu.HBM else arg
        for arg, space in zip(args, spaces)
    ]
    return pl.pallas_call(
        kernel,
        out_shape=[jax.ShapeDtypeStruct(shape, dtype) for shape, dtype in outs],
        in_specs=[pl.BlockSpec(memory_space=space) for space in spaces],
        out_specs=[pl.BlockSpec(memory_space=pltpu.VMEM)] * len(outs),
        scratch_shapes=scratch,
        compiler_params=pltpu.CompilerParams(vmem_limit_bytes=VMEM_BYTES),
        name=name,
        cost_estimate=pl.CostEstimate(flops=2000000000, bytes_accessed=20000000, transcendentals=0),
    )(*args)


def per_device(legendre, signs, inv_noise, inv_signal, harmonic_order_values, cycle_rows):
    slots, quarter, total = legendre.shape
    _, cycles, length = signs.shape
    probes = lax.axis_size("probe")
    tall = lax.axis_size("y")
    places = tall * lax.axis_size("z") * lax.axis_size("core")
    count = harmonic_order_values.shape[0]
    outer = length // LANES
    rows = probes * 2
    folded = ((outer * cycles, LANES), F32)
    by_device = ((places, LANES), F32)

    def everywhere(send):
        received = lax.all_to_all(
            send.reshape(probes * places, LANES), ("probe", "y"), 0, 0, tiled=True
        )
        (joined,) = call(
            functools.partial(join_kernel, tall), [by_device], [], (received,), "join"
        )
        return lax.all_to_all(joined, ("z", "core"), 0, 0, tiled=True)

    (
        send, inner_table, outer_table, limits, signs_near, row_line, signal,
        noise_near,
    ) = call(
        functools.partial(first_kernel, slots, tall),
        [
            ((probes, places, LANES), F32),
            ((4 * LANES, 2 * count), BF16),
            ((outer, 2 * count), F32),
            ((8, LANES), jnp.int32),
            (signs.shape, jnp.int32),
            ((1, total), jnp.int32),
            ((1, quarter), F32),
            (inv_noise.shape, F32),
        ],
        [
            pltpu.VMEM((1, count), jnp.int32),
            pltpu.VMEM((1, total), jnp.int32),
            pltpu.SemaphoreType.DMA((5,)),
        ],
        (
            harmonic_order_values.reshape(1, count), signs, cycle_rows.reshape(1, total),
            inv_signal.reshape(1, probes * quarter), inv_noise,
        ),
        "cycle_sums",
        range(5),
    )
    received = everywhere(send)
    send, terms, leg_hi, leg_lo, chosen = call(
        functools.partial(second_kernel, tall),
        [
            ((probes, places, LANES), F32),
            ((slots, rows, quarter), F32),
            ((slots, total, quarter), BF16),
            ((slots, total, quarter), BF16),
            ((total, total), BF16),
        ],
        [],
        (received, row_line, signal, limits, legendre),
        "degrees_there_and_back",
    )
    received = everywhere(send)
    send, weighted, scalars = call(
        functools.partial(third_kernel, slots, probes, tall),
        [by_device, folded, ((2 * rows, LANES), F32)],
        [pltpu.VMEM((cycles, probes * outer, LANES), F32)],
        (received, signs_near, noise_near, inner_table, outer_table),
        "cycles_there_and_back",
    )
    received = lax.all_to_all(send, ("y", "z", "core"), 0, 0, tiled=True)
    height = quarter // LANES * slots * 2 + outer * cycles
    (send,) = call(
        functools.partial(fourth_kernel, tall),
        [((probes, height, LANES), F32)],
        [],
        (received, signal, limits, leg_hi, leg_lo, chosen, terms, weighted, scalars),
        "image_terms",
    )
    received = lax.all_to_all(send, "probe", 0, 0, tiled=True)
    return call(
        last_kernel,
        [((1, slots, 2, probes * quarter), F32), ((cycles, length), F32)],
        [],
        (received,),
        "outputs",
    )


def solution(mesh):
    cores = 2
    tall = math.isqrt(mesh.shape["sky"] // cores)
    split = jax.sharding.Mesh(
        mesh.devices.reshape(mesh.shape["probe"], tall, -1, cores), ("probe", "y", "z", "core")
    )
    sky = ("y", "z", "core")
    in_specs = (P(sky, "probe", None), P("probe", sky, None), P(sky, None), P(), P(), P())
    out_specs = (P("probe", sky, None, None), P(sky, None))

    def run(*args):
        return tuple(
            jax.shard_map(
                per_device, mesh=split, in_specs=in_specs, out_specs=out_specs, check_vma=False
            )(*args)
        )

    return run
```

```python
import functools
import math

import jax
import jax.numpy as jnp
from jax import lax
from jax.experimental import pallas as pl
from jax.experimental.pallas import tpu as pltpu
from jax.sharding import PartitionSpec as P

F32 = jnp.float32
BF16 = jnp.bfloat16
LANES = 128
VMEM_BYTES = 24 * 1024 * 1024


def iota(shape, dim):
    return lax.broadcasted_iota(jnp.int32, shape, dim)


def dot(a, b):
    return jnp.dot(a, b, preferred_element_type=F32)


def dot_rows(a, b):
    return lax.dot_general(a, b, (((1,), (1,)), ((), ())), preferred_element_type=F32)


def halves(value):
    high = value.astype(BF16)
    return high, (value - high.astype(F32)).astype(BF16)


def fold(flat_ref, f):
    return jnp.concatenate(
        [
            flat_ref[f : f + 1, j * LANES : (j + 1) * LANES]
            for j in range(flat_ref.shape[1] // LANES)
        ],
        axis=0,
    )


def cosine(phase, turn):
    shift = turn.bit_length() - 3
    quadrant = (phase + turn // 8) >> shift
    angle = (phase - (quadrant << shift)).astype(F32) * (2.0 * math.pi / turn)
    square = angle * angle
    cos = 1.0 + square * (
        -1.0 / 2 + square * (1.0 / 24 + square * (-1.0 / 720 + square * (1.0 / 40320)))
    )
    sin = angle * (
        1.0 + square * (-1.0 / 6 + square * (1.0 / 120 + square * (-1.0 / 5040 + square / 362880)))
    )
    value = jnp.where((quadrant & 1) == 1, sin, cos)
    return jnp.where(((quadrant + 1) & 2) == 2, -value, value)


def cosine_and_sine(rows, step, turn):
    half = LANES // 2
    lane = iota((rows, LANES), 1)
    phase = iota((rows, LANES), 0) * (lane & (half - 1)) * step
    return cosine(phase - jnp.where(lane >= half, turn // 4, 0), turn)


def ones_where(condition):
    return jnp.where(condition, 1.0, 0.0).astype(BF16)


def both_picks(line):
    half = LANES // 2
    count = line.shape[1]
    shape = (LANES, 2 * count)
    row, col = iota(shape, 0), iota(shape, 1)
    wide = jnp.concatenate([line, line], axis=1)
    return ones_where(row == wide + jnp.where(col >= count, half, 0))


def turned_rows(pieces):
    rows = jnp.concatenate(pieces, axis=0)
    if rows.shape[0] < LANES:
        rows = jnp.concatenate(
            [rows, jnp.zeros((LANES - rows.shape[0], rows.shape[1]), F32)], axis=0
        )
    return rows.T


def own_rows(received_ref, source, groups):
    places = received_ref.shape[1] // groups
    total = received_ref[source, :places]
    for g in range(1, groups):
        total = total + received_ref[source, g * places : (g + 1) * places]
    total = total.T
    half = LANES // 2
    return jnp.where(lax.axis_index("core") == 0, total[:half], total[half:])


def first_kernel(
    slots, orders_hbm, signs_hbm, rows_hbm, signal_hbm, noise_hbm,
    send_ref, inner_ref, outer_ref, limits_ref, signs_ref,
    rows_ref, signal_ref, noise_ref,
    orders_ref, near_rows_ref, sems,
):
    count = orders_ref.shape[1]
    probes, places = send_ref.shape[:2]
    _, cycles, cycle_length = signs_ref.shape
    outer = cycle_length // LANES
    cores = count // slots // places
    total = rows_ref.shape[1]
    own = lax.axis_index("probe")
    quarter = signal_ref.shape[1]
    own_signal = signal_hbm.at[:, pl.ds(pl.multiple_of(own * quarter, LANES), quarter)]

    copies = [
        pltpu.make_async_copy(source, target, sems.at[n])
        for n, (source, target) in enumerate(
            [
                (orders_hbm, orders_ref),
                (signs_hbm, signs_ref),
                (rows_hbm, near_rows_ref),
                (own_signal, signal_ref),
                (noise_hbm, noise_ref),
            ]
        )
    ]
    for copy in copies:
        copy.start()

    high_table = halves(cosine_and_sine(LANES, 64, cycle_length))
    low_table = halves(cosine_and_sine(LANES, 1, cycle_length))
    outer_table = halves(cosine_and_sine(outer, cycle_length // outer, cycle_length))
    slot, place = iota((count, count), 0), iota((count, count), 1)
    slot_picks = ones_where(
        slot == (place % places * cores + place // places % cores) * slots
        + place // (places * cores)
    )

    copies[0].wait()
    orders = orders_ref[...]
    row = iota((8, count), 0)
    parts = jnp.where(row == 0, orders >> 6, jnp.where(row == 1, orders & 63, 0))
    parts = dot(parts.astype(F32).astype(BF16), slot_picks).astype(jnp.int32)
    high, low = parts[:1], parts[1:2]
    for k in range(slots):
        own_place = (k * cores + lax.axis_index("core")) * places + lax.axis_index("place")
        picked = jnp.where(iota((1, count), 1) == own_place, high * 64 + low, 0).astype(F32)
        picked = jnp.sum(picked, axis=1, keepdims=True).astype(jnp.int32)
        limits_ref[k : k + 1, :] = jnp.broadcast_to(picked, (1, LANES))
    high_picks, low_picks = both_picks(high), both_picks(low)
    high_part = dot(high_table[0], high_picks) + dot(high_table[1], high_picks)
    low_part = dot(low_table[0], low_picks) + dot(low_table[1], low_picks)
    scale_factor = 1.0 / math.sqrt(cycle_length)
    high_cos, high_sin = high_part[:, :count] * scale_factor, high_part[:, count:] * scale_factor
    low_cos, low_sin = low_part[:, :count], low_part[:, count:]
    inner_cos = high_cos * low_cos - high_sin * low_sin
    inner_sin = high_sin * low_cos + high_cos * low_sin
    inner = halves(jnp.concatenate([inner_cos, inner_sin], axis=1))
    for n in range(4):
        inner_ref[n * LANES : (n + 1) * LANES, :] = inner[n // 2]
    outer_part = dot(outer_table[0], low_picks) + dot(outer_table[1], low_picks)
    outer_ref[...] = outer_part

    copies[1].wait()
    rows = probes * 2
    row = iota((rows, count), 0)
    pixels = jnp.concatenate(
        [fold(signs_ref.at[0], f).astype(F32) for f in range(cycles)], axis=0
    ).astype(BF16)
    sums = dot(jnp.concatenate([pixels, pixels], axis=1), inner_ref[LANES : 3 * LANES, :])
    pieces = [[None] * cycles for _ in range(slots)]
    per_slot = count // slots
    for f in range(cycles):
        cos_sum, sin_sum = twiddle_sums(sums[f * outer : (f + 1) * outer], outer_part)
        field = jnp.where(
            row == own * 2, cos_sum, jnp.where(row == own * 2 + 1, sin_sum, 0.0)
        )
        for k in range(slots):
            pieces[k][f] = field[:, k * per_slot : (k + 1) * per_slot]
    out = turned_rows(
        [
            pieces[k][f][:, c * places : (c + 1) * places]
            for c in range(cores)
            for k in range(slots)
            for f in range(cycles)
        ]
    )
    for p in range(probes):
        send_ref[p] = out

    for copy in copies[2:]:
        copy.wait()
    cycle_rows = near_rows_ref[...]
    row = iota((8, total), 0)
    parts = jnp.where(row == 0, cycle_rows >> 6, jnp.where(row == 1, cycle_rows & 63, 0))
    cycle, place = iota((total, total), 0), iota((total, total), 1)
    picks = ones_where(
        cycle == (place % places * cores + place // (places * cycles)) * cycles
        + place // places % cycles
    )
    parts = dot(parts.astype(F32).astype(BF16), picks).astype(jnp.int32)
    rows_ref[...] = parts[:1] * 64 + parts[1:2]


def twiddle_sums(sums, table):
    count = table.shape[1] // 2
    cos, sin = table[:, :count], table[:, count:]
    by_cos, by_sin = sums[:, :count], sums[:, count:]
    return (
        jnp.sum(cos * by_cos - sin * by_sin, axis=0, keepdims=True),
        jnp.sum(sin * by_cos + cos * by_sin, axis=0, keepdims=True),
    )


def latitude_values(by_core, chosen, slots, cycles, rows):
    values = [
        jnp.concatenate(
            [
                values[(k * cycles + f) * rows : (k * cycles + f + 1) * rows]
                for values in by_core
                for f in range(cycles)
            ],
            axis=1,
        )
        for k in range(slots)
    ]
    both = jnp.concatenate(halves(jnp.concatenate(values, axis=0)), axis=0)
    return dot_rows(both, chosen).astype(BF16)


def degree_sums(leg_hi, leg_lo, values, k, rows, order, first_degree):
    width = values.shape[0] // 2
    across = dot(values, leg_hi) + dot(values, leg_lo)
    terms = across[k * rows : (k + 1) * rows] + across[
        width + k * rows : width + (k + 1) * rows
    ]
    degrees = first_degree + iota(terms.shape, 1)
    return jnp.where(degrees >= order, terms, 0.0)


def second_kernel(
    received_ref, rows_ref, signal_ref, limits_ref, legendre_ref,
    send_ref, terms_ref, scalars_ref, hi_ref, lo_ref, chosen_ref,
):
    cores = received_ref.shape[0]
    probes, places = send_ref.shape[:2]
    slots, quarter, total = legendre_ref.shape
    cycles = total // (places * cores)
    rows = probes * 2
    width = slots * rows
    chosen = ones_where(iota((total, total), 0) == rows_ref[...])
    chosen_ref[...] = chosen
    values = latitude_values(
        [own_rows(received_ref, c, probes) for c in range(cores)], chosen, slots, cycles, rows
    )
    first_degree = lax.axis_index("probe") * quarter
    signal = signal_ref[...]
    norm = jnp.zeros((rows, 1), F32)
    prior = jnp.zeros((rows, 1), F32)
    halved = []
    for k in range(slots):
        halved.append(halves(legendre_ref[k]))
        hi_ref[k], lo_ref[k] = halved[k][0].T, halved[k][1].T
    both = []
    for k in range(slots):
        terms = degree_sums(
            hi_ref[k], lo_ref[k], values, k, rows, limits_ref[k : k + 1, :1], first_degree
        )
        terms_ref[k] = terms
        squares = terms * terms
        norm = norm + jnp.sum(squares, axis=1, keepdims=True)
        prior = prior + jnp.sum(squares * signal, axis=1, keepdims=True)
        both.append(jnp.concatenate(halves(terms), axis=0))
    fields = []
    for k in range(slots):
        field = dot(both[k], halved[k][0]) + dot(both[k], halved[k][1])
        fields.append(field[:rows] + field[rows:])
    both = jnp.concatenate(halves(jnp.concatenate(fields, axis=0)), axis=0)
    by_cycle = dot(both, chosen)
    by_cycle = by_cycle[:width] + by_cycle[width:]
    out = turned_rows(
        [
            by_cycle[k * rows : (k + 1) * rows, place * places : (place + 1) * places]
            for c in range(cores)
            for k in range(slots)
            for place in range(c * cycles, (c + 1) * cycles)
        ]
    )
    for p in range(probes):
        send_ref[p] = out
    scalars_ref[:rows, :] = jnp.broadcast_to(norm, (rows, LANES))
    scalars_ref[rows:, :] = jnp.broadcast_to(prior, (rows, LANES))


def third_kernel(
    slots, received_ref, signs_ref, inv_noise_ref, inner_ref, outer_ref, scalars_ref,
    send_ref, weighted_ref, mapped_ref,
):
    cores = received_ref.shape[0]
    places = send_ref.shape[0] // cores
    probes = received_ref.shape[1] // places
    cycles = inv_noise_ref.shape[0]
    outer, count = outer_ref.shape[0], outer_ref.shape[1] // 2
    rows = probes * 2
    own = lax.axis_index("probe")

    by_core = [own_rows(received_ref, c, probes) for c in range(cores)]
    outer_cos, outer_sin = outer_ref[:, :count], outer_ref[:, count:]
    per_slot = count // slots
    row = iota((rows, count), 0)
    power = jnp.zeros((rows, LANES), F32)
    power_row = iota((rows, LANES), 0)
    pieces = [[None] * cycles for _ in range(slots)]
    table = inner_ref[LANES : 3 * LANES, :].T
    table = jnp.concatenate([table, table], axis=0)

    def map_cycle(f):
        coeffs = jnp.concatenate(
            [
                by_core[c][(k * cycles + f) * rows : (k * cycles + f + 1) * rows]
                for k in range(slots)
                for c in range(cores)
            ],
            axis=1,
        )
        high, low = [], []
        for p in range(probes):
            cos_coeff, sin_coeff = coeffs[2 * p : 2 * p + 1], coeffs[2 * p + 1 : 2 * p + 2]
            by_cos = cos_coeff * outer_cos + sin_coeff * outer_sin
            by_sin = sin_coeff * outer_cos - cos_coeff * outer_sin
            hi, lo = halves(jnp.concatenate([by_cos, by_sin], axis=1))
            high.append(hi)
            low.append(lo)
        mapped = dot(
            jnp.concatenate(
                [jnp.concatenate(high, axis=0), jnp.concatenate(low, axis=0)], axis=1
            ),
            table,
        )
        return mapped[:, :LANES] + mapped[:, LANES:]

    def weigh_cycle(f, mapped):
        mapped_ref[f] = mapped
        pixels = jnp.concatenate([fold(inv_noise_ref, f)] * probes, axis=0) * mapped
        squares = pixels * mapped
        lines = [
            jnp.sum(squares[p * outer : (p + 1) * outer], axis=0, keepdims=True)
            for p in range(probes)
        ]
        hi, lo = halves(pixels)
        sums = dot(jnp.concatenate([hi, lo, hi, lo], axis=1), inner_ref[...])
        return lines, [sums[p * outer : (p + 1) * outer] for p in range(probes)]

    def finish_cycle(f, lines, sums):
        nonlocal power
        field = jnp.zeros((rows, count), F32)
        for p in range(probes):
            power = power + jnp.where(power_row == 2 * p, lines[p], 0.0)
            cos_sum, sin_sum = twiddle_sums(sums[p], outer_ref[...])
            field = jnp.where(row == 2 * p, cos_sum, field)
            field = jnp.where(row == 2 * p + 1, sin_sum, field)
        for k in range(slots):
            pieces[k][f] = field[:, k * per_slot : (k + 1) * per_slot]

    mapped, done = map_cycle(0), None
    for f in range(cycles):
        later = map_cycle(f + 1) if f + 1 < cycles else None
        lines, sums = weigh_cycle(f, mapped)
        if done:
            finish_cycle(*done)
        mapped, done = later, (f, lines, sums)
    finish_cycle(*done)
    for f in range(cycles):
        picked = mapped_ref[f, pl.ds(pl.multiple_of(own * outer, outer), outer), :]
        weighted_ref[pl.ds(f, outer, stride=cycles), :] = picked * fold(
            signs_ref.at[0], f
        ).astype(F32)
    power = jnp.broadcast_to(jnp.sum(power, axis=1, keepdims=True), (rows, per_slot))
    out = turned_rows(
        [pieces[k][f] for k in range(slots) for f in range(cycles)]
        + [scalars_ref[:, :per_slot], power]
    )
    for c in range(cores):
        send_ref[pl.ds(c, places, stride=cores), :] = out[c * places : (c + 1) * places]


def fourth_kernel(
    cores, received_ref, signal_ref, limits_ref, hi_ref, lo_ref, chosen_ref, terms_ref,
    weighted_ref, send_ref,
):
    probes = send_ref.shape[0]
    slots, total, quarter = hi_ref.shape
    cycles = total // received_ref.shape[0]
    places = received_ref.shape[0] // cores
    rows = probes * 2
    blocks = quarter // LANES
    block_rows = blocks * slots * 2
    by_core = [received_ref[pl.ds(c, places, stride=cores), :].T for c in range(cores)]
    start = slots * cycles * rows
    scalars = jnp.sum(by_core[0][start : start + 3 * rows], axis=1, keepdims=True)
    for values in by_core[1:]:
        scalars = scalars + jnp.sum(values[start : start + 3 * rows], axis=1, keepdims=True)
    lane = iota((rows, LANES), 1)
    tile = jnp.where(
        lane == 0, scalars[:rows], jnp.where(lane == 1, scalars[rows : 2 * rows], scalars[2 * rows :])
    )
    for p in range(probes):
        send_ref[p, 2 * block_rows : 2 * block_rows + rows, :] = tile
        send_ref[p, 2 * block_rows + rows :, :] = weighted_ref[...]
    values = latitude_values(by_core, chosen_ref[...], slots, cycles, rows)
    first_degree = lax.axis_index("probe") * quarter
    signal = signal_ref[...]
    for k in range(slots):
        noise_terms = degree_sums(
            hi_ref[k], lo_ref[k], values, k, rows, limits_ref[k : k + 1, :1], first_degree
        )
        terms = terms_ref[k]
        image = signal * terms + noise_terms
        for p in range(probes):
            for b in range(blocks):
                place = (b * slots + k) * 2
                own = (slice(p * 2, p * 2 + 2), slice(b * LANES, (b + 1) * LANES))
                send_ref[p, place : place + 2, :] = terms[own]
                send_ref[p, block_rows + place : block_rows + place + 2, :] = image[own]


def last_kernel(received_ref, residual_ref, variance_ref):
    probes = received_ref.shape[0]
    slots = residual_ref.shape[1]
    quarter = residual_ref.shape[3] // probes
    blocks = quarter // LANES
    block_rows = blocks * slots * 2
    rows = probes * 2
    cycles, length = variance_ref.shape
    own = lax.axis_index("probe")
    start = 2 * block_rows
    tiles = [received_ref[p, start : start + rows, :] for p in range(probes)]
    degree_part = tiles[0]
    for tile in tiles[1:]:
        degree_part = degree_part + tile
    shape = (rows, LANES)
    norm = jnp.broadcast_to(degree_part[:, :1], shape)
    curve = jnp.broadcast_to(degree_part[:, 1:2] + tiles[0][:, 2:3], shape)
    ratios = [
        (norm[2 * p : 2 * p + 1] + norm[2 * p + 1 : 2 * p + 2])
        / (curve[2 * p : 2 * p + 1] + curve[2 * p + 1 : 2 * p + 2])
        for p in range(probes)
    ]
    start = start + rows
    total = received_ref[0, start:, :] * ratios[0]
    for p in range(1, probes):
        total = total + received_ref[p, start:, :] * ratios[p]
    total = total * (1.0 / probes)
    for j in range(length // LANES):
        variance_ref[:, j * LANES : (j + 1) * LANES] = total[j * cycles : (j + 1) * cycles]
    own_ratio = ratios[0]
    for p in range(1, probes):
        own_ratio = jnp.where(own == p, ratios[p], own_ratio)
    for x in range(probes):
        residual = (
            received_ref[x, :block_rows, :]
            - own_ratio * received_ref[x, block_rows : 2 * block_rows, :]
        )
        for b in range(blocks):
            for k in range(slots):
                place = x * quarter + b * LANES
                row = (b * slots + k) * 2
                residual_ref[0, k, :, place : place + LANES] = residual[row : row + 2]


def call(kernel, outs, scratch, args, name, far=()):
    spaces = [pltpu.HBM if i in far else pltpu.VMEM for i in range(len(args))]
    args = [
        pltpu.with_memory_space_constraint(arg, space) if space == pltpu.HBM else arg
        for arg, space in zip(args, spaces)
    ]
    return pl.pallas_call(
        kernel,
        out_shape=[jax.ShapeDtypeStruct(shape, dtype) for shape, dtype in outs],
        in_specs=[pl.BlockSpec(memory_space=space) for space in spaces],
        out_specs=[pl.BlockSpec(memory_space=pltpu.VMEM)] * len(outs),
        scratch_shapes=scratch,
        compiler_params=pltpu.CompilerParams(vmem_limit_bytes=VMEM_BYTES),
        name=name,
        cost_estimate=pl.CostEstimate(flops=2000000000, bytes_accessed=20000000, transcendentals=0),
    )(*args)


def per_device(legendre, signs, inv_noise, inv_signal, harmonic_order_values, cycle_rows):
    slots, quarter, total = legendre.shape
    _, cycles, length = signs.shape
    probes = lax.axis_size("probe")
    places = lax.axis_size("place")
    cores = lax.axis_size("core")
    count = harmonic_order_values.shape[0]
    outer = length // LANES
    rows = probes * 2
    folded = ((outer * cycles, LANES), F32)

    def everywhere(send):
        received = lax.all_to_all(
            send.reshape(probes * places, LANES), ("probe", "place"), 0, 0, tiled=True
        )
        return lax.all_gather(received, "core", axis=0)

    (
        send, inner_table, outer_table, limits, signs_near, row_line, signal,
        noise_near,
    ) = call(
        functools.partial(first_kernel, slots),
        [
            ((probes, places, LANES), F32),
            ((4 * LANES, 2 * count), BF16),
            ((outer, 2 * count), F32),
            ((8, LANES), jnp.int32),
            (signs.shape, jnp.int32),
            ((1, total), jnp.int32),
            ((1, quarter), F32),
            (inv_noise.shape, F32),
        ],
        [
            pltpu.VMEM((1, count), jnp.int32),
            pltpu.VMEM((1, total), jnp.int32),
            pltpu.SemaphoreType.DMA((5,)),
        ],
        (
            harmonic_order_values.reshape(1, count), signs, cycle_rows.reshape(1, total),
            inv_signal.reshape(1, probes * quarter), inv_noise,
        ),
        "cycle_sums",
        range(5),
    )
    received = everywhere(send)
    send, terms, scalars, leg_hi, leg_lo, chosen = call(
        second_kernel,
        [
            ((probes, places, LANES), F32),
            ((slots, rows, quarter), F32),
            ((2 * rows, LANES), F32),
            ((slots, total, quarter), BF16),
            ((slots, total, quarter), BF16),
            ((total, total), BF16),
        ],
        [],
        (received, row_line, signal, limits, legendre),
        "degrees_there_and_back",
    )
    received = everywhere(send)
    send, weighted = call(
        functools.partial(third_kernel, slots),
        [((places * cores, LANES), F32), folded],
        [pltpu.VMEM((cycles, probes * outer, LANES), F32)],
        (received, signs_near, noise_near, inner_table, outer_table, scalars),
        "cycles_there_and_back",
    )
    received = lax.all_to_all(send, ("place", "core"), 0, 0, tiled=True)
    height = quarter // LANES * slots * 4 + rows + outer * cycles
    (send,) = call(
        functools.partial(fourth_kernel, cores),
        [((probes, height, LANES), F32)],
        [],
        (received, signal, limits, leg_hi, leg_lo, chosen, terms, weighted),
        "image_terms",
    )
    received = lax.all_to_all(send, "probe", 0, 0, tiled=True)
    return call(
        last_kernel,
        [((1, slots, 2, probes * quarter), F32), ((cycles, length), F32)],
        [],
        (received,),
        "outputs",
    )


def solution(mesh):
    cores = 2
    split = jax.sharding.Mesh(
        mesh.devices.reshape(mesh.shape["probe"], -1, cores), ("probe", "place", "core")
    )
    sky = ("place", "core")
    in_specs = (P(sky, "probe", None), P("probe", sky, None), P(sky, None), P(), P(), P())
    out_specs = (P("probe", sky, None, None), P(sky, None))

    def run(*args):
        return tuple(
            jax.shard_map(
                per_device, mesh=split, in_specs=in_specs, out_specs=out_specs, check_vma=False
            )(*args)
        )

    return run
```

```python
import functools
import math

import jax
import jax.numpy as jnp
from jax import lax
from jax.experimental import pallas as pl
from jax.experimental.pallas import tpu as pltpu
from jax.sharding import PartitionSpec as P

F32 = jnp.float32
BF16 = jnp.bfloat16
LANES = 128
VMEM_BYTES = 24 * 1024 * 1024


def iota(shape, dim):
    return lax.broadcasted_iota(jnp.int32, shape, dim)


def dot(a, b):
    return jnp.dot(a, b, preferred_element_type=F32)


def dot_rows(a, b):
    return lax.dot_general(a, b, (((1,), (1,)), ((), ())), preferred_element_type=F32)


def halves(value):
    high = value.astype(BF16)
    return high, (value - high.astype(F32)).astype(BF16)


def fold(flat_ref, f):
    return jnp.concatenate(
        [
            flat_ref[f : f + 1, j * LANES : (j + 1) * LANES]
            for j in range(flat_ref.shape[1] // LANES)
        ],
        axis=0,
    )


def cosine(phase, turn):
    shift = turn.bit_length() - 3
    quadrant = (phase + turn // 8) >> shift
    angle = (phase - (quadrant << shift)).astype(F32) * (2.0 * math.pi / turn)
    square = angle * angle
    cos = 1.0 + square * (
        -1.0 / 2 + square * (1.0 / 24 + square * (-1.0 / 720 + square * (1.0 / 40320)))
    )
    sin = angle * (
        1.0 + square * (-1.0 / 6 + square * (1.0 / 120 + square * (-1.0 / 5040 + square / 362880)))
    )
    value = jnp.where((quadrant & 1) == 1, sin, cos)
    return jnp.where(((quadrant + 1) & 2) == 2, -value, value)


def cosine_and_sine(rows, step, turn):
    half = LANES // 2
    lane = iota((rows, LANES), 1)
    phase = iota((rows, LANES), 0) * (lane & (half - 1)) * step
    return cosine(phase - jnp.where(lane >= half, turn // 4, 0), turn)


def ones_where(condition):
    return jnp.where(condition, 1.0, 0.0).astype(BF16)


def both_picks(line):
    half = LANES // 2
    count = line.shape[1]
    shape = (LANES, 2 * count)
    row, col = iota(shape, 0), iota(shape, 1)
    wide = jnp.concatenate([line, line], axis=1)
    return ones_where(row == wide + jnp.where(col >= count, half, 0))


def turned_rows(pieces):
    rows = jnp.concatenate(pieces, axis=0)
    if rows.shape[0] < LANES:
        rows = jnp.concatenate(
            [rows, jnp.zeros((LANES - rows.shape[0], rows.shape[1]), F32)], axis=0
        )
    return rows.T


def own_rows(received_ref, source, groups):
    places = received_ref.shape[1] // groups
    total = received_ref[source, :places]
    for g in range(1, groups):
        total = total + received_ref[source, g * places : (g + 1) * places]
    total = total.T
    half = LANES // 2
    return jnp.where(lax.axis_index("core") == 0, total[:half], total[half:])


def first_kernel(
    slots, orders_hbm, signs_hbm, rows_hbm, signal_hbm, noise_hbm,
    send_ref, inner_ref, outer_ref, limits_ref, signs_ref,
    rows_ref, signal_ref, noise_ref,
    orders_ref, near_rows_ref, sems,
):
    count = orders_ref.shape[1]
    probes, places = send_ref.shape[:2]
    _, cycles, cycle_length = signs_ref.shape
    outer = cycle_length // LANES
    cores = count // slots // places
    total = rows_ref.shape[1]
    own = lax.axis_index("probe")
    quarter = signal_ref.shape[1]
    own_signal = signal_hbm.at[:, pl.ds(pl.multiple_of(own * quarter, LANES), quarter)]

    copies = [
        pltpu.make_async_copy(source, target, sems.at[n])
        for n, (source, target) in enumerate(
            [
                (orders_hbm, orders_ref),
                (signs_hbm, signs_ref),
                (rows_hbm, near_rows_ref),
                (own_signal, signal_ref),
                (noise_hbm, noise_ref),
            ]
        )
    ]
    for copy in copies:
        copy.start()

    high_table = halves(cosine_and_sine(LANES, 64, cycle_length))
    low_table = halves(cosine_and_sine(LANES, 1, cycle_length))
    outer_table = halves(cosine_and_sine(outer, cycle_length // outer, cycle_length))
    slot, place = iota((count, count), 0), iota((count, count), 1)
    slot_picks = ones_where(
        slot == (place % places * cores + place // places % cores) * slots
        + place // (places * cores)
    )

    copies[0].wait()
    orders = orders_ref[...]
    row = iota((8, count), 0)
    parts = jnp.where(row == 0, orders >> 6, jnp.where(row == 1, orders & 63, 0))
    parts = dot(parts.astype(F32).astype(BF16), slot_picks).astype(jnp.int32)
    high, low = parts[:1], parts[1:2]
    for k in range(slots):
        own_place = (k * cores + lax.axis_index("core")) * places + lax.axis_index("place")
        picked = jnp.where(iota((1, count), 1) == own_place, high * 64 + low, 0).astype(F32)
        picked = jnp.sum(picked, axis=1, keepdims=True).astype(jnp.int32)
        limits_ref[k : k + 1, :] = jnp.broadcast_to(picked, (1, LANES))
    high_picks, low_picks = both_picks(high), both_picks(low)
    high_part = dot(high_table[0], high_picks) + dot(high_table[1], high_picks)
    low_part = dot(low_table[0], low_picks) + dot(low_table[1], low_picks)
    scale_factor = 1.0 / math.sqrt(cycle_length)
    high_cos, high_sin = high_part[:, :count] * scale_factor, high_part[:, count:] * scale_factor
    low_cos, low_sin = low_part[:, :count], low_part[:, count:]
    inner_cos = high_cos * low_cos - high_sin * low_sin
    inner_sin = high_sin * low_cos + high_cos * low_sin
    inner = halves(jnp.concatenate([inner_cos, inner_sin], axis=1))
    for n in range(4):
        inner_ref[n * LANES : (n + 1) * LANES, :] = inner[n // 2]
    outer_part = dot(outer_table[0], low_picks) + dot(outer_table[1], low_picks)
    outer_ref[...] = outer_part

    copies[1].wait()
    rows = probes * 2
    row = iota((rows, count), 0)
    pixels = jnp.concatenate(
        [fold(signs_ref.at[0], f).astype(F32) for f in range(cycles)], axis=0
    ).astype(BF16)
    sums = dot(jnp.concatenate([pixels, pixels], axis=1), inner_ref[LANES : 3 * LANES, :])
    pieces = [[None] * cycles for _ in range(slots)]
    per_slot = count // slots
    for f in range(cycles):
        cos_sum, sin_sum = twiddle_sums(sums[f * outer : (f + 1) * outer], outer_part)
        field = jnp.where(
            row == own * 2, cos_sum, jnp.where(row == own * 2 + 1, sin_sum, 0.0)
        )
        for k in range(slots):
            pieces[k][f] = field[:, k * per_slot : (k + 1) * per_slot]
    out = turned_rows(
        [
            pieces[k][f][:, c * places : (c + 1) * places]
            for c in range(cores)
            for k in range(slots)
            for f in range(cycles)
        ]
    )
    for p in range(probes):
        send_ref[p] = out

    for copy in copies[2:]:
        copy.wait()
    cycle_rows = near_rows_ref[...]
    row = iota((8, total), 0)
    parts = jnp.where(row == 0, cycle_rows >> 6, jnp.where(row == 1, cycle_rows & 63, 0))
    cycle, place = iota((total, total), 0), iota((total, total), 1)
    picks = ones_where(
        cycle == (place % places * cores + place // (places * cycles)) * cycles
        + place // places % cycles
    )
    parts = dot(parts.astype(F32).astype(BF16), picks).astype(jnp.int32)
    rows_ref[...] = parts[:1] * 64 + parts[1:2]


def twiddle_sums(sums, table):
    count = table.shape[1] // 2
    cos, sin = table[:, :count], table[:, count:]
    by_cos, by_sin = sums[:, :count], sums[:, count:]
    return (
        jnp.sum(cos * by_cos - sin * by_sin, axis=0, keepdims=True),
        jnp.sum(sin * by_cos + cos * by_sin, axis=0, keepdims=True),
    )


def latitude_values(by_core, chosen, slots, cycles, rows):
    values = [
        jnp.concatenate(
            [
                values[(k * cycles + f) * rows : (k * cycles + f + 1) * rows]
                for values in by_core
                for f in range(cycles)
            ],
            axis=1,
        )
        for k in range(slots)
    ]
    both = jnp.concatenate(halves(jnp.concatenate(values, axis=0)), axis=0)
    return dot_rows(both, chosen).astype(BF16)


def degree_sums(leg_hi, leg_lo, values, k, rows, order, first_degree):
    width = values.shape[0] // 2
    across = dot(values, leg_hi) + dot(values, leg_lo)
    terms = across[k * rows : (k + 1) * rows] + across[
        width + k * rows : width + (k + 1) * rows
    ]
    degrees = first_degree + iota(terms.shape, 1)
    return jnp.where(degrees >= order, terms, 0.0)


def second_kernel(
    received_ref, rows_ref, signal_ref, limits_ref, legendre_ref,
    send_ref, terms_ref, scalars_ref, hi_ref, lo_ref, chosen_ref,
):
    cores = received_ref.shape[0]
    probes, places = send_ref.shape[:2]
    slots, quarter, total = legendre_ref.shape
    cycles = total // (places * cores)
    rows = probes * 2
    width = slots * rows
    chosen = ones_where(iota((total, total), 0) == rows_ref[...])
    chosen_ref[...] = chosen
    values = latitude_values(
        [own_rows(received_ref, c, probes) for c in range(cores)], chosen, slots, cycles, rows
    )
    first_degree = lax.axis_index("probe") * quarter
    signal = signal_ref[...]
    norm = jnp.zeros((rows, 1), F32)
    prior = jnp.zeros((rows, 1), F32)
    halved = []
    for k in range(slots):
        halved.append(halves(legendre_ref[k]))
        hi_ref[k], lo_ref[k] = halved[k][0].T, halved[k][1].T
    both = []
    for k in range(slots):
        terms = degree_sums(
            hi_ref[k], lo_ref[k], values, k, rows, limits_ref[k : k + 1, :1], first_degree
        )
        terms_ref[k] = terms
        squares = terms * terms
        norm = norm + jnp.sum(squares, axis=1, keepdims=True)
        prior = prior + jnp.sum(squares * signal, axis=1, keepdims=True)
        both.append(jnp.concatenate(halves(terms), axis=0))
    fields = []
    for k in range(slots):
        field = dot(both[k], halved[k][0]) + dot(both[k], halved[k][1])
        fields.append(field[:rows] + field[rows:])
    both = jnp.concatenate(halves(jnp.concatenate(fields, axis=0)), axis=0)
    by_cycle = dot(both, chosen)
    by_cycle = by_cycle[:width] + by_cycle[width:]
    out = turned_rows(
        [
            by_cycle[k * rows : (k + 1) * rows, place * places : (place + 1) * places]
            for c in range(cores)
            for k in range(slots)
            for place in range(c * cycles, (c + 1) * cycles)
        ]
    )
    for p in range(probes):
        send_ref[p] = out
    scalars_ref[:rows, :] = jnp.broadcast_to(norm, (rows, LANES))
    scalars_ref[rows:, :] = jnp.broadcast_to(prior, (rows, LANES))


def third_kernel(
    slots, received_ref, signs_ref, inv_noise_ref, inner_ref, outer_ref, scalars_ref,
    send_ref, weighted_ref, mapped_ref,
):
    cores = received_ref.shape[0]
    places = send_ref.shape[0] // cores
    probes = received_ref.shape[1] // places
    cycles = inv_noise_ref.shape[0]
    outer, count = outer_ref.shape[0], outer_ref.shape[1] // 2
    rows = probes * 2
    own = lax.axis_index("probe")

    by_core = [own_rows(received_ref, c, probes) for c in range(cores)]
    outer_cos, outer_sin = outer_ref[:, :count], outer_ref[:, count:]
    per_slot = count // slots
    row = iota((rows, count), 0)
    power = jnp.zeros((rows, LANES), F32)
    power_row = iota((rows, LANES), 0)
    pieces = [[None] * cycles for _ in range(slots)]
    table = inner_ref[LANES : 3 * LANES, :].T
    table = jnp.concatenate([table, table], axis=0)

    def map_cycle(f):
        coeffs = jnp.concatenate(
            [
                by_core[c][(k * cycles + f) * rows : (k * cycles + f + 1) * rows]
                for k in range(slots)
                for c in range(cores)
            ],
            axis=1,
        )
        high, low = [], []
        for p in range(probes):
            cos_coeff, sin_coeff = coeffs[2 * p : 2 * p + 1], coeffs[2 * p + 1 : 2 * p + 2]
            by_cos = cos_coeff * outer_cos + sin_coeff * outer_sin
            by_sin = sin_coeff * outer_cos - cos_coeff * outer_sin
            hi, lo = halves(jnp.concatenate([by_cos, by_sin], axis=1))
            high.append(hi)
            low.append(lo)
        mapped = dot(
            jnp.concatenate(
                [jnp.concatenate(high, axis=0), jnp.concatenate(low, axis=0)], axis=1
            ),
            table,
        )
        return mapped[:, :LANES] + mapped[:, LANES:]

    def weigh_cycle(f, mapped):
        mapped_ref[f] = mapped
        pixels = jnp.concatenate([fold(inv_noise_ref, f)] * probes, axis=0) * mapped
        squares = pixels * mapped
        lines = [
            jnp.sum(squares[p * outer : (p + 1) * outer], axis=0, keepdims=True)
            for p in range(probes)
        ]
        hi, lo = halves(pixels)
        sums = dot(jnp.concatenate([hi, lo, hi, lo], axis=1), inner_ref[...])
        return lines, [sums[p * outer : (p + 1) * outer] for p in range(probes)]

    def finish_cycle(f, lines, sums):
        nonlocal power
        field = jnp.zeros((rows, count), F32)
        for p in range(probes):
            power = power + jnp.where(power_row == 2 * p, lines[p], 0.0)
            cos_sum, sin_sum = twiddle_sums(sums[p], outer_ref[...])
            field = jnp.where(row == 2 * p, cos_sum, field)
            field = jnp.where(row == 2 * p + 1, sin_sum, field)
        for k in range(slots):
            pieces[k][f] = field[:, k * per_slot : (k + 1) * per_slot]

    mapped, done = map_cycle(0), None
    for f in range(cycles):
        later = map_cycle(f + 1) if f + 1 < cycles else None
        lines, sums = weigh_cycle(f, mapped)
        if done:
            finish_cycle(*done)
        mapped, done = later, (f, lines, sums)
    finish_cycle(*done)
    for f in range(cycles):
        picked = mapped_ref[f, pl.ds(pl.multiple_of(own * outer, outer), outer), :]
        weighted_ref[pl.ds(f, outer, stride=cycles), :] = picked * fold(
            signs_ref.at[0], f
        ).astype(F32)
    power = jnp.broadcast_to(jnp.sum(power, axis=1, keepdims=True), (rows, per_slot))
    out = turned_rows(
        [pieces[k][f] for k in range(slots) for f in range(cycles)]
        + [scalars_ref[:, :per_slot], power]
    )
    for c in range(cores):
        send_ref[pl.ds(c, places, stride=cores), :] = out[c * places : (c + 1) * places]


def fourth_kernel(
    cores, received_ref, signal_ref, limits_ref, hi_ref, lo_ref, chosen_ref, terms_ref,
    weighted_ref, send_ref,
):
    probes = send_ref.shape[0]
    slots, total, quarter = hi_ref.shape
    cycles = total // received_ref.shape[0]
    places = received_ref.shape[0] // cores
    rows = probes * 2
    blocks = quarter // LANES
    block_rows = blocks * slots * 2
    by_core = [received_ref[pl.ds(c, places, stride=cores), :].T for c in range(cores)]
    start = slots * cycles * rows
    scalars = jnp.sum(by_core[0][start : start + 3 * rows], axis=1, keepdims=True)
    for values in by_core[1:]:
        scalars = scalars + jnp.sum(values[start : start + 3 * rows], axis=1, keepdims=True)
    norm = scalars[:rows]
    curve = scalars[rows : 2 * rows] + scalars[2 * rows :] * (1.0 / probes)
    pairs = [
        part[2 * p : 2 * p + 1] + part[2 * p + 1 : 2 * p + 2]
        for part in (norm, curve)
        for p in range(probes)
    ]
    tile = jnp.broadcast_to(jnp.concatenate(pairs, axis=0), (rows, LANES))
    for p in range(probes):
        send_ref[p, 2 * block_rows : 2 * block_rows + rows, :] = tile
        send_ref[p, 2 * block_rows + rows :, :] = weighted_ref[...]
    values = latitude_values(by_core, chosen_ref[...], slots, cycles, rows)
    first_degree = lax.axis_index("probe") * quarter
    signal = signal_ref[...]
    for k in range(slots):
        noise_terms = degree_sums(
            hi_ref[k], lo_ref[k], values, k, rows, limits_ref[k : k + 1, :1], first_degree
        )
        terms = terms_ref[k]
        image = signal * terms + noise_terms
        for p in range(probes):
            for b in range(blocks):
                place = (b * slots + k) * 2
                own = (slice(p * 2, p * 2 + 2), slice(b * LANES, (b + 1) * LANES))
                send_ref[p, place : place + 2, :] = terms[own]
                send_ref[p, block_rows + place : block_rows + place + 2, :] = image[own]


def last_kernel(received_ref, residual_ref, variance_ref):
    probes = received_ref.shape[0]
    slots = residual_ref.shape[1]
    quarter = residual_ref.shape[3] // probes
    blocks = quarter // LANES
    block_rows = blocks * slots * 2
    rows = probes * 2
    cycles, length = variance_ref.shape
    own = lax.axis_index("probe")
    start = 2 * block_rows
    tiles = [received_ref[p, start : start + rows, :] for p in range(probes)]
    sums = tiles[0]
    for tile in tiles[1:]:
        sums = sums + tile
    ratios = [sums[p : p + 1] / sums[probes + p : probes + p + 1] for p in range(probes)]
    start = start + rows
    total = received_ref[0, start:, :] * ratios[0]
    for p in range(1, probes):
        total = total + received_ref[p, start:, :] * ratios[p]
    total = total * (1.0 / probes)
    for j in range(length // LANES):
        variance_ref[:, j * LANES : (j + 1) * LANES] = total[j * cycles : (j + 1) * cycles]
    own_ratio = ratios[0]
    for p in range(1, probes):
        own_ratio = jnp.where(own == p, ratios[p], own_ratio)
    for x in range(probes):
        residual = (
            received_ref[x, :block_rows, :]
            - own_ratio * received_ref[x, block_rows : 2 * block_rows, :]
        )
        for b in range(blocks):
            for k in range(slots):
                place = x * quarter + b * LANES
                row = (b * slots + k) * 2
                residual_ref[0, k, :, place : place + LANES] = residual[row : row + 2]


def call(kernel, outs, scratch, args, name, far=()):
    spaces = [pltpu.HBM if i in far else pltpu.VMEM for i in range(len(args))]
    args = [
        pltpu.with_memory_space_constraint(arg, space) if space == pltpu.HBM else arg
        for arg, space in zip(args, spaces)
    ]
    return pl.pallas_call(
        kernel,
        out_shape=[jax.ShapeDtypeStruct(shape, dtype) for shape, dtype in outs],
        in_specs=[pl.BlockSpec(memory_space=space) for space in spaces],
        out_specs=[pl.BlockSpec(memory_space=pltpu.VMEM)] * len(outs),
        scratch_shapes=scratch,
        compiler_params=pltpu.CompilerParams(vmem_limit_bytes=VMEM_BYTES),
        name=name,
        cost_estimate=pl.CostEstimate(flops=2000000000, bytes_accessed=20000000, transcendentals=0),
    )(*args)


def per_device(legendre, signs, inv_noise, inv_signal, harmonic_order_values, cycle_rows):
    slots, quarter, total = legendre.shape
    _, cycles, length = signs.shape
    probes = lax.axis_size("probe")
    places = lax.axis_size("place")
    cores = lax.axis_size("core")
    count = harmonic_order_values.shape[0]
    outer = length // LANES
    rows = probes * 2
    folded = ((outer * cycles, LANES), F32)

    def everywhere(send):
        received = lax.all_to_all(
            send.reshape(probes * places, LANES), ("probe", "place"), 0, 0, tiled=True
        )
        return lax.all_gather(received, "core", axis=0)

    (
        send, inner_table, outer_table, limits, signs_near, row_line, signal,
        noise_near,
    ) = call(
        functools.partial(first_kernel, slots),
        [
            ((probes, places, LANES), F32),
            ((4 * LANES, 2 * count), BF16),
            ((outer, 2 * count), F32),
            ((8, LANES), jnp.int32),
            (signs.shape, jnp.int32),
            ((1, total), jnp.int32),
            ((1, quarter), F32),
            (inv_noise.shape, F32),
        ],
        [
            pltpu.VMEM((1, count), jnp.int32),
            pltpu.VMEM((1, total), jnp.int32),
            pltpu.SemaphoreType.DMA((5,)),
        ],
        (
            harmonic_order_values.reshape(1, count), signs, cycle_rows.reshape(1, total),
            inv_signal.reshape(1, probes * quarter), inv_noise,
        ),
        "cycle_sums",
        range(5),
    )
    received = everywhere(send)
    send, terms, scalars, leg_hi, leg_lo, chosen = call(
        second_kernel,
        [
            ((probes, places, LANES), F32),
            ((slots, rows, quarter), F32),
            ((2 * rows, LANES), F32),
            ((slots, total, quarter), BF16),
            ((slots, total, quarter), BF16),
            ((total, total), BF16),
        ],
        [],
        (received, row_line, signal, limits, legendre),
        "degrees_there_and_back",
    )
    received = everywhere(send)
    send, weighted = call(
        functools.partial(third_kernel, slots),
        [((places * cores, LANES), F32), folded],
        [pltpu.VMEM((cycles, probes * outer, LANES), F32)],
        (received, signs_near, noise_near, inner_table, outer_table, scalars),
        "cycles_there_and_back",
    )
    received = lax.all_to_all(send, ("place", "core"), 0, 0, tiled=True)
    height = quarter // LANES * slots * 4 + rows + outer * cycles
    (send,) = call(
        functools.partial(fourth_kernel, cores),
        [((probes, height, LANES), F32)],
        [],
        (received, signal, limits, leg_hi, leg_lo, chosen, terms, weighted),
        "image_terms",
    )
    received = lax.all_to_all(send, "probe", 0, 0, tiled=True)
    return call(
        last_kernel,
        [((1, slots, 2, probes * quarter), F32), ((cycles, length), F32)],
        [],
        (received,),
        "outputs",
    )


def solution(mesh):
    cores = 2
    split = jax.sharding.Mesh(
        mesh.devices.reshape(mesh.shape["probe"], -1, cores), ("probe", "place", "core")
    )
    sky = ("place", "core")
    in_specs = (P(sky, "probe", None), P("probe", sky, None), P(sky, None), P(), P(), P())
    out_specs = (P("probe", sky, None, None), P(sky, None))

    def run(*args):
        return tuple(
            jax.shard_map(
                per_device, mesh=split, in_specs=in_specs, out_specs=out_specs, check_vma=False
            )(*args)
        )

    return run
```
